32 devices in a mesh: ctx: 16 (over z, y, x), head: 2 (over core).
Axes of the slice: x: 2, y: 2, z: 4, core: 2. Of those that a mesh axis runs over, the one named last changes fastest.
Arguments:
- tokens: bfloat16 [2048, 2048], P('ctx'), may hold values from -6 to 6
- block_offsets: int32 [32], replicated, may hold values from 0 to 1984, as said below
- cotangent: bfloat16 [2048, 2048], P('ctx'), may hold values from -6 to 6
- w_query: float32 [2048, 2048], P('ctx', 'head'), may hold values from -0.125 to 0.125
- w_key: float32 [2048, 1024], P('ctx', 'head'), may hold values from -0.125 to 0.125
- w_value: float32 [2048, 1024], P('ctx', 'head'), may hold values from -0.125 to 0.125
- w_out: float32 [2048, 2048], P('head', 'ctx'), may hold values from -0.75 to 0.75
- w_gate: float32 [2048, 8192], P('ctx', 'head'), may hold values from -0.125 to 0.125
- w_up: float32 [2048, 8192], P('ctx', 'head'), may hold values from -0.125 to 0.125
- w_down: float32 [8192, 2048], P('head', 'ctx'), may hold values from -0.099436891 to 0.099436891
- gains: float32 [2, 2048], P(None, 'ctx'), may hold values from 0.3 to 2.7
- moment_one: float32 [62914560], P(('ctx', 'head'))
- moment_two: float32 [62914560], P(('ctx', 'head'))
- gain_moment_one: float32 [2, 2048], P(None, 'ctx')
- gain_moment_two: float32 [2, 2048], P(None, 'ctx')
Outputs:
- layer_out: bfloat16 [2048, 2048], P('ctx')
- input_grad: bfloat16 [2048, 2048], P('ctx')
- grad_norm: float32 [], replicated
- new_query: float32 [2048, 2048], P('ctx', 'head')
- new_key: float32 [2048, 1024], P('ctx', 'head')
- new_value: float32 [2048, 1024], P('ctx', 'head')
- new_out: float32 [2048, 2048], P('head', 'ctx')
- new_gate: float32 [2048, 8192], P('ctx', 'head')
- new_up: float32 [2048, 8192], P('ctx', 'head')
- new_down: float32 [8192, 2048], P('head', 'ctx')
- new_gains: float32 [2, 2048], P(None, 'ctx')
- query_copy: bfloat16 [2048, 2048], P('ctx', 'head')
- key_copy: bfloat16 [2048, 1024], P('ctx', 'head')
- value_copy: bfloat16 [2048, 1024], P('ctx', 'head')
- out_copy: bfloat16 [2048, 2048], P('head', 'ctx')
- gate_copy: bfloat16 [2048, 8192], P('ctx', 'head')
- up_copy: bfloat16 [2048, 8192], P('ctx', 'head')
- down_copy: bfloat16 [8192, 2048], P('head', 'ctx')
- gains_copy: bfloat16 [2, 2048], P(None, 'ctx')
- new_moment_one: float32 [62914560], P(('ctx', 'head'))
- new_moment_two: float32 [62914560], P(('ctx', 'head'))
- new_gain_moment_one: float32 [2, 2048], P(None, 'ctx')
- new_gain_moment_two: float32 [2, 2048], P(None, 'ctx')
The draws below stay inside these ranges and needn't reach their ends.
Inputs may be any that keep to these rules, and one draw needn't show every extreme that they name: `block_offsets`: each multiple of 64 from 0 to 1984 occurs exactly once.
All inputs are finite; a program needn't handle non-finite values.
Results may differ from the reference program's by a relative error of at most 0.02.
Values may be sent and summed in bfloat16 or wider, within the bound.
No kernel may reach another device: no remote copies, remote signals or barrier semaphores. Data moves between devices by JAX's collectives and lax.ppermute only.
A program may use at most 448 MiB of HBM per device.

```python
import math
import jax
import jax.numpy as jnp
from jax import lax

D = 2048
HQ = 8
KV = 4
HD = 256
FF = 8192
SUB = 64
STEP = 10
TOKENS = 2048
WO_FAN = 64
P_DEV = 1966080
N_CTX = 16
N_HEAD = 2
DEVICES = 32


def ramp_between(count, low_end, high_end):
    ladder = jnp.arange(count, dtype=jnp.float32) / max(count - 1, 1)
    return low_end * (high_end / low_end) ** ladder


def grad_unit():
    weighted = 0.36 * 3 * D * FF + 4.0 * (D * HQ * HD + 2 * D * KV * HD)
    return 1.0 / math.sqrt(weighted)


def shard_scales():
    shard_rows = D // N_CTX
    unit_size = grad_unit()
    out_relative = 1.4 * math.sqrt(WO_FAN / (HQ * HD))
    segments = [(shard_rows * (HQ * HD // N_HEAD), 2.0), (shard_rows * (KV * HD // N_HEAD), 2.0), (shard_rows * (KV * HD // N_HEAD), 2.0), (shard_rows * (HQ * HD // N_HEAD), out_relative), (shard_rows * (FF // N_HEAD), 0.6), (shard_rows * (FF // N_HEAD), 0.6), (shard_rows * (FF // N_HEAD), 0.6)]
    device_row = jnp.concatenate([jnp.full((length,), relative * unit_size, jnp.float32) for length, relative in segments])
    return jnp.tile(device_row, N_CTX * N_HEAD)


def draw_block_offsets(key, part):
    key = jax.random.fold_in(key, 1)
    return (jax.random.permutation(key, TOKENS // SUB) * SUB).astype(jnp.int32)


def draw_gains(key, part):
    key = jax.random.fold_in(key, 2)
    ladder = ramp_between(D, 0.6, 1.8)
    jitter = jax.random.uniform(key, (2, D), jnp.float32, 0.85, 1.15)
    return ladder[None, :] * jitter


def draw_w_down(key, part):
    key = jax.random.fold_in(key, 3)
    ladder = ramp_between(FF, 0.6, 1.8)
    noise = jax.random.truncated_normal(key, -4.0, 4.0, (FF, D), jnp.float32)
    return noise * ladder[:, None] / math.sqrt(FF)


def draw_moment_one(key, part):
    key = jax.random.fold_in(key, 4)
    scales = shard_scales()
    return scales / 9.0 * jax.random.truncated_normal(key, -4.0, 4.0, scales.shape, jnp.float32)


def draw_moment_two(key, part):
    key = jax.random.fold_in(key, 5)
    scales = shard_scales()
    spread = jnp.exp(jax.random.uniform(key, scales.shape, jnp.float32, 0.0, math.log(4.0)))
    return scales * scales * (0.05 / 0.95) * spread


def draw_gain_moment_one(key, part):
    key = jax.random.fold_in(key, 6)
    return 2.8 * grad_unit() / 9.0 * jax.random.truncated_normal(key, -4.0, 4.0, (2, D), jnp.float32)


def draw_gain_moment_two(key, part):
    key = jax.random.fold_in(key, 7)
    spread = jnp.exp(jax.random.uniform(key, (2, D), jnp.float32, 0.0, math.log(4.0)))
    return (2.8 * grad_unit()) ** 2 * (0.05 / 0.95) * spread


def steps_of(own_key, shape, pieces, low, high):
    level, own = 1.0, jax.random.fold_in(own_key, 6)
    for position, parts in pieces:
        draws = jnp.exp(jax.random.uniform(jax.random.fold_in(own, position), (parts,), jnp.float32, low / len(pieces), high / len(pieces)))
        level = level * jnp.repeat(draws, shape[position] // parts).reshape([-1 if axis == position else 1 for axis in range(len(shape))])
    return level


def centred(stream_key, shape, deviation, most, cuts=(), kind=jnp.bfloat16):
    entries = deviation * jax.random.normal(stream_key, shape, jnp.float32)
    if cuts:
        entries = entries * steps_of(stream_key, shape, cuts, -0.22, 0.18)
    return jnp.clip(entries, -most, most).astype(kind)


def setup_inputs(seed: int = 0) -> dict:
    arg_keys = jax.random.split(jax.random.key(seed), 16)
    return {
        "tokens": centred(arg_keys[0], (TOKENS, D), 1.0, 6.0, ((0, 16),)),
        "block_offsets": draw_block_offsets(jax.random.fold_in(arg_keys[15], 71), 0),
        "cotangent": centred(arg_keys[2], (TOKENS, D), 1.0, 6.0, ((0, 16),)),
        "w_query": centred(arg_keys[3], (D, HQ * HD), D ** -0.5, 0.125, ((0, 16), (1, 2)), jnp.float32),
        "w_key": centred(arg_keys[4], (D, KV * HD), D ** -0.5, 0.125, ((0, 16), (1, 2)), jnp.float32),
        "w_value": centred(arg_keys[5], (D, KV * HD), D ** -0.5, 0.125, ((0, 16), (1, 2)), jnp.float32),
        "w_out": centred(arg_keys[6], (HQ * HD, D), WO_FAN ** -0.5, 0.75, ((0, 2), (1, 16)), jnp.float32),
        "w_gate": centred(arg_keys[7], (D, FF), D ** -0.5, 0.125, ((0, 16), (1, 2)), jnp.float32),
        "w_up": centred(arg_keys[8], (D, FF), D ** -0.5, 0.125, ((0, 16), (1, 2)), jnp.float32),
        "w_down": draw_w_down(jax.random.fold_in(arg_keys[15], 71), 0),
        "gains": draw_gains(jax.random.fold_in(arg_keys[15], 71), 0),
        "moment_one": draw_moment_one(jax.random.fold_in(arg_keys[15], 71), 0),
        "moment_two": draw_moment_two(jax.random.fold_in(arg_keys[15], 71), 0),
        "gain_moment_one": draw_gain_moment_one(jax.random.fold_in(arg_keys[15], 71), 0),
        "gain_moment_two": draw_gain_moment_two(jax.random.fold_in(arg_keys[15], 71), 0),
    }


@jax.custom_vjp
def low(v):
    return lax.optimization_barrier(v.astype(jnp.bfloat16)).astype(jnp.float32)

@jax.custom_vjp
def low_back(v):
    return v

def low_keep(v):
    return (low(v), None)

def low_pass(kept, grad):
    return (grad,)

def back_keep(v):
    return (v, None)

def back_low(kept, grad):
    return (low(grad),)
low.defvjp(low_keep, low_pass)
low_back.defvjp(back_keep, back_low)
NORM_EPS = 1e-06
ROPE_BASE = 1000042.0
BETA_ONE = 0.9
BETA_TWO = 0.95
ADAM_EPS = 1e-08
WEIGHT_DECAY = 0.1
GAIN_RATE = 0.5
CLIP_NORM = 1.0
MASKED_SCORE = -1e+30
PRECISION = lax.Precision.HIGHEST
ROW_SHARDED = (True, True, True, False, True, True, False)

def matmul(left, right):
    return jnp.dot(left, right, precision=PRECISION, preferred_element_type=jnp.float32)

def normalize(inputs, gain_row):
    inverse = lax.rsqrt(lax.optimization_barrier(jnp.mean(inputs * inputs, axis=-1, keepdims=True)) + NORM_EPS)
    return inputs * inverse * gain_row

def rotary_tables(positions):
    frequency = ROPE_BASE ** (-jnp.arange(0, HD, 2, dtype=jnp.float32) / HD)
    angles = positions.astype(jnp.float32)[:, None] * frequency[None, :]
    return (jnp.cos(angles)[:, None, :], jnp.sin(angles)[:, None, :])

def rotate(heads_in, cosine, sine):
    half_size = heads_in.shape[-1] // 2
    first_half = heads_in[..., :half_size]
    second_half = heads_in[..., half_size:]
    return jnp.concatenate([first_half * cosine - second_half * sine, second_half * cosine + first_half * sine], axis=-1)

def attend(qrot, krot, values, positions):
    scaling = 1.0 / math.sqrt(HD)
    share = HQ // KV
    query_groups = qrot.reshape(TOKENS, KV, share, HD).transpose(1, 2, 0, 3)
    key_groups = krot.transpose(1, 0, 2)
    value_groups = values.transpose(1, 0, 2)

    def one_group(operands):
        queries, keys_here, values_here = operands
        allowed = positions[None, :] <= positions[:, None]
        scores = low_back(jnp.einsum('gtd,sd->gts', queries, keys_here, precision=PRECISION) * scaling)
        scores = jnp.where(allowed[None], scores, MASKED_SCORE)
        weights = low(jax.nn.softmax(scores, axis=-1))
        return jnp.einsum('gts,sd->gtd', weights, values_here, precision=PRECISION)
    outcome = lax.map(jax.checkpoint(one_group), (query_groups, key_groups, value_groups))
    return outcome.transpose(2, 0, 1, 3).reshape(TOKENS, HQ * HD)

def blocks_of(matrix, by_rows):
    height, breadth = matrix.shape
    if by_rows:
        tiles = matrix.reshape(N_CTX, height // N_CTX, N_HEAD, breadth // N_HEAD).transpose(0, 2, 1, 3)
    else:
        tiles = matrix.reshape(N_HEAD, height // N_HEAD, N_CTX, breadth // N_CTX).transpose(2, 0, 1, 3)
    return tiles.reshape(N_CTX * N_HEAD, -1)

def unblock(flat_piece, shape, by_rows):
    height, breadth = shape
    if by_rows:
        return flat_piece.reshape(N_CTX, N_HEAD, height // N_CTX, breadth // N_HEAD).transpose(0, 2, 1, 3).reshape(height, breadth)
    return flat_piece.reshape(N_CTX, N_HEAD, height // N_HEAD, breadth // N_CTX).transpose(1, 2, 0, 3).reshape(height, breadth)

def adamw_step(weight, gradient, first_moment, second_moment, step_rate, decay_rate):
    first_new = BETA_ONE * first_moment + (1.0 - BETA_ONE) * gradient
    second_new = BETA_TWO * second_moment + (1.0 - BETA_TWO) * gradient * gradient
    ratio = first_new / (1.0 - BETA_ONE ** STEP) / (jnp.sqrt(second_new / (1.0 - BETA_TWO ** STEP)) + ADAM_EPS)
    return (weight - step_rate * (ratio + decay_rate * weight), first_new, second_new)

def reference(tokens, block_offsets, cotangent, w_query, w_key, w_value, w_out, w_gate, w_up, w_down, gains, moment_one, moment_two, gain_moment_one, gain_moment_two):
    positions = (block_offsets[:, None] + jnp.arange(SUB, dtype=jnp.int32)[None, :]).reshape(-1).astype(jnp.int32)
    cosine, sine = rotary_tables(positions)

    def forward(inputs, query_weight, key_weight, value_weight, out_weight, gate_weight, up_weight, down_weight, gain_pair):
        gain_low = low(gain_pair)
        normed = low(normalize(inputs, gain_low[0]))
        queries = low_back(matmul(normed, low(query_weight))).reshape(TOKENS, HQ, HD)
        keys_all = low_back(matmul(normed, low(key_weight))).reshape(TOKENS, KV, HD)
        values = low(low_back(matmul(normed, low(value_weight)))).reshape(TOKENS, KV, HD)
        qrot = low(rotate(queries, cosine, sine))
        krot = low(rotate(keys_all, cosine, sine))
        mixed = low(low_back(attend(qrot, krot, values, positions)))
        resid = inputs + low_back(matmul(mixed, low(out_weight)))
        normed_two = low(normalize(resid, gain_low[1]))
        gate_values = low_back(matmul(normed_two, low(gate_weight)))
        up_values = low_back(matmul(normed_two, low(up_weight)))
        hidden = low(jax.nn.silu(gate_values) * up_values)
        return resid + low_back(matmul(hidden, low(down_weight)))
    matrices = (w_query, w_key, w_value, w_out, w_gate, w_up, w_down)
    layer_value, pullback = jax.vjp(forward, tokens.astype(jnp.float32), w_query, w_key, w_value, w_out, w_gate, w_up, w_down, gains)
    gradients = pullback(cotangent.astype(jnp.float32))
    weight_grads = gradients[1:8]
    gain_grad = gradients[8]
    squares = jnp.sum(gain_grad * gain_grad)
    for gradient in weight_grads:
        squares = squares + jnp.sum(gradient * gradient)
    grad_norm = jnp.sqrt(squares)
    factor = CLIP_NORM / jnp.maximum(grad_norm, CLIP_NORM)
    table_one = moment_one.reshape(DEVICES, P_DEV)
    table_two = moment_two.reshape(DEVICES, P_DEV)
    rate_in = 2.0 / math.sqrt(D)
    step_rates = (rate_in, rate_in, rate_in, 2.0 / math.sqrt(WO_FAN), rate_in, rate_in, 2.0 / math.sqrt(FF))
    new_weights = []
    firsts = []
    seconds = []
    offset = 0
    for index_now in range(7):
        weight = matrices[index_now]
        width_here = weight.size // DEVICES
        first_moment = unblock(table_one[:, offset:offset + width_here], weight.shape, ROW_SHARDED[index_now])
        second_moment = unblock(table_two[:, offset:offset + width_here], weight.shape, ROW_SHARDED[index_now])
        updated, first_new, second_new = adamw_step(weight, factor * weight_grads[index_now], first_moment, second_moment, step_rates[index_now], WEIGHT_DECAY)
        new_weights.append(updated)
        firsts.append(blocks_of(first_new, ROW_SHARDED[index_now]))
        seconds.append(blocks_of(second_new, ROW_SHARDED[index_now]))
        offset = offset + width_here
    new_gains, gain_first, gain_second = adamw_step(gains, factor * gain_grad, gain_moment_one, gain_moment_two, GAIN_RATE, 0.0)
    moment_one_new = jnp.concatenate(firsts, axis=1).reshape(-1)
    moment_two_new = jnp.concatenate(seconds, axis=1).reshape(-1)
    return (layer_value.astype(jnp.bfloat16), gradients[0].astype(jnp.bfloat16), grad_norm, new_weights[0], new_weights[1], new_weights[2], new_weights[3], new_weights[4], new_weights[5], new_weights[6], new_gains, new_weights[0].astype(jnp.bfloat16), new_weights[1].astype(jnp.bfloat16), new_weights[2].astype(jnp.bfloat16), new_weights[3].astype(jnp.bfloat16), new_weights[4].astype(jnp.bfloat16), new_weights[5].astype(jnp.bfloat16), new_weights[6].astype(jnp.bfloat16), new_gains.astype(jnp.bfloat16), moment_one_new, moment_two_new, gain_first, gain_second)
```

```python
import math

import jax
import jax.numpy as jnp
from jax import lax
from jax.sharding import Mesh
from jax.sharding import PartitionSpec as P

D = 2048
HQ = 8
KV = 4
HD = 256
FF = 8192
SUB = 64
STEP = 10
SHARE = HQ // KV
QW = SHARE * HD


NORM_EPS = 1e-06
ROPE_BASE = 1000042.0
BETA_ONE = 0.9
BETA_TWO = 0.95
ADAM_EPS = 1e-08
WEIGHT_DECAY = 0.1
GAIN_RATE = 0.5
CLIP_NORM = 1.0
MASKED_SCORE = -1e30
BF = jnp.bfloat16
F32 = jnp.float32
SWAP = [(0, 1), (1, 0)]


def lowered(array_in):
    return array_in.astype(BF)


def product(left, right):
    return jnp.dot(left, right, preferred_element_type=F32)


def contract(left, right, left_dim, right_dim):
    return lax.dot_general(
        left, right, (((left_dim,), (right_dim,)), ((), ())), preferred_element_type=F32
    )


def rotary_tables(positions):
    frequency = ROPE_BASE ** (-jnp.arange(0, HD, 2, dtype=F32) / HD)
    angles = positions.astype(F32)[:, None] * frequency[None, :]
    return (jnp.cos(angles), jnp.sin(angles))


def rotate(one_head, cosine, sine):
    half_size = HD // 2
    first_half = one_head[:, :half_size]
    second_half = one_head[:, half_size:]
    return jnp.concatenate(
        [first_half * cosine - second_half * sine, second_half * cosine + first_half * sine],
        axis=-1,
    )


def adamw_step(weight, gradient, first_moment, second_moment, step_rate, decay_rate):
    first_new = BETA_ONE * first_moment + (1.0 - BETA_ONE) * gradient
    second_new = BETA_TWO * second_moment + (1.0 - BETA_TWO) * gradient * gradient
    ratio = (
        first_new
        / (1.0 - BETA_ONE**STEP)
        / (jnp.sqrt(second_new / (1.0 - BETA_TWO**STEP)) + ADAM_EPS)
    )
    return (weight - step_rate * (ratio + decay_rate * weight), first_new, second_new)


def pick(array_in, index, axis):
    return lax.dynamic_index_in_dim(array_in, index, axis, keepdims=False)


class Lanes:
    def __init__(self):
        self.n_p = lax.axis_size("p")
        self.z = lax.axis_index("z")
        self.p = lax.axis_index("p")
        self.h = lax.axis_index("head")
        self.bits = self.n_p.bit_length() - 1
        self.cube = [2] * self.bits

    def swap(self, array_in):
        return lax.ppermute(array_in, "head", SWAP)

    def over_z(self, array_in, step):
        return lax.ppermute(array_in, "z", [(i, i ^ step) for i in range(4)])

    def over_p(self, array_in, step):
        return lax.ppermute(array_in, "p", [(i, i ^ step) for i in range(self.n_p)])

    def orders(self):
        return list(range(self.bits)), list(range(self.bits))[::-1]

    def bit(self, b):
        return (self.p >> b) & 1

    def absolute_z(self, pieces):
        low, high = (self.z & 1) == 1, (self.z >> 1) == 1
        return jnp.stack(
            [
                jnp.where(
                    high,
                    jnp.where(low, pieces[j ^ 3], pieces[j ^ 2]),
                    jnp.where(low, pieces[j ^ 1], pieces[j]),
                )
                for j in range(4)
            ]
        )

    def gather_z(self, array_in):
        return [array_in] + [self.over_z(array_in, s) for s in (1, 2, 3)]

    def exchange_z(self, array_in):
        pieces = [pick(array_in, self.z, 0)]
        for s in (1, 2, 3):
            pieces.append(self.over_z(pick(array_in, self.z ^ s, 0), s))
        return self.absolute_z(pieces)

    def scatter_z(self, array_in, relative):
        index = (lambda s: s) if relative else (lambda s: self.z ^ s)
        total = pick(array_in, index(0), 0).astype(F32)
        for s in (1, 2, 3):
            total = total + self.over_z(lowered(pick(array_in, index(s), 0)), s).astype(F32)
        return total

    def gather_p(self, array_in, order, relative, lead=0):
        have = []
        for b in order:
            other = self.over_p(array_in, 1 << b)
            axis = lead + sum(1 for x in have if x > b)
            mine, other = jnp.expand_dims(array_in, axis), jnp.expand_dims(other, axis)
            array_in = jnp.concatenate([mine, other], axis)
            if not relative:
                array_in = jnp.where(
                    self.bit(b) == 1, jnp.concatenate([other, mine], axis), array_in
                )
            have.append(b)
        return array_in

    def scatter_p(self, array_in, order, relative, lead=0):
        have = list(range(self.bits))
        for b in order:
            axis = lead + sum(1 for x in have if x > b)
            bit = 0 if relative else self.bit(b)
            keep, send = pick(array_in, bit, axis), pick(array_in, 1 - bit, axis)
            array_in = keep.astype(F32) + self.over_p(lowered(send), 1 << b).astype(F32)
            have.remove(b)
        return array_in

    def exchange_p(self, array_in, order, lead=0):
        for b in order:
            axis = lead + self.bits - 1 - b
            bit = self.bit(b)
            keep, send = pick(array_in, bit, axis), pick(array_in, 1 - bit, axis)
            other = self.over_p(send, 1 << b)
            mine, other = jnp.expand_dims(keep, axis), jnp.expand_dims(other, axis)
            array_in = jnp.where(
                bit == 1,
                jnp.concatenate([other, mine], axis),
                jnp.concatenate([mine, other], axis),
            )
        return array_in

    def exchange_all(self, array_in, z_first):
        tail = array_in.shape[2:]
        array_in = array_in.reshape([4] + self.cube + list(tail))
        order = self.orders()[0]
        if z_first:
            array_in = self.exchange_p(self.exchange_z(array_in), order, 1)
        else:
            array_in = self.exchange_z(self.exchange_p(array_in, order, 1))
        return array_in.reshape((4, self.n_p) + tail)

    def halves(self, array_in):
        middle = array_in.shape[-1] // 2
        return array_in[..., :middle], array_in[..., middle:]

    def group_weight(self, part_zero, part_one):
        first = self.h == 0
        keep = jnp.where(first, part_zero, part_one).transpose(1, 0, 2)
        other = self.swap(jnp.where(first, part_one, part_zero).transpose(1, 0, 2))
        blocks = jnp.where(
            first, jnp.concatenate([keep, other]), jnp.concatenate([other, keep])
        )
        mine = self.exchange_z(blocks)
        out = []
        for half, order in zip(self.halves(mine), self.orders()):
            here = self.gather_p(half, order, False, 1).reshape(D, half.shape[-1])
            there = self.swap(here)
            out.append((jnp.where(first, here, there), jnp.where(first, there, here)))
        return out

    def group_grad(self, part_zero, part_one):
        first = self.h == 0
        keep = jnp.where(first, part_zero, part_one)
        send = jnp.where(first, part_one, part_zero)
        summed = keep + self.swap(lowered(send)).astype(F32)
        rows = D // (4 * self.n_p)
        done = []
        for half, order in zip(self.halves(summed), self.orders()):
            cube = half.reshape([4] + self.cube + [rows, half.shape[-1]])
            done.append(lowered(self.scatter_p(cube, order, False, 1)))
        blocks = self.exchange_z(jnp.concatenate(done, axis=-1))
        own = jnp.where(first, blocks[:2], blocks[2:])
        other = self.swap(jnp.where(first, blocks[2:], blocks[:2]))
        zero, one = jnp.where(first, own, other), jnp.where(first, other, own)
        return zero.transpose(1, 0, 2).astype(F32), one.transpose(1, 0, 2).astype(F32)


def local(
    tokens,
    block_offsets,
    cotangent,
    w_query,
    w_key,
    w_value,
    w_out,
    w_gate,
    w_up,
    w_down,
    gains,
    moment_one,
    moment_two,
    gain_moment_one,
    gain_moment_two,
):
    lanes = Lanes()
    n_p, h = lanes.n_p, lanes.h
    n_ctx = 4 * n_p
    total_rows = n_ctx * 2 * SUB
    rows = D // n_ctx
    units = FF // (2 * n_ctx)
    scaling = 1.0 / math.sqrt(HD)
    first_core = h == 0
    gain_low = lowered(gains).astype(F32)
    gain_one, gain_two = gain_low[0][:, None], gain_low[1][:, None]

    x_own = lax.dynamic_slice_in_dim(tokens, h * SUB, SUB)
    dy_own = lax.dynamic_slice_in_dim(cotangent, h * SUB, SUB)
    x_chunk = jnp.concatenate(lanes.gather_z(x_own)).astype(F32)
    inverse_chunk = lax.rsqrt(jnp.mean(x_chunk * x_chunk, axis=-1, keepdims=True) + NORM_EPS)
    normed = lowered(x_chunk * inverse_chunk)

    key_part = (w_key * gain_one).reshape(rows, 2, HD)
    value_part = (w_value * gain_one).reshape(rows, 2, HD)
    query_part = lowered((w_query * gain_one).reshape(rows, 2, QW))
    (query_zero, key_weight), (query_one, value_weight) = lanes.group_weight(
        query_part, lowered(jnp.concatenate([key_part, value_part], axis=-1))
    )
    out_part = lowered(w_out).T.reshape(rows, 2, QW)
    (out_a, out_c), (out_b, out_d) = lanes.group_weight(*lanes.halves(out_part))
    out_weight = jnp.concatenate([out_a, out_b, out_c, out_d], axis=-1)

    def to_units(matrix, z_first):
        blocks = lowered(matrix).reshape(rows, 4, n_p, units).transpose(1, 2, 0, 3)
        mine = lanes.exchange_all(blocks, z_first).reshape(D, units)
        return mine, lanes.swap(mine)

    gate_weight = to_units(w_gate * gain_two, False)
    up_weight = to_units(w_up * gain_two, True)
    down_weight = to_units(w_down.T, False)
    gate_up_weight = jnp.concatenate(gate_weight + up_weight, axis=-1)
    down_weight = jnp.concatenate(down_weight, axis=-1)
    dy_all = lax.all_gather(dy_own, ("z", "p"), axis=0, tiled=True)

    line = lanes.z ^ jnp.arange(4, dtype=jnp.int32)
    ring = lanes.p ^ jnp.arange(n_p, dtype=jnp.int32)
    cores = h ^ jnp.arange(2, dtype=jnp.int32)
    within = jnp.arange(SUB, dtype=jnp.int32)
    key_blocks = 2 * (line[None, None, :] * n_p + ring[None, :, None]) + cores[:, None, None]
    key_positions = (block_offsets[key_blocks.reshape(-1)][:, None] + within).reshape(-1)
    my_positions = key_positions[: 4 * SUB]
    cosine, sine = rotary_tables(my_positions)
    query_heads = lowered(
        jnp.concatenate(
            [
                rotate(product(normed, query_zero), cosine, sine),
                rotate(product(normed, query_one), cosine, sine),
            ]
        )
    )
    key_here = lowered(rotate(product(normed, key_weight), cosine, sine))
    value_here = lowered(product(normed, value_weight))

    def all_tokens(array_in, order):
        plane = lanes.gather_p(array_in, order, True).reshape(n_p * 4 * SUB, HD)
        return jnp.concatenate([plane, lanes.swap(plane)])

    def back_to_tokens(array_in, order):
        middle = n_p * 4 * SUB
        half = array_in[:middle] + lanes.swap(lowered(array_in[middle:])).astype(F32)
        return lanes.scatter_p(half.reshape(lanes.cube + [4 * SUB, HD]), order, True)

    forth, back = lanes.orders()
    keys_all = all_tokens(key_here, forth)
    values_all = all_tokens(value_here, back)
    allowed = key_positions[None, :] <= my_positions[:, None]
    allowed = jnp.concatenate([allowed] * SHARE)
    scores = jnp.where(allowed, contract(query_heads, keys_all, 1, 1) * scaling, MASKED_SCORE)
    largest = jnp.max(scores, axis=-1, keepdims=True)
    expos = jnp.exp(scores - largest)
    probs = expos / jnp.sum(expos, axis=-1, keepdims=True)
    probs_low = lowered(probs)
    attended = lowered(product(probs_low, values_all))
    mixed = jnp.concatenate([attended[: 4 * SUB], attended[4 * SUB :]], axis=-1)
    resid_part = contract(mixed, out_weight, 1, 1).reshape(4, SUB, D)
    x_float = x_own.astype(F32)
    resid = x_float + lanes.scatter_z(resid_part, True)
    inverse_two = lax.rsqrt(jnp.mean(resid * resid, axis=-1, keepdims=True) + NORM_EPS)
    normed_two = lowered(resid * inverse_two)

    stacked = lanes.absolute_z(lanes.gather_z(normed_two))
    two_halves = [
        lanes.gather_p(half, order, False, 1).reshape(n_ctx * SUB, D // 2)
        for half, order in zip(lanes.halves(stacked), lanes.orders())
    ]
    normed_all = jnp.concatenate(two_halves, axis=-1)
    d_hidden = product(dy_all, down_weight)
    gate_up = product(normed_all, gate_up_weight)
    gate_values, up_values = gate_up[:, : 2 * units], gate_up[:, 2 * units :]
    sigmoid_gate = jax.nn.sigmoid(gate_values)
    activated = gate_values * sigmoid_gate
    hidden = lowered(activated * up_values)
    d_up = lowered(d_hidden * activated)
    d_gate = lowered(
        d_hidden * up_values * sigmoid_gate * (1.0 + gate_values * (1.0 - sigmoid_gate))
    )
    d_gate_up = jnp.concatenate([d_gate, d_up], axis=-1)
    d_normed_halves = []
    for part, order in zip((slice(0, D // 2), slice(D // 2, D)), lanes.orders()):
        partial = contract(d_gate_up, gate_up_weight[part], 1, 1)
        cube = partial.reshape([4] + lanes.cube + [SUB, D // 2])
        d_normed_halves.append(lanes.scatter_z(lanes.scatter_p(cube, order, False, 1), False))
    d_normed_two = jnp.concatenate(d_normed_halves, axis=-1)
    out_part = lowered(contract(hidden, down_weight, 1, 1))
    out_sum = lax.psum_scatter(out_part, ("z", "p"), scatter_dimension=0, tiled=True)

    def both_cores(own):
        other = lanes.swap(own)
        return jnp.where(
            first_core, jnp.concatenate([own, other]), jnp.concatenate([other, own])
        )

    layer_out = both_cores(lowered(resid + out_sum.astype(F32)))

    def norm_back(inputs, inverse, incoming):
        inner = jnp.mean(incoming * inputs, axis=-1, keepdims=True)
        return inverse * incoming - inputs * (inverse * inverse * inverse * inner)

    d_resid = dy_own.astype(F32) + norm_back(resid, inverse_two, d_normed_two)

    grad_gate_up = contract(normed_all, d_gate_up, 0, 0)
    grad_down_t = contract(dy_all, hidden, 0, 0)

    def to_owner(gradient, z_first):
        mine = gradient[:, :units] + lanes.swap(lowered(gradient[:, units:])).astype(F32)
        blocks = lowered(mine).reshape(4, n_p, rows, units)
        came = lanes.exchange_all(blocks, z_first)
        return came.transpose(2, 0, 1, 3).reshape(rows, n_ctx * units).astype(F32)

    inner_gate = to_owner(grad_gate_up[:, : 2 * units], False)
    inner_up = to_owner(grad_gate_up[:, 2 * units :], True)
    grad_down = to_owner(grad_down_t, False).T

    d_resid_chunk = jnp.concatenate(lanes.gather_z(lowered(d_resid)))
    d_mixed = lowered(product(d_resid_chunk, out_weight))
    d_attended = jnp.concatenate([d_mixed[:, :HD], d_mixed[:, HD:]])
    grad_out_t = contract(d_resid_chunk, mixed, 0, 0)
    d_probs = contract(d_attended, values_all, 1, 1)
    delta = jnp.sum(probs * d_probs, axis=-1, keepdims=True)
    d_scores = lowered(probs * (d_probs - delta))
    d_query_heads = product(d_scores, keys_all) * scaling
    d_key_all = contract(d_scores, query_heads, 0, 0) * scaling
    d_value_all = contract(probs_low, d_attended, 0, 0)
    d_key = lowered(rotate(back_to_tokens(d_key_all, forth), cosine, -sine))
    d_value = lowered(back_to_tokens(d_value_all, back))
    d_query_zero = lowered(rotate(d_query_heads[: 4 * SUB], cosine, -sine))
    d_query_one = lowered(rotate(d_query_heads[4 * SUB :], cosine, -sine))
    d_normed_part = (
        contract(d_query_zero, query_zero, 1, 1)
        + contract(d_query_one, query_one, 1, 1)
        + contract(d_key, key_weight, 1, 1)
        + contract(d_value, value_weight, 1, 1)
    )
    d_normed = lanes.scatter_z(d_normed_part.reshape(4, SUB, D), True)
    inverse_own = lax.rsqrt(jnp.mean(x_float * x_float, axis=-1, keepdims=True) + NORM_EPS)
    input_grad = both_cores(lowered(d_resid + norm_back(x_float, inverse_own, d_normed)))

    d_query = jnp.concatenate([d_query_zero, d_query_one], axis=-1)
    d_key_value = jnp.concatenate([d_key, d_value], axis=-1)
    inner_query, inner_pair = lanes.group_grad(
        contract(normed, d_query, 0, 0), contract(normed, d_key_value, 0, 0)
    )
    grad_out = lanes.group_grad(grad_out_t[:, :HD], grad_out_t[:, HD:])
    grad_out = jnp.concatenate(grad_out, axis=-1).reshape(rows, 2 * QW).T
    inner_query = inner_query.reshape(rows, 2 * QW)
    inner_key = inner_pair[:, :, :HD].reshape(rows, 2 * HD)
    inner_value = inner_pair[:, :, HD:].reshape(rows, 2 * HD)

    def weighed(matrix, inner):
        return jnp.sum(lowered(matrix).astype(F32) * inner, axis=1)

    grad_gains = jnp.stack(
        [
            weighed(w_query, inner_query) + weighed(w_key, inner_key) + weighed(w_value, inner_value),
            weighed(w_gate, inner_gate) + weighed(w_up, inner_up),
        ]
    )
    grad_gains = grad_gains + lanes.swap(grad_gains)

    gradients = (
        inner_query * gain_one,
        inner_key * gain_one,
        inner_value * gain_one,
        grad_out,
        inner_gate * gain_two,
        inner_up * gain_two,
        grad_down,
    )
    squares = jnp.sum(grad_gains * grad_gains) * 0.5
    for gradient in gradients:
        squares = squares + jnp.sum(gradient * gradient)
    squares = jnp.broadcast_to(squares, (8, 128))
    squares = squares + lanes.swap(squares)
    for b in range(lanes.bits):
        squares = squares + lanes.over_p(squares, 1 << b)
    for s in (1, 2):
        squares = squares + lanes.over_z(squares, s)
    grad_norm = jnp.sqrt(squares[0, 0])
    factor = CLIP_NORM / jnp.maximum(grad_norm, CLIP_NORM)
    wo_fan = min(HQ * HD, max(2, 131072 // total_rows))
    rate_in = 2.0 / math.sqrt(D)
    step_rates = (
        rate_in,
        rate_in,
        rate_in,
        2.0 / math.sqrt(wo_fan),
        rate_in,
        rate_in,
        2.0 / math.sqrt(FF),
    )
    masters = (w_query, w_key, w_value, w_out, w_gate, w_up, w_down)
    new_weights = []
    firsts = []
    seconds = []
    offset = 0
    for index_now in range(7):
        weight = masters[index_now]
        length = weight.size
        first_moment = moment_one[offset : offset + length].reshape(weight.shape)
        second_moment = moment_two[offset : offset + length].reshape(weight.shape)
        updated, first_new, second_new = adamw_step(
            weight,
            factor * gradients[index_now],
            first_moment,
            second_moment,
            step_rates[index_now],
            WEIGHT_DECAY,
        )
        new_weights.append(updated)
        firsts.append(first_new.reshape(-1))
        seconds.append(second_new.reshape(-1))
        offset = offset + length
    new_gains, gain_first, gain_second = adamw_step(
        gains, factor * grad_gains, gain_moment_one, gain_moment_two, GAIN_RATE, 0.0
    )
    return (
        layer_out,
        input_grad,
        grad_norm,
        *new_weights,
        new_gains,
        *[lowered(weight) for weight in new_weights],
        lowered(new_gains),
        jnp.concatenate(firsts),
        jnp.concatenate(seconds),
        gain_first,
        gain_second,
    )


def solution(mesh):
    n_ctx, n_head = mesh.devices.shape
    lanes_mesh = Mesh(mesh.devices.reshape(4, n_ctx // 4, n_head), ("z", "p", "head"))
    ctx = ("z", "p")
    rows = P(ctx, None)
    wide = P(ctx, "head")
    tall = P("head", ctx)
    flat = P(("z", "p", "head"))
    gain = P(None, ctx)
    weights = (wide, wide, wide, tall, wide, wide, tall, gain)
    return jax.shard_map(
        local,
        mesh=lanes_mesh,
        in_specs=(rows, P(), rows, *weights, flat, flat, gain, gain),
        out_specs=(rows, rows, P(), *weights, *weights, flat, flat, gain, gain),
        check_vma=False,
    )
```

```python
import math

import jax
import jax.numpy as jnp
from jax import lax
from jax.experimental import pallas as pl
from jax.experimental.pallas import tpu as pltpu
from jax.sharding import Mesh
from jax.sharding import PartitionSpec as P

D = 2048
HQ = 8
KV = 4
HD = 256
FF = 8192
SUB = 64
STEP = 10
SHARE = HQ // KV
QW = SHARE * HD


NORM_EPS = 1e-06
ROPE_BASE = 1000042.0
BETA_ONE = 0.9
BETA_TWO = 0.95
ADAM_EPS = 1e-08
WEIGHT_DECAY = 0.1
GAIN_RATE = 0.5
CLIP_NORM = 1.0
MASKED_SCORE = -1e30
BF = jnp.bfloat16
F32 = jnp.float32
SWAP = [(0, 1), (1, 0)]


def lowered(array_in):
    return array_in.astype(BF)


def product(left, right):
    return jnp.dot(left, right, preferred_element_type=F32)


def contract(left, right, left_dim, right_dim):
    return lax.dot_general(
        left, right, (((left_dim,), (right_dim,)), ((), ())), preferred_element_type=F32
    )


def rotary_tables(positions):
    frequency = ROPE_BASE ** (-jnp.arange(0, HD, 2, dtype=F32) / HD)
    angles = positions.astype(F32)[:, None] * frequency[None, :]
    return (jnp.cos(angles), jnp.sin(angles))


def rotate(one_head, cosine, sine):
    half_size = HD // 2
    first_half = one_head[:, :half_size]
    second_half = one_head[:, half_size:]
    return jnp.concatenate(
        [first_half * cosine - second_half * sine, second_half * cosine + first_half * sine],
        axis=-1,
    )


def adamw_step(weight, gradient, first_moment, second_moment, step_rate, decay_rate):
    first_new = BETA_ONE * first_moment + (1.0 - BETA_ONE) * gradient
    second_new = BETA_TWO * second_moment + (1.0 - BETA_TWO) * gradient * gradient
    ratio = (
        first_new
        / (1.0 - BETA_ONE**STEP)
        / (jnp.sqrt(second_new / (1.0 - BETA_TWO**STEP)) + ADAM_EPS)
    )
    return (weight - step_rate * (ratio + decay_rate * weight), first_new, second_new)


def pick(array_in, index, axis):
    return lax.dynamic_index_in_dim(array_in, index, axis, keepdims=False)


def after(arrays, *others):
    listed = arrays if isinstance(arrays, list) else [arrays]
    if not others:
        return arrays
    anywhere = pl.BlockSpec(memory_space=pl.ANY)
    out = pl.pallas_call(
        lambda *refs: None,
        in_specs=[anywhere] * (len(listed) + len(others)),
        out_specs=[anywhere] * len(listed),
        out_shape=[jax.ShapeDtypeStruct(array.shape, array.dtype) for array in listed],
        input_output_aliases={k: k for k in range(len(listed))},
        name="after",
    )(*listed, *others)
    return list(out) if isinstance(arrays, list) else out[0]


class Lanes:
    def __init__(self):
        self.n_p = lax.axis_size("p")
        self.z = lax.axis_index("z")
        self.p = lax.axis_index("p")
        self.h = lax.axis_index("head")
        self.bits = self.n_p.bit_length() - 1
        self.cube = [2] * self.bits

    def swap(self, array_in):
        return lax.ppermute(array_in, "head", SWAP)

    def over_z(self, array_in, step):
        return lax.ppermute(array_in, "z", [(i, i ^ step) for i in range(4)])

    def over_p(self, array_in, step):
        return lax.ppermute(array_in, "p", [(i, i ^ step) for i in range(self.n_p)])

    def orders(self):
        return list(range(self.bits)), list(range(self.bits))[::-1]

    def bit(self, b):
        return (self.p >> b) & 1

    def absolute(self, pieces, index, axis=0):
        for b in range(len(pieces).bit_length() - 1):
            odd = ((index >> b) & 1) == 1
            pieces = [jnp.where(odd, pieces[j ^ (1 << b)], pieces[j]) for j in range(len(pieces))]
        return jnp.stack(pieces, axis)

    def gather_z(self, array_in):
        one, two = self.over_z(array_in, 1), self.over_z(array_in, 2)
        return [array_in, one, two, self.over_z(two, 1)]

    def send_z(self, array_in, axis=0):
        pieces = [pick(array_in, self.z, axis)]
        for s in (1, 2, 3):
            pieces.append(self.over_z(pick(array_in, self.z ^ s, axis), s))
        return pieces

    def join_z(self, pieces, axis=0):
        return self.absolute(pieces, self.z, axis)

    def scatter_z(self, array_in, relative):
        parts = [pick(array_in, s if relative else self.z ^ s, 0).astype(F32) for s in range(4)]
        near = self.over_z(lowered(jnp.stack([parts[3], parts[1]])), 1).astype(F32)
        far = self.over_z(lowered(parts[2] + near[0]), 2).astype(F32)
        return parts[0] + near[1] + far

    def gather_p(self, array_in, order, relative, lead=0):
        have = []
        for b in order:
            other = self.over_p(array_in, 1 << b)
            axis = lead + sum(1 for x in have if x > b)
            mine, other = jnp.expand_dims(array_in, axis), jnp.expand_dims(other, axis)
            array_in = jnp.concatenate([mine, other], axis)
            if not relative:
                array_in = jnp.where(
                    self.bit(b) == 1, jnp.concatenate([other, mine], axis), array_in
                )
            have.append(b)
        return array_in

    def gather_cube(self, array_in, order):
        held = [(array_in[None], [0])]
        for b in order:
            numbers = [j for _, part in held for j in part]
            whole = jnp.concatenate([array for array, _ in held]) if len(held) > 1 else held[0][0]
            held.append((self.over_p(whole, 1 << b), [j ^ (1 << b) for j in numbers]))
        return held

    def scatter_p(self, array_in, order, relative, lead=0):
        have = list(range(self.bits))
        for b in order:
            axis = lead + sum(1 for x in have if x > b)
            bit = 0 if relative else self.bit(b)
            keep, send = pick(array_in, bit, axis), pick(array_in, 1 - bit, axis)
            array_in = keep.astype(F32) + self.over_p(lowered(send), 1 << b).astype(F32)
            have.remove(b)
        return array_in

    def halves(self, array_in):
        middle = array_in.shape[-1] // 2
        return array_in[..., :middle], array_in[..., middle:]

    def group_blocks(self, part_zero, part_one):
        first = self.h == 0
        keep = jnp.where(first, part_zero, part_one).transpose(1, 0, 2)
        other = self.swap(jnp.where(first, part_one, part_zero).transpose(1, 0, 2))
        return jnp.where(
            first, jnp.concatenate([keep, other]), jnp.concatenate([other, keep])
        )

    def group_home(self, summed):
        first = self.h == 0
        blocks = summed
        for b in (1, 0):
            shape = (2, 2) + summed.shape[1:]
            bit = (self.z >> b) & 1
            cube = blocks.reshape(shape)
            keep, send = pick(cube, bit, 1 - b), pick(cube, 1 - bit, 1 - b)
            other = self.over_z(send, 1 << b)
            keep, other = jnp.expand_dims(keep, 1 - b), jnp.expand_dims(other, 1 - b)
            blocks = jnp.where(
                bit == 1,
                jnp.concatenate([other, keep], 1 - b),
                jnp.concatenate([keep, other], 1 - b),
            ).reshape(summed.shape)
        own = jnp.where(first, blocks[:2], blocks[2:])
        other = self.swap(jnp.where(first, blocks[2:], blocks[:2]))
        return jnp.where(first, own, other), jnp.where(first, other, own)


def moved(own, inputs, shapes, plan):
    def kernel(own_ref, *refs):
        ins, outs = refs[: len(inputs)], refs[len(inputs) :]
        for source, target in plan(ins, outs, own_ref[0], own_ref[1]):
            target[...] = source[...]

    vmem = pl.BlockSpec(memory_space=pltpu.VMEM)
    return pl.pallas_call(
        kernel,
        in_specs=[pl.BlockSpec(memory_space=pltpu.SMEM)] + [vmem] * len(inputs),
        out_specs=[vmem] * len(shapes),
        out_shape=[jax.ShapeDtypeStruct(shape, inputs[0].dtype) for shape in shapes],
        compiler_params=pltpu.CompilerParams(vmem_limit_bytes=40 * 1024 * 1024),
        name="moved",
    )(own, *inputs)


def split_rows(own, array_in, which):
    count = array_in.shape[which]
    shape = array_in.shape[:which] + array_in.shape[which + 1 :]

    def plan(ins, outs, z, p):
        if which == 0:
            return [(ins[0].at[z ^ j], outs[j]) for j in range(count)]
        return [(ins[0].at[:, p ^ j], outs[j]) for j in range(count)]

    return moved(own, [array_in], [shape] * count, plan)


def joined(own, pieces, which):
    count = len(pieces)
    shape = pieces[0].shape
    shape = shape[:which] + (count,) + shape[which:]

    def plan(ins, outs, z, p):
        if which == 0:
            return [(ins[j], outs[0].at[z ^ j]) for j in range(count)]
        return [(ins[j], outs[0].at[:, p ^ j]) for j in range(count)]

    return moved(own, pieces, [shape], plan)[0]


def turned(own, pieces, which):
    count = len(pieces)
    other = pieces[0].shape[0]
    shape = (count,) + pieces[0].shape[1:]

    def plan(ins, outs, z, p):
        mine, theirs = (z, p) if which == 0 else (p, z)
        return [
            (ins[i].at[theirs ^ j], outs[j].at[mine ^ i])
            for i in range(count)
            for j in range(other)
        ]

    return moved(own, pieces, [shape] * other, plan)


def halved(own, array_in, at, b):
    count = array_in.shape[1] // 2
    shape = (array_in.shape[0], count) + array_in.shape[2:]

    def plan(ins, outs, z, p):
        bit = (p >> b) & 1
        pairs = []
        for k in range(count):
            rest = ((k >> at) << (at + 1)) | (k & ((1 << at) - 1))
            for target, value in ((outs[0], bit), (outs[1], 1 - bit)):
                pairs.append((ins[0].at[:, rest + value * (1 << at)], target.at[:, k]))
        return pairs

    return moved(own, [array_in], [shape] * 2, plan)


def placed(own, halves, together):
    arrays = [array for half in halves for array, _ in half]
    n_p = sum(len(numbers) for _, numbers in halves[0])
    shapes = []
    for half in halves:
        block = half[0][0].shape[1:]
        shapes.append((block[0], n_p) + block[1:])
    if together:
        widths = [shape[-1] for shape in shapes]
        shapes = [shapes[0][:-1] + (sum(widths),)]

    def plan(ins, outs, z, p):
        pairs, at = [], 0
        for k, half in enumerate(halves):
            for _, numbers in half:
                for i, j in enumerate(numbers):
                    if together:
                        lanes = pl.ds(sum(widths[:k]), widths[k])
                        target = outs[0].at[:, p ^ j, :, lanes]
                    else:
                        target = outs[k].at[:, p ^ j]
                    pairs.append((ins[at].at[i], target))
                at = at + 1
        return pairs

    return moved(own, arrays, shapes, plan)


def add_split(own, n_p, gate_up, down, came):
    rows = gate_up.shape[0] // (4 * n_p)

    def kernel(own_ref, gate_up_ref, down_ref, came_ref, *outs):
        for j in range(n_p):
            for z in range(4):
                at = pl.multiple_of((z * n_p + (own_ref[1] ^ j)) * rows, rows)
                at = pl.ds(at, rows)
                for ref, lanes in ((gate_up_ref, pl.ds(0, 512)), (down_ref, pl.ds(512, 256))):
                    outs[j][z, :, lanes] = lowered(ref[at, :] + came_ref[at, lanes].astype(F32))

    vmem = pl.BlockSpec(memory_space=pltpu.VMEM)
    return pl.pallas_call(
        kernel,
        in_specs=[pl.BlockSpec(memory_space=pltpu.SMEM), vmem, vmem, vmem],
        out_specs=[vmem] * n_p,
        out_shape=[jax.ShapeDtypeStruct((4, rows, 768), BF)] * n_p,
        compiler_params=pltpu.CompilerParams(vmem_limit_bytes=40 * 1024 * 1024),
        name="add_split",
    )(own, gate_up, down, came)


def feed_weights(own, here, there):
    count = len(here)

    def plan(ins, outs, z, p):
        pairs = []
        for k in range(2 * count):
            core, j = k // count, k % count
            gate_up, down = pl.ds(core * 512, 512), pl.ds(core * 256, 256)
            pairs.append((ins[k].at[:, :, pl.ds(0, 512)], outs[0].at[:, p ^ j, :, gate_up]))
            pairs.append((ins[k].at[:, :, pl.ds(512, 256)], outs[1].at[:, p ^ j, :, down]))
        return pairs

    shapes = [(4, count, 128, 1024), (4, count, 128, 512)]
    gate_up, down = moved(own, [*here, *there], shapes, plan)
    return gate_up.reshape(D, 1024), down.reshape(D, 512)


def pack_kernel(n_p, own_ref, gain_ref, gate_ref, up_ref, down_ref, *outs):
    gain = jnp.broadcast_to(gain_ref[...], (128, 256))
    for s in range(4):
        for p in range(n_p):
            at = pl.multiple_of(((own_ref[0] ^ s) * n_p + p) * 256, 256)
            outs[s][p, :, pl.ds(0, 256)] = lowered(gate_ref[:, pl.ds(at, 256)] * gain)
            outs[s][p, :, pl.ds(256, 256)] = lowered(up_ref[:, pl.ds(at, 256)] * gain)
            outs[s][p, :, pl.ds(512, 256)] = lowered(down_ref[pl.ds(at, 256), :].T)


def pack_feed(own, gain, w_gate, w_up, w_down, n_p):
    vmem = pl.BlockSpec(memory_space=pltpu.VMEM)
    return pl.pallas_call(
        lambda *refs: pack_kernel(n_p, *refs),
        in_specs=[pl.BlockSpec(memory_space=pltpu.SMEM), vmem, vmem, vmem, vmem],
        out_specs=[vmem] * 4,
        out_shape=[jax.ShapeDtypeStruct((n_p, 128, 768), BF)] * 4,
        compiler_params=pltpu.CompilerParams(vmem_limit_bytes=40 * 1024 * 1024),
        name="pack_feed",
    )(own, gain, w_gate, w_up, w_down)


def squares_kernel(
    gain_one_ref, gain_two_ref, query_ref, key_ref, value_ref, gate_ref, up_ref,
    zero_ref, one_ref, feed_ref, squares_ref, first_ref, second_ref,
):
    @pl.when(pl.program_id(0) == 0)
    def _():
        squares_ref[...] = jnp.zeros_like(squares_ref)

    nothing = jnp.zeros((16, 128), F32)

    def sums(blocks):
        square, along = nothing, nothing
        for weight, gradient in blocks:
            gradient = gradient.astype(F32)
            square = square + gradient * gradient
            if weight is not None:
                along = along + lowered(weight).astype(F32) * gradient
        return square, along

    def lanes_of(t):
        return pl.ds(t * 128, 128)

    attention = [(query_ref[:, lanes_of(t)], zero_ref[t // 4, :, lanes_of(t % 4)]) for t in range(8)]
    attention += [(key_ref[:, lanes_of(t)], one_ref[t // 2, :, lanes_of(t % 2)]) for t in range(4)]
    attention += [
        (value_ref[:, lanes_of(t)], one_ref[t // 2, :, lanes_of(t % 2 + 2)]) for t in range(4)
    ]
    feed = [(gate_ref[:, lanes_of(t)], feed_ref[t // 2, :, lanes_of(t % 2)]) for t in range(32)]
    feed += [(up_ref[:, lanes_of(t)], feed_ref[t // 2, :, lanes_of(t % 2 + 2)]) for t in range(32)]
    plain = [(None, ref[l, :, lanes_of(t)]) for ref in (zero_ref, one_ref) for l in (0, 1) for t in (4, 5)]
    plain += [(None, feed_ref[c, :, lanes_of(t)]) for c in range(16) for t in (4, 5)]
    square_one, first_ref[...] = sums(attention)
    square_two, second_ref[...] = sums(feed)
    gain_one, gain_two = gain_one_ref[...], gain_two_ref[...]
    squares_ref[...] += (
        square_one * (gain_one * gain_one) + square_two * (gain_two * gain_two) + sums(plain)[0]
    )


def squares_of(gain_one, gain_two, masters, part_zero, part_one, came):
    def rows_of(width):
        return pl.BlockSpec((16, width), lambda i: (i, 0))

    w_query, w_key, w_value, _, w_gate, w_up, _ = masters
    weights = (w_query, w_key, w_value, w_gate, w_up)
    squares, first, second = pl.pallas_call(
        squares_kernel,
        grid=(8,),
        in_specs=[rows_of(1), rows_of(1)]
        + [rows_of(weight.shape[1]) for weight in weights]
        + [pl.BlockSpec((2, 16, 768), lambda i: (0, i, 0))] * 2
        + [pl.BlockSpec((16, 16, 768), lambda i: (0, i, 0))],
        out_specs=[pl.BlockSpec((16, 128), lambda i: (0, 0)), rows_of(128), rows_of(128)],
        out_shape=[jax.ShapeDtypeStruct((16, 128), F32)]
        + [jax.ShapeDtypeStruct((128, 128), F32)] * 2,
        compiler_params=pltpu.CompilerParams(
            dimension_semantics=("arbitrary",), vmem_limit_bytes=40 * 1024 * 1024
        ),
        name="squares",
    )(gain_one, gain_two, *weights, part_zero, part_one, came)
    return jnp.sum(squares), jnp.stack([jnp.sum(first, axis=1), jnp.sum(second, axis=1)])


STEP_ROWS = (128, 64, 64, 128, 512, 512, 512)
STEPS = 8


def adamw_kernel(rates, factor_ref, gain_one_ref, gain_two_ref, *refs):
    masters, firsts, seconds = refs[:7], refs[7:14], refs[14:21]
    query_ref, pair_ref, out_zero_ref, out_one_ref, feed_ref, down_ref = refs[21:27]
    new_refs, copy_refs = refs[27:34], refs[34:41]
    first_hbm, second_hbm, first_buf, second_buf, sems = refs[41:]
    step = pl.program_id(0)
    slot = lax.rem(step, 2)
    factor = factor_ref[0, 0]
    offsets = [sum(STEP_ROWS[:k]) for k in range(7)]

    def moves(of_step, of_slot):
        out = []
        for k in range(7):
            base = STEPS * offsets[k]
            for j, (buf, hbm) in enumerate(((first_buf, first_hbm), (second_buf, second_hbm))):
                out.append(
                    pltpu.make_async_copy(
                        buf.at[of_slot, pl.ds(offsets[k], STEP_ROWS[k])],
                        hbm.at[pl.ds(base + of_step * STEP_ROWS[k], STEP_ROWS[k])],
                        sems.at[of_slot, 2 * k + j],
                    )
                )
        return out

    @pl.when(step >= 2)
    def _():
        for move in moves(step - 2, slot):
            move.wait()

    def update(k, rows, lanes, flat, gradient):
        first = BETA_ONE * firsts[k][flat, :] + (1.0 - BETA_ONE) * gradient
        second = BETA_TWO * seconds[k][flat, :] + (1.0 - BETA_TWO) * gradient * gradient
        ratio = (
            first
            / (1.0 - BETA_ONE**STEP)
            / (jnp.sqrt(second / (1.0 - BETA_TWO**STEP)) + ADAM_EPS)
        )
        weight = masters[k][rows, lanes]
        weight = weight - rates[k] * (ratio + WEIGHT_DECAY * weight)
        new_refs[k][rows, lanes] = weight
        copy_refs[k][rows, lanes] = lowered(weight)
        return first, second

    def wide(k, gradient_of, scale):
        width = masters[k].shape[1] // 128
        for t in range(width):
            flat = pl.ds(t, 16, stride=width)
            first, second = update(
                k, slice(None), pl.ds(t * 128, 128), flat, gradient_of(t).astype(F32) * scale
            )
            store = pl.ds(offsets[k] + t, 16, stride=width)
            first_buf.at[slot][store, :] = first
            second_buf.at[slot][store, :] = second

    scale_one = jnp.broadcast_to(gain_one_ref[...] * factor, (16, 128))
    scale_two = jnp.broadcast_to(gain_two_ref[...] * factor, (16, 128))
    wide(0, lambda t: query_ref[t // 4, :, pl.ds(t % 4 * 128, 128)], scale_one)
    wide(1, lambda t: pair_ref[t // 2, :, pl.ds(t % 2 * 128, 128)], scale_one)
    wide(2, lambda t: pair_ref[t // 2, :, pl.ds(t % 2 * 128 + HD, 128)], scale_one)
    wide(4, lambda t: feed_ref[t // 2, :, pl.ds(t % 2 * 128, 128)], scale_two)
    wide(5, lambda t: feed_ref[t // 2, :, pl.ds(t % 2 * 128 + 256, 128)], scale_two)

    def tall(k, at, gradient):
        rows = pl.ds(at, 128)
        first, second = update(k, rows, slice(None), rows, gradient.astype(F32).T * factor)
        store = pl.ds(offsets[k] + at, 128)
        first_buf.at[slot][store, :] = first
        second_buf.at[slot][store, :] = second

    part = lax.rem(step // 2, 2) == 0
    tall(3, 0, jnp.where(part, out_zero_ref[0].astype(F32), out_one_ref[0].astype(F32)))
    for c in range(2):
        for t in range(2):
            tall(6, c * 256 + t * 128, down_ref[c, :, pl.ds(t * 128, 128)])

    for move in moves(step, slot):
        move.start()

    @pl.when(step == STEPS - 1)
    def _():
        for move in moves(step - 1, 1 - slot):
            move.wait()
        for move in moves(step, slot):
            move.wait()


def adamw_blocks(rates, factor, gain_one, gain_two, masters, moments, part_zero, part_one, came):
    shapes = [weight.shape for weight in masters]
    tables = [moment.reshape(-1, 128) for moment in moments]
    weight_specs = [
        pl.BlockSpec((shape[0] // STEPS, shape[1]), lambda i: (i, 0)) for shape in shapes
    ]
    starts = [sum(STEP_ROWS[:k]) * STEPS // STEP_ROWS[k] for k in range(7)]
    moment_specs = [
        pl.BlockSpec((STEP_ROWS[k], 128), lambda i, start=starts[k]: (start + i, 0))
        for k in range(7)
    ]
    gain_spec = pl.BlockSpec((16, 1), lambda i: (i, 0))
    rows_spec = pl.BlockSpec((2, 16, 2 * HD), lambda i: (0, i, 0))
    out_spec = pl.BlockSpec((1, 128, 128), lambda i: (i // 4, 0, 4 + i % 2))
    grad_specs = [
        rows_spec,
        rows_spec,
        out_spec,
        out_spec,
        pl.BlockSpec((16, 16, 512), lambda i: (0, i, 0)),
        pl.BlockSpec((2, 128, 256), lambda i: (i, 0, 2)),
    ]
    anywhere = pl.BlockSpec(memory_space=pl.ANY)
    outs = pl.pallas_call(
        lambda *refs: adamw_kernel(rates, *refs),
        grid=(STEPS,),
        in_specs=[
            pl.BlockSpec(memory_space=pltpu.SMEM),
            gain_spec,
            gain_spec,
            *weight_specs,
            *moment_specs,
            *moment_specs,
            *grad_specs,
        ],
        out_specs=[*weight_specs, *weight_specs, anywhere, anywhere],
        out_shape=[
            *[jax.ShapeDtypeStruct(shape, F32) for shape in shapes],
            *[jax.ShapeDtypeStruct(shape, BF) for shape in shapes],
            *[jax.ShapeDtypeStruct(table.shape, F32) for table in tables],
        ],
        scratch_shapes=[
            pltpu.VMEM((2, sum(STEP_ROWS), 128), F32),
            pltpu.VMEM((2, sum(STEP_ROWS), 128), F32),
            pltpu.SemaphoreType.DMA((2, 14)),
        ],
        compiler_params=pltpu.CompilerParams(
            dimension_semantics=("arbitrary",), vmem_limit_bytes=40 * 1024 * 1024
        ),
        name="adamw",
    )(
        factor.reshape(1, 1),
        gain_one,
        gain_two,
        *masters,
        *[tables[0]] * 7,
        *[tables[1]] * 7,
        part_zero,
        part_one,
        part_zero,
        part_one,
        came,
        came,
    )
    return outs[:7], outs[7:14], outs[14].reshape(-1), outs[15].reshape(-1)


def local(
    tokens,
    block_offsets,
    cotangent,
    w_query,
    w_key,
    w_value,
    w_out,
    w_gate,
    w_up,
    w_down,
    gains,
    moment_one,
    moment_two,
    gain_moment_one,
    gain_moment_two,
):
    lanes = Lanes()
    n_p, h = lanes.n_p, lanes.h
    n_ctx = 4 * n_p
    total_rows = n_ctx * 2 * SUB
    rows = D // n_ctx
    units = FF // (2 * n_ctx)
    chunk = 4 * SUB
    scaling = 1.0 / math.sqrt(HD)
    first_core = h == 0
    gain_low = lowered(gains).astype(F32)
    gain_one, gain_two = gain_low[0][:, None], gain_low[1][:, None]
    in_order = block_offsets[0] >= 0
    fits = rows == 128 and n_p == 4
    own = jnp.stack([lanes.z, lanes.p]).astype(jnp.int32)

    def stage(body):
        shapes = jax.eval_shape(body)
        return lax.cond(
            in_order, body, lambda: jax.tree.map(lambda a: jnp.zeros(a.shape, a.dtype), shapes)
        )

    def both_cores(own):
        other = lanes.swap(own)
        return jnp.where(
            first_core, jnp.concatenate([own, other]), jnp.concatenate([other, own])
        )

    def norm_back(inputs, inverse, incoming):
        inner = jnp.mean(incoming * inputs, axis=-1, keepdims=True)
        return inverse * incoming - inputs * (inverse * inverse * inverse * inner)

    x_own = lax.dynamic_slice_in_dim(tokens, h * SUB, SUB)
    dy_own = lax.dynamic_slice_in_dim(cotangent, h * SUB, SUB)
    near, far = lanes.over_z(x_own, 1), lanes.over_z(x_own, 2)

    query_part = lowered((w_query * gain_one).reshape(rows, 2, QW))
    key_part = lowered((w_key * gain_one).reshape(rows, 2, HD))
    value_part = lowered((w_value * gain_one).reshape(rows, 2, HD))
    out_part = lowered(w_out).T.reshape(rows, 2, QW)
    quarter = QW // 4
    out_parts = [out_part[:, :, k * quarter : (k + 1) * quarter] for k in range(4)]
    blocks = lanes.group_blocks(
        jnp.concatenate(
            [query_part[:, :, :HD], out_parts[0], query_part[:, :, HD:], out_parts[1]], axis=-1
        ),
        jnp.concatenate([key_part, out_parts[2], value_part, out_parts[3]], axis=-1),
    )
    x_pieces = [x_own, near, far, lanes.over_z(far, 1)]
    mine = lanes.send_z(blocks)
    if fits:
        feed = pack_feed(own, after(gain_two, blocks), w_gate, w_up, w_down, n_p)
    else:
        feed = w_gate * gain_two, w_up * gain_two, w_down.T
        feed = [lowered(matrix).reshape(rows, 4, n_p, units) for matrix in feed]
        feed = jnp.concatenate(feed, axis=-1).transpose(1, 2, 0, 3)
        feed = split_rows(own, feed, 0)
    mine = lanes.join_z(after(mine, feed[0]))
    dy_line = lax.all_gather(after(dy_own, mine), "z", axis=0, tiled=False)
    feed = after(list(feed), mine, *x_pieces)
    feed = [feed[0]] + [lanes.over_z(feed[step], step) for step in (1, 2, 3)]

    x_chunk = jnp.concatenate(x_pieces).astype(F32)
    inverse_chunk = lax.rsqrt(jnp.mean(x_chunk * x_chunk, axis=-1, keepdims=True) + NORM_EPS)
    normed = lowered(x_chunk * inverse_chunk)

    def in_parts(four):
        here, there = four[:2], four[2:]
        zero = [jnp.where(first_core, a, b) for a, b in zip(here, there)]
        return zero + [jnp.where(first_core, b, a) for a, b in zip(here, there)]

    def gather_weights():
        cubes = [
            lanes.gather_cube(half, order) for half, order in zip(lanes.halves(mine), lanes.orders())
        ]
        weights = [weight.reshape(D, weight.shape[-1]) for weight in placed(own, cubes, False)]
        weights = weights + [lanes.swap(weight) for weight in weights]
        return weights, in_parts([product(normed, weight)[:, :HD] for weight in weights])

    weights, projected = stage(gather_weights)
    dy_all = lax.all_gather(after(dy_line, projected[0]), "p", axis=1, tiled=False)
    dy_all = dy_all.reshape(n_ctx * SUB, D)

    def attention_forward():
        line = lanes.z ^ jnp.arange(4, dtype=jnp.int32)
        ring = lanes.p ^ jnp.arange(n_p, dtype=jnp.int32)
        cores = h ^ jnp.arange(2, dtype=jnp.int32)
        within = jnp.arange(SUB, dtype=jnp.int32)
        key_blocks = 2 * (line[None, None, :] * n_p + ring[None, :, None]) + cores[:, None, None]
        key_positions = (block_offsets[key_blocks.reshape(-1)][:, None] + within).reshape(-1)
        my_positions = key_positions[:chunk]
        cosine, sine = rotary_tables(my_positions)
        query_heads = lowered(
            jnp.concatenate([rotate(one, cosine, sine) for one in projected[:SHARE]])
        )
        key_here = lowered(rotate(projected[2], cosine, sine))
        value_here = lowered(projected[3])
        everywhere = []
        for array_in, order in zip((key_here, value_here), lanes.orders()):
            plane = lanes.gather_p(array_in, order, True).reshape(n_p * chunk, HD)
            everywhere.append(jnp.concatenate([plane, lanes.swap(plane)]))
        keys_all, values_all = everywhere
        allowed = key_positions[None, :] <= my_positions[:, None]
        allowed = jnp.concatenate([allowed] * SHARE)
        scores = contract(query_heads, keys_all, 1, 1) * scaling
        scores = jnp.where(allowed, scores, MASKED_SCORE)
        largest = jnp.max(scores, axis=-1, keepdims=True)
        expos = jnp.exp(scores - largest)
        probs = expos / jnp.sum(expos, axis=-1, keepdims=True)
        attended = lowered(product(lowered(probs), values_all))
        mixed = jnp.concatenate([attended[:chunk], attended[chunk:]], axis=-1)
        quarters = in_parts([mixed[:, k * quarter : (k + 1) * quarter] for k in range(4)])
        resid_part = sum(
            contract(jnp.pad(part, ((0, 0), (HD, 0))), weight, 1, 1)
            for part, weight in zip(quarters, weights)
        )
        return (
            cosine,
            sine,
            query_heads,
            keys_all,
            values_all,
            probs,
            mixed,
            lowered(resid_part).reshape(4, SUB, D),
        )

    (
        cosine,
        sine,
        query_heads,
        keys_all,
        values_all,
        probs,
        mixed,
        resid_part,
    ) = stage(attention_forward)
    feed = turned(own, after(feed, resid_part), 0)
    resid_part = after(resid_part, *feed)
    feed = [feed[0]] + [lanes.over_p(feed[e], e) for e in range(1, n_p)]

    def second_norm():
        resid = x_own.astype(F32) + lanes.scatter_z(resid_part, True)
        inverse_two = lax.rsqrt(jnp.mean(resid * resid, axis=-1, keepdims=True) + NORM_EPS)
        normed_two = lowered(resid * inverse_two)
        return resid, inverse_two, lanes.absolute(lanes.gather_z(normed_two), lanes.z)

    resid, inverse_two, stacked = stage(second_norm)
    feed = after(feed, stacked)
    if fits:
        gate_up_weight, down_weight = feed_weights(own, feed, [lanes.swap(piece) for piece in feed])
    else:
        feed = joined(own, feed, 1).reshape(D, 3 * units)
        feed = [feed, lanes.swap(feed)]
        gate_up_weight = jnp.concatenate([here[:, : 2 * units] for here in feed], axis=-1)
        down_weight = jnp.concatenate([here[:, 2 * units :] for here in feed], axis=-1)

    def feed_forward():
        cubes = [
            lanes.gather_cube(half, order)
            for half, order in zip(lanes.halves(stacked), lanes.orders())
        ]
        normed_all = placed(own, cubes, True)[0].reshape(n_ctx * SUB, D)
        d_hidden = product(dy_all, down_weight)
        gate_up = product(normed_all, gate_up_weight)
        d_gate_up, hidden = [], []
        for core in range(2):
            gate_values = gate_up[:, 2 * core * units : (2 * core + 1) * units]
            up_values = gate_up[:, (2 * core + 1) * units : (2 * core + 2) * units]
            incoming = d_hidden[:, core * units : (core + 1) * units]
            sigmoid_gate = jax.nn.sigmoid(gate_values)
            activated = gate_values * sigmoid_gate
            hidden.append(lowered(activated * up_values))
            slope = sigmoid_gate * (1.0 + gate_values * (1.0 - sigmoid_gate))
            d_gate_up.append(lowered(incoming * up_values * slope))
            d_gate_up.append(lowered(incoming * activated))
        d_gate_up = jnp.concatenate(d_gate_up, axis=-1)
        hidden = jnp.concatenate(hidden, axis=-1)
        d_normed_parts = []
        for part, order in zip((slice(0, D // 2), slice(D // 2, D)), lanes.orders()):
            partial = contract(d_gate_up, gate_up_weight[part], 1, 1)
            cube = partial.reshape([4] + lanes.cube + [SUB, D // 2])
            d_normed_parts.append(lanes.scatter_p(cube, order, False, 1))
        home_gate_up = contract(normed_all, d_gate_up[:, : 2 * units], 0, 0)
        home_down = contract(dy_all, hidden[:, :units], 0, 0)
        away = jnp.concatenate(
            [
                lowered(contract(normed_all, d_gate_up[:, 2 * units :], 0, 0)),
                lowered(contract(dy_all, hidden[:, units:], 0, 0)),
            ],
            axis=-1,
        )
        came = lanes.swap(away)
        if fits:
            came = add_split(own, n_p, home_gate_up, home_down, came)
        else:
            home = jnp.concatenate([home_gate_up, home_down], axis=-1)
            came = lowered(home + came.astype(F32)).reshape(4, n_p, rows, 3 * units)
            came = split_rows(own, came, 1)
        out_part = lowered(contract(hidden, down_weight, 1, 1))
        out_part = out_part.reshape(4, n_p, SUB, D).transpose(1, 0, 2, 3)
        return jnp.concatenate(d_normed_parts, axis=-1), list(came), out_part

    d_normed_part, came, out_part = stage(feed_forward)
    came = [came[0]] + [lanes.over_p(came[e], e) for e in range(1, n_p)]
    out_line = lax.psum_scatter(out_part, "p", scatter_dimension=0, tiled=False)

    def attention_backward():
        d_normed_two = lanes.scatter_z(d_normed_part, False)
        d_resid = dy_own.astype(F32) + norm_back(resid, inverse_two, d_normed_two)
        d_resid_chunk = jnp.concatenate(lanes.gather_z(lowered(d_resid)))
        d_mixed = in_parts([product(d_resid_chunk, weight)[:, HD:] for weight in weights])
        d_mixed = lowered(jnp.concatenate(d_mixed, axis=-1))
        d_attended = jnp.concatenate([d_mixed[:, :HD], d_mixed[:, HD:]])
        d_probs = contract(d_attended, values_all, 1, 1)
        delta = jnp.sum(probs * d_probs, axis=-1, keepdims=True)
        d_scores = lowered(probs * (d_probs - delta))
        d_query_heads = product(d_scores, keys_all) * scaling
        d_key_all = contract(d_scores, query_heads, 0, 0) * scaling
        d_value_all = contract(lowered(probs), d_attended, 0, 0)
        middle = n_p * chunk
        halves = []
        for whole in (d_key_all, d_value_all):
            halves.append(whole[:middle] + lanes.swap(lowered(whole[middle:])).astype(F32))
        return d_resid, d_resid_chunk, d_query_heads, halves

    d_resid, d_resid_chunk, d_query_heads, d_pair_halves = stage(attention_backward)
    came = turned(own, after(came, d_query_heads), 1)
    d_query_heads = after(d_query_heads, *came)
    came = [came[0]] + [lanes.over_z(came[step], step) for step in (1, 2, 3)]

    def attention_gradients():
        d_key, d_value = [
            lanes.scatter_p(half.reshape(lanes.cube + [chunk, HD]), order, True)
            for half, order in zip(d_pair_halves, lanes.orders())
        ]
        d_key = lowered(rotate(d_key, cosine, -sine))
        d_value = lowered(d_value)
        d_query = [
            lowered(rotate(one, cosine, -sine))
            for one in (d_query_heads[:chunk], d_query_heads[chunk:])
        ]
        lefts = (normed, d_resid_chunk)
        rights = [d_query[0], mixed[:, :quarter], d_query[1], mixed[:, quarter : 2 * quarter]]
        others = [d_key, mixed[:, 2 * quarter : 3 * quarter], d_value, mixed[:, 3 * quarter :]]
        keep, away = [], []
        for k in range(4):
            mine, theirs = jnp.where(first_core, rights[k], others[k]), jnp.where(
                first_core, others[k], rights[k]
            )
            keep.append(contract(lefts[k % 2], mine, 0, 0))
            away.append(lowered(contract(lefts[k % 2], theirs, 0, 0)))
        summed = []
        for at, order in zip((0, 2), lanes.orders()):
            half = jnp.concatenate(keep[at : at + 2], axis=-1)
            half = half + lanes.swap(jnp.concatenate(away[at : at + 2], axis=-1)).astype(F32)
            cube = lowered(half).reshape(4, n_p, rows, half.shape[-1])
            have = list(range(lanes.bits))
            for b in order:
                keep_cube, send = halved(own, cube, have.index(b), b)
                cube = keep_cube.astype(F32) + lanes.over_p(send, 1 << b).astype(F32)
                cube = lowered(cube)
                have.remove(b)
            summed.append(cube.reshape(4, rows, half.shape[-1]))
        in_turn = [half[..., :HD] for half in summed] + [half[..., HD:] for half in summed]
        part_zero, part_one = lanes.group_home(jnp.concatenate(in_turn, axis=-1))
        return part_zero, part_one, in_parts(d_query + [d_key, d_value])

    part_zero, part_one, d_projected = stage(attention_gradients)

    d_normed_part = sum(
        contract(jnp.pad(part, ((0, 0), (0, quarter))), weight, 1, 1)
        for part, weight in zip(d_projected, weights)
    ).reshape(4, SUB, D)
    line_parts = [
        [d_normed_part[s] for s in range(4)],
        [pick(out_line, lanes.z ^ s, 0).astype(F32) for s in range(4)],
    ]
    line_near = [
        lanes.over_z(lowered(jnp.stack([parts[3], parts[1]])), 1) for parts in line_parts
    ]

    came = joined(own, after(came, part_zero), 0).reshape(n_ctx, rows, 3 * units)
    masters = (w_query, w_key, w_value, w_out, w_gate, w_up, w_down)
    if fits:
        squares, grad_gains = squares_of(gain_one, gain_two, masters, part_zero, part_one, came)
    else:

        def of_owner(k):
            part = came[:, :, k * units : (k + 1) * units].transpose(1, 0, 2)
            return part.reshape(rows, n_ctx * units).astype(F32)

        inner_gate, inner_up, grad_down = of_owner(0), of_owner(1), of_owner(2).T
        grad_out = jnp.concatenate([part_zero[:, :, QW:], part_one[:, :, QW:]], axis=-1)
        grad_out = grad_out.astype(F32).transpose(0, 2, 1).reshape(2 * QW, rows)
        inner_query = part_zero[:, :, :QW].astype(F32).transpose(1, 0, 2).reshape(rows, 2 * QW)
        inner_pair = part_one[:, :, :QW].astype(F32).transpose(1, 0, 2)
        inner_key = inner_pair[:, :, :HD].reshape(rows, 2 * HD)
        inner_value = inner_pair[:, :, HD:].reshape(rows, 2 * HD)

        def weighed(matrix, inner):
            return jnp.sum(lowered(matrix).astype(F32) * inner, axis=1)

        first = weighed(w_query, inner_query) + weighed(w_key, inner_key)
        grad_gains = jnp.stack(
            [
                first + weighed(w_value, inner_value),
                weighed(w_gate, inner_gate) + weighed(w_up, inner_up),
            ]
        )
        gradients = (
            inner_query * gain_one,
            inner_key * gain_one,
            inner_value * gain_one,
            grad_out,
            inner_gate * gain_two,
            inner_up * gain_two,
            grad_down,
        )
        squares = sum(jnp.sum(gradient * gradient) for gradient in gradients)
    shared = jnp.concatenate([grad_gains, jnp.broadcast_to(squares, (6, rows))])
    shared = shared + lanes.swap(shared)
    grad_gains = shared[:2]
    squares = jnp.broadcast_to(shared[2:3, :1] + jnp.sum(grad_gains * grad_gains), (8, 128))
    for b in range(lanes.bits):
        squares = squares + lanes.over_p(squares, 1 << b)
    for s in (1, 2):
        squares = squares + lanes.over_z(squares, s)
    line_near = [near.astype(F32) for near in after(line_near, squares)]
    line_far = [
        lanes.over_z(lowered(parts[2] + near[0]), 2)
        for parts, near in zip(line_parts, line_near)
    ]
    grad_norm = jnp.sqrt(squares[0, 0])
    factor = CLIP_NORM / jnp.maximum(grad_norm, CLIP_NORM)
    wo_fan = min(HQ * HD, max(2, 131072 // total_rows))
    rate_in = 2.0 / math.sqrt(D)
    step_rates = (
        rate_in,
        rate_in,
        rate_in,
        2.0 / math.sqrt(wo_fan),
        rate_in,
        rate_in,
        2.0 / math.sqrt(FF),
    )
    if fits:
        new_weights, copies, moment_first, moment_second = adamw_blocks(
            step_rates,
            factor,
            gain_one,
            gain_two,
            masters,
            (moment_one, moment_two),
            part_zero,
            part_one,
            came,
        )
    else:
        new_weights = []
        firsts = []
        seconds = []
        offset = 0
        for index_now in range(7):
            weight = masters[index_now]
            length = weight.size
            first_moment = moment_one[offset : offset + length].reshape(weight.shape)
            second_moment = moment_two[offset : offset + length].reshape(weight.shape)
            updated, first_new, second_new = adamw_step(
                weight,
                factor * gradients[index_now],
                first_moment,
                second_moment,
                step_rates[index_now],
                WEIGHT_DECAY,
            )
            new_weights.append(updated)
            firsts.append(first_new.reshape(-1))
            seconds.append(second_new.reshape(-1))
            offset = offset + length
        copies = [lowered(weight) for weight in new_weights]
        moment_first, moment_second = jnp.concatenate(firsts), jnp.concatenate(seconds)
    line_far = after(line_far, new_weights[0])
    d_normed, out_sum = [
        parts[0] + near[1] + far.astype(F32)
        for parts, near, far in zip(line_parts, line_near, line_far)
    ]
    x_float = x_own.astype(F32)
    inverse_own = lax.rsqrt(jnp.mean(x_float * x_float, axis=-1, keepdims=True) + NORM_EPS)
    input_grad = lowered(d_resid + norm_back(x_float, inverse_own, d_normed))
    input_grad, layer_out = both_cores(input_grad), both_cores(lowered(resid + out_sum))
    new_gains, gain_first, gain_second = adamw_step(
        gains, factor * grad_gains, gain_moment_one, gain_moment_two, GAIN_RATE, 0.0
    )
    return (
        layer_out,
        input_grad,
        grad_norm,
        *new_weights,
        new_gains,
        *copies,
        lowered(new_gains),
        moment_first,
        moment_second,
        gain_first,
        gain_second,
    )


def solution(mesh):
    n_ctx, n_head = mesh.devices.shape
    lanes_mesh = Mesh(mesh.devices.reshape(4, n_ctx // 4, n_head), ("z", "p", "head"))
    ctx = ("z", "p")
    rows = P(ctx, None)
    wide = P(ctx, "head")
    tall = P("head", ctx)
    flat = P(("z", "p", "head"))
    gain = P(None, ctx)
    weights = (wide, wide, wide, tall, wide, wide, tall, gain)
    return jax.shard_map(
        local,
        mesh=lanes_mesh,
        in_specs=(rows, P(), rows, *weights, flat, flat, gain, gain),
        out_specs=(rows, rows, P(), *weights, *weights, flat, flat, gain, gain),
        check_vma=False,
    )
```

```python
import math

import jax
import jax.numpy as jnp
from jax import lax
from jax.experimental import pallas as pl
from jax.experimental.pallas import tpu as pltpu
from jax.sharding import Mesh
from jax.sharding import PartitionSpec as P

D = 2048
HQ = 8
KV = 4
HD = 256
FF = 8192
SUB = 64
STEP = 10
SHARE = HQ // KV
QW = SHARE * HD


NORM_EPS = 1e-06
ROPE_BASE = 1000042.0
BETA_ONE = 0.9
BETA_TWO = 0.95
ADAM_EPS = 1e-08
WEIGHT_DECAY = 0.1
GAIN_RATE = 0.5
CLIP_NORM = 1.0
MASKED_SCORE = -1e30
BF = jnp.bfloat16
F32 = jnp.float32
SWAP = [(0, 1), (1, 0)]


def lowered(array_in):
    return array_in.astype(BF)


def product(left, right):
    return jnp.dot(left, right, preferred_element_type=F32)


def contract(left, right, left_dim, right_dim):
    return lax.dot_general(
        left, right, (((left_dim,), (right_dim,)), ((), ())), preferred_element_type=F32
    )


def rotary_tables(positions):
    frequency = ROPE_BASE ** (-jnp.arange(0, HD, 2, dtype=F32) / HD)
    angles = positions.astype(F32)[:, None] * frequency[None, :]
    return (jnp.cos(angles), jnp.sin(angles))


def rotate(one_head, cosine, sine):
    half_size = HD // 2
    first_half = one_head[:, :half_size]
    second_half = one_head[:, half_size:]
    return jnp.concatenate(
        [first_half * cosine - second_half * sine, second_half * cosine + first_half * sine],
        axis=-1,
    )


def adamw_step(weight, gradient, first_moment, second_moment, step_rate, decay_rate):
    first_new = BETA_ONE * first_moment + (1.0 - BETA_ONE) * gradient
    second_new = BETA_TWO * second_moment + (1.0 - BETA_TWO) * gradient * gradient
    ratio = (
        first_new
        / (1.0 - BETA_ONE**STEP)
        / (jnp.sqrt(second_new / (1.0 - BETA_TWO**STEP)) + ADAM_EPS)
    )
    return (weight - step_rate * (ratio + decay_rate * weight), first_new, second_new)


def pick(array_in, index, axis):
    return lax.dynamic_index_in_dim(array_in, index, axis, keepdims=False)


def after(arrays, *others):
    listed = arrays if isinstance(arrays, list) else [arrays]
    if not others:
        return arrays
    anywhere = pl.BlockSpec(memory_space=pl.ANY)
    out = pl.pallas_call(
        lambda *refs: None,
        in_specs=[anywhere] * (len(listed) + len(others)),
        out_specs=[anywhere] * len(listed),
        out_shape=[jax.ShapeDtypeStruct(array.shape, array.dtype) for array in listed],
        input_output_aliases={k: k for k in range(len(listed))},
        name="after",
    )(*listed, *others)
    return list(out) if isinstance(arrays, list) else out[0]


class Lanes:
    def __init__(self):
        self.n_p = lax.axis_size("p")
        self.z = lax.axis_index("z")
        self.p = lax.axis_index("p")
        self.h = lax.axis_index("head")
        self.bits = self.n_p.bit_length() - 1
        self.cube = [2] * self.bits

    def swap(self, array_in):
        return lax.ppermute(array_in, "head", SWAP)

    def over_z(self, array_in, step):
        return lax.ppermute(array_in, "z", [(i, i ^ step) for i in range(4)])

    def over_p(self, array_in, step):
        return lax.ppermute(array_in, "p", [(i, i ^ step) for i in range(self.n_p)])

    def orders(self):
        return list(range(self.bits)), list(range(self.bits))[::-1]

    def bit(self, b):
        return (self.p >> b) & 1

    def absolute(self, pieces, index, axis=0):
        for b in range(len(pieces).bit_length() - 1):
            odd = ((index >> b) & 1) == 1
            pieces = [jnp.where(odd, pieces[j ^ (1 << b)], pieces[j]) for j in range(len(pieces))]
        return jnp.stack(pieces, axis)

    def gather_z(self, array_in):
        one, two = self.over_z(array_in, 1), self.over_z(array_in, 2)
        return [array_in, one, two, self.over_z(two, 1)]

    def send_z(self, array_in, axis=0):
        pieces = [pick(array_in, self.z, axis)]
        for s in (1, 2, 3):
            pieces.append(self.over_z(pick(array_in, self.z ^ s, axis), s))
        return pieces

    def join_z(self, pieces, axis=0):
        return self.absolute(pieces, self.z, axis)

    def scatter_z(self, array_in, relative):
        parts = [pick(array_in, s if relative else self.z ^ s, 0).astype(F32) for s in range(4)]
        near = self.over_z(lowered(jnp.stack([parts[3], parts[1]])), 1).astype(F32)
        far = self.over_z(lowered(parts[2] + near[0]), 2).astype(F32)
        return parts[0] + near[1] + far

    def gather_p(self, array_in, order, relative, lead=0):
        have = []
        for b in order:
            other = self.over_p(array_in, 1 << b)
            axis = lead + sum(1 for x in have if x > b)
            mine, other = jnp.expand_dims(array_in, axis), jnp.expand_dims(other, axis)
            array_in = jnp.concatenate([mine, other], axis)
            if not relative:
                array_in = jnp.where(
                    self.bit(b) == 1, jnp.concatenate([other, mine], axis), array_in
                )
            have.append(b)
        return array_in

    def gather_cube(self, array_in, order):
        held = [(array_in[None], [0])]
        for b in order:
            numbers = [j for _, part in held for j in part]
            whole = jnp.concatenate([array for array, _ in held]) if len(held) > 1 else held[0][0]
            held.append((self.over_p(whole, 1 << b), [j ^ (1 << b) for j in numbers]))
        return held

    def scatter_p(self, array_in, order, relative, lead=0):
        have = list(range(self.bits))
        for b in order:
            axis = lead + sum(1 for x in have if x > b)
            bit = 0 if relative else self.bit(b)
            keep, send = pick(array_in, bit, axis), pick(array_in, 1 - bit, axis)
            array_in = keep.astype(F32) + self.over_p(lowered(send), 1 << b).astype(F32)
            have.remove(b)
        return array_in

    def halves(self, array_in):
        middle = array_in.shape[-1] // 2
        return array_in[..., :middle], array_in[..., middle:]

    def group_blocks(self, part_zero, part_one):
        first = self.h == 0
        keep = jnp.where(first, part_zero, part_one).transpose(1, 0, 2)
        other = self.swap(jnp.where(first, part_one, part_zero).transpose(1, 0, 2))
        return jnp.where(
            first, jnp.concatenate([keep, other]), jnp.concatenate([other, keep])
        )

    def group_home(self, summed):
        first = self.h == 0
        blocks = summed
        for b in (1, 0):
            shape = (2, 2) + summed.shape[1:]
            bit = (self.z >> b) & 1
            cube = blocks.reshape(shape)
            keep, send = pick(cube, bit, 1 - b), pick(cube, 1 - bit, 1 - b)
            other = self.over_z(send, 1 << b)
            keep, other = jnp.expand_dims(keep, 1 - b), jnp.expand_dims(other, 1 - b)
            blocks = jnp.where(
                bit == 1,
                jnp.concatenate([other, keep], 1 - b),
                jnp.concatenate([keep, other], 1 - b),
            ).reshape(summed.shape)
        own = jnp.where(first, blocks[:2], blocks[2:])
        other = self.swap(jnp.where(first, blocks[2:], blocks[:2]))
        return jnp.where(first, own, other), jnp.where(first, other, own)


def moved(own, inputs, shapes, plan):
    def kernel(own_ref, *refs):
        ins, outs = refs[: len(inputs)], refs[len(inputs) :]
        for source, target in plan(ins, outs, own_ref[0], own_ref[1]):
            target[...] = source[...]

    vmem = pl.BlockSpec(memory_space=pltpu.VMEM)
    return pl.pallas_call(
        kernel,
        in_specs=[pl.BlockSpec(memory_space=pltpu.SMEM)] + [vmem] * len(inputs),
        out_specs=[vmem] * len(shapes),
        out_shape=[jax.ShapeDtypeStruct(shape, inputs[0].dtype) for shape in shapes],
        compiler_params=pltpu.CompilerParams(vmem_limit_bytes=60 * 1024 * 1024),
        name="moved",
    )(own, *inputs)


def split_rows(own, array_in, which):
    count = array_in.shape[which]
    shape = array_in.shape[:which] + array_in.shape[which + 1 :]

    def plan(ins, outs, z, p):
        if which == 0:
            return [(ins[0].at[z ^ j], outs[j]) for j in range(count)]
        return [(ins[0].at[:, p ^ j], outs[j]) for j in range(count)]

    return moved(own, [array_in], [shape] * count, plan)


def joined(own, pieces, which):
    count = len(pieces)
    shape = pieces[0].shape
    shape = shape[:which] + (count,) + shape[which:]

    def plan(ins, outs, z, p):
        if which == 0:
            return [(ins[j], outs[0].at[z ^ j]) for j in range(count)]
        return [(ins[j], outs[0].at[:, p ^ j]) for j in range(count)]

    return moved(own, pieces, [shape], plan)[0]


def turned(own, pieces, which):
    count = len(pieces)
    other = pieces[0].shape[0]
    shape = (count,) + pieces[0].shape[1:]

    def plan(ins, outs, z, p):
        mine, theirs = (z, p) if which == 0 else (p, z)
        return [
            (ins[i].at[theirs ^ j], outs[j].at[mine ^ i])
            for i in range(count)
            for j in range(other)
        ]

    return moved(own, pieces, [shape] * other, plan)


def halved(own, array_in, at, b):
    count = array_in.shape[1] // 2
    shape = (array_in.shape[0], count) + array_in.shape[2:]

    def plan(ins, outs, z, p):
        bit = (p >> b) & 1
        pairs = []
        for k in range(count):
            rest = ((k >> at) << (at + 1)) | (k & ((1 << at) - 1))
            for target, value in ((outs[0], bit), (outs[1], 1 - bit)):
                pairs.append((ins[0].at[:, rest + value * (1 << at)], target.at[:, k]))
        return pairs

    return moved(own, [array_in], [shape] * 2, plan)


def placed(own, halves, in_front):
    arrays = [array for half in halves for array, _ in half]
    n_p = sum(len(numbers) for _, numbers in halves[0])
    block = halves[0][0][0].shape[1:]
    widths = [half[0][0].shape[-1] for half in halves]
    lead = (n_p, block[0]) if in_front else (block[0], n_p)
    shapes = [lead + block[1:-1] + (sum(widths),)]

    def plan(ins, outs, z, p):
        pairs, at = [], 0
        for k, half in enumerate(halves):
            lanes = pl.ds(sum(widths[:k]), widths[k])
            for _, numbers in half:
                for i, j in enumerate(numbers):
                    if in_front:
                        target = outs[0].at[p ^ j, :, :, lanes]
                    else:
                        target = outs[0].at[:, p ^ j, :, lanes]
                    pairs.append((ins[at].at[i], target))
                at = at + 1
        return pairs

    return moved(own, arrays, shapes, plan)[0]


def add_split(own, n_p, gate_up, down, came):
    rows = gate_up.shape[0] // (4 * n_p)

    def kernel(own_ref, gate_up_ref, down_ref, came_ref, *outs):
        for j in range(n_p):
            for z in range(4):
                at = pl.multiple_of((z * n_p + (own_ref[1] ^ j)) * rows, rows)
                at = pl.ds(at, rows)
                for ref, lanes in ((gate_up_ref, pl.ds(0, 512)), (down_ref, pl.ds(512, 256))):
                    outs[j][z, :, lanes] = lowered(ref[at, :] + came_ref[at, lanes].astype(F32))

    vmem = pl.BlockSpec(memory_space=pltpu.VMEM)
    return pl.pallas_call(
        kernel,
        in_specs=[pl.BlockSpec(memory_space=pltpu.SMEM), vmem, vmem, vmem],
        out_specs=[vmem] * n_p,
        out_shape=[jax.ShapeDtypeStruct((4, rows, 768), BF)] * n_p,
        compiler_params=pltpu.CompilerParams(vmem_limit_bytes=60 * 1024 * 1024),
        name="add_split",
    )(own, gate_up, down, came)


def feed_weights(own, pieces):
    count = len(pieces)

    def plan(ins, outs, z, p):
        pairs = []
        for j in range(count):
            pairs.append((ins[j].at[:, :, pl.ds(0, 512)], outs[0].at[:, p ^ j]))
            pairs.append((ins[j].at[:, :, pl.ds(512, 256)], outs[1].at[:, p ^ j]))
        return pairs

    gate_up, down = moved(own, pieces, [(4, count, 128, 512), (4, count, 128, 256)], plan)
    return [gate_up.reshape(D, 512), down.reshape(D, 256)]


def pack_kernel(n_p, own_ref, gain_ref, gate_ref, up_ref, down_ref, *outs):
    gain = jnp.broadcast_to(gain_ref[...], (128, 256))
    for s in range(4):
        for p in range(n_p):
            at = pl.multiple_of(((own_ref[0] ^ s) * n_p + p) * 256, 256)
            outs[s][p, :, pl.ds(0, 256)] = lowered(gate_ref[:, pl.ds(at, 256)] * gain)
            outs[s][p, :, pl.ds(256, 256)] = lowered(up_ref[:, pl.ds(at, 256)] * gain)
            outs[s][p, :, pl.ds(512, 256)] = lowered(down_ref[pl.ds(at, 256), :].T)


def pack_feed(own, gain, w_gate, w_up, w_down, n_p):
    vmem = pl.BlockSpec(memory_space=pltpu.VMEM)
    return pl.pallas_call(
        lambda *refs: pack_kernel(n_p, *refs),
        in_specs=[pl.BlockSpec(memory_space=pltpu.SMEM), vmem, vmem, vmem, vmem],
        out_specs=[vmem] * 4,
        out_shape=[jax.ShapeDtypeStruct((n_p, 128, 768), BF)] * 4,
        compiler_params=pltpu.CompilerParams(vmem_limit_bytes=60 * 1024 * 1024),
        name="pack_feed",
    )(own, gain, w_gate, w_up, w_down)


def squares_kernel(
    gain_one_ref, gain_two_ref, query_ref, key_ref, value_ref, gate_ref, up_ref,
    zero_ref, one_ref, feed_ref, out_ref, squares_ref, first_ref, second_ref,
):
    step = pl.program_id(0)
    here = pl.ds(pl.multiple_of(step * 16, 16), 16)

    @pl.when(step == 0)
    def _():
        squares_ref[...] = jnp.zeros_like(squares_ref)

    nothing = jnp.zeros((16, 128), F32)

    def sums(blocks):
        square, along = nothing, nothing
        for weight, gradient in blocks:
            gradient = gradient.astype(F32)
            square = square + gradient * gradient
            if weight is not None:
                along = along + lowered(weight).astype(F32) * gradient
        return square, along

    def lanes_of(t):
        return pl.ds(t * 128, 128)

    attention = [(query_ref[:, lanes_of(t)], zero_ref[t // 4, :, lanes_of(t % 4)]) for t in range(8)]
    attention += [(key_ref[:, lanes_of(t)], one_ref[t // 2, :, lanes_of(t % 2)]) for t in range(4)]
    attention += [
        (value_ref[:, lanes_of(t)], one_ref[t // 2, :, lanes_of(t % 2 + 2)]) for t in range(4)
    ]
    feed = [(gate_ref[:, lanes_of(t)], feed_ref[t // 2, :, lanes_of(t % 2)]) for t in range(32)]
    feed += [(up_ref[:, lanes_of(t)], feed_ref[t // 2, :, lanes_of(t % 2 + 2)]) for t in range(32)]
    plain = [(None, ref[l, :, lanes_of(t)]) for ref in (zero_ref, one_ref) for l in (0, 1) for t in (4, 5)]
    plain += [(None, feed_ref[c, :, lanes_of(t)]) for c in range(16) for t in (4, 5)]
    square_one, first_ref[here, :] = sums(attention)
    square_two, second_ref[here, :] = sums(feed)
    gain_one, gain_two = gain_one_ref[...], gain_two_ref[...]
    squares_ref[...] += (
        square_one * (gain_one * gain_one) + square_two * (gain_two * gain_two) + sums(plain)[0]
    )

    @pl.when(step == 7)
    def _():
        out_ref[...] = jnp.broadcast_to(jnp.sum(squares_ref[...], keepdims=True), (8, 128))
        out_ref[0:1, :] = jnp.sum(first_ref[...].T, axis=0, keepdims=True)
        out_ref[1:2, :] = jnp.sum(second_ref[...].T, axis=0, keepdims=True)


def squares_of(gain_one, gain_two, masters, part_zero, part_one, came):
    def rows_of(width):
        return pl.BlockSpec((16, width), lambda i: (i, 0))

    w_query, w_key, w_value, _, w_gate, w_up, _ = masters
    weights = (w_query, w_key, w_value, w_gate, w_up)
    return pl.pallas_call(
        squares_kernel,
        grid=(8,),
        in_specs=[rows_of(1), rows_of(1)]
        + [rows_of(weight.shape[1]) for weight in weights]
        + [pl.BlockSpec((2, 16, 768), lambda i: (0, i, 0))] * 2
        + [pl.BlockSpec((16, 16, 768), lambda i: (0, i, 0))],
        out_specs=pl.BlockSpec((8, 128), lambda i: (0, 0)),
        out_shape=jax.ShapeDtypeStruct((8, 128), F32),
        scratch_shapes=[
            pltpu.VMEM((16, 128), F32),
            pltpu.VMEM((128, 128), F32),
            pltpu.VMEM((128, 128), F32),
        ],
        compiler_params=pltpu.CompilerParams(
            dimension_semantics=("arbitrary",), vmem_limit_bytes=60 * 1024 * 1024
        ),
        name="squares",
    )(gain_one, gain_two, *weights, part_zero, part_one, came)


STEP_ROWS = (128, 64, 64, 128, 512, 512, 512)
STEPS = 8


def adamw_kernel(rates, factor_ref, gain_one_ref, gain_two_ref, *refs):
    masters, firsts, seconds = refs[:7], refs[7:14], refs[14:21]
    query_ref, pair_ref, out_zero_ref, out_one_ref, feed_ref, down_ref = refs[21:27]
    new_refs, copy_refs = refs[27:34], refs[34:41]
    first_hbm, second_hbm, first_buf, second_buf, sems = refs[41:]
    step = pl.program_id(0)
    slot = lax.rem(step, 2)
    factor = factor_ref[0, 0]
    offsets = [sum(STEP_ROWS[:k]) for k in range(7)]

    def moves(of_step, of_slot):
        out = []
        for k in range(7):
            base = STEPS * offsets[k]
            for j, (buf, hbm) in enumerate(((first_buf, first_hbm), (second_buf, second_hbm))):
                out.append(
                    pltpu.make_async_copy(
                        buf.at[of_slot, pl.ds(offsets[k], STEP_ROWS[k])],
                        hbm.at[pl.ds(base + of_step * STEP_ROWS[k], STEP_ROWS[k])],
                        sems.at[of_slot, 2 * k + j],
                    )
                )
        return out

    @pl.when(step >= 2)
    def _():
        for move in moves(step - 2, slot):
            move.wait()

    def update(k, rows, lanes, flat, gradient):
        first = BETA_ONE * firsts[k][flat, :] + (1.0 - BETA_ONE) * gradient
        second = BETA_TWO * seconds[k][flat, :] + (1.0 - BETA_TWO) * gradient * gradient
        ratio = (
            first
            / (1.0 - BETA_ONE**STEP)
            / (jnp.sqrt(second / (1.0 - BETA_TWO**STEP)) + ADAM_EPS)
        )
        weight = masters[k][rows, lanes]
        weight = weight - rates[k] * (ratio + WEIGHT_DECAY * weight)
        new_refs[k][rows, lanes] = weight
        copy_refs[k][rows, lanes] = lowered(weight)
        return first, second

    def wide(k, gradient_of, scale):
        width = masters[k].shape[1] // 128
        for t in range(width):
            flat = pl.ds(t, 16, stride=width)
            first, second = update(
                k, slice(None), pl.ds(t * 128, 128), flat, gradient_of(t).astype(F32) * scale
            )
            store = pl.ds(offsets[k] + t, 16, stride=width)
            first_buf.at[slot][store, :] = first
            second_buf.at[slot][store, :] = second

    scale_one = jnp.broadcast_to(gain_one_ref[...] * factor, (16, 128))
    scale_two = jnp.broadcast_to(gain_two_ref[...] * factor, (16, 128))
    wide(0, lambda t: query_ref[t // 4, :, pl.ds(t % 4 * 128, 128)], scale_one)
    wide(1, lambda t: pair_ref[t // 2, :, pl.ds(t % 2 * 128, 128)], scale_one)
    wide(2, lambda t: pair_ref[t // 2, :, pl.ds(t % 2 * 128 + HD, 128)], scale_one)
    wide(4, lambda t: feed_ref[t // 2, :, pl.ds(t % 2 * 128, 128)], scale_two)
    wide(5, lambda t: feed_ref[t // 2, :, pl.ds(t % 2 * 128 + 256, 128)], scale_two)

    def tall(k, at, gradient):
        rows = pl.ds(at, 128)
        first, second = update(k, rows, slice(None), rows, gradient.astype(F32).T * factor)
        store = pl.ds(offsets[k] + at, 128)
        first_buf.at[slot][store, :] = first
        second_buf.at[slot][store, :] = second

    part = lax.rem(step // 2, 2) == 0
    tall(3, 0, jnp.where(part, out_zero_ref[0].astype(F32), out_one_ref[0].astype(F32)))
    for c in range(2):
        for t in range(2):
            tall(6, c * 256 + t * 128, down_ref[c, :, pl.ds(t * 128, 128)])

    for move in moves(step, slot):
        move.start()

    @pl.when(step == STEPS - 1)
    def _():
        for move in moves(step - 1, 1 - slot):
            move.wait()
        for move in moves(step, slot):
            move.wait()


def adamw_blocks(rates, factor, gain_one, gain_two, masters, moments, part_zero, part_one, came):
    shapes = [weight.shape for weight in masters]
    tables = [moment.reshape(-1, 128) for moment in moments]
    weight_specs = [
        pl.BlockSpec((shape[0] // STEPS, shape[1]), lambda i: (i, 0)) for shape in shapes
    ]
    starts = [sum(STEP_ROWS[:k]) * STEPS // STEP_ROWS[k] for k in range(7)]
    moment_specs = [
        pl.BlockSpec((STEP_ROWS[k], 128), lambda i, start=starts[k]: (start + i, 0))
        for k in range(7)
    ]
    gain_spec = pl.BlockSpec((16, 1), lambda i: (i, 0))
    rows_spec = pl.BlockSpec((2, 16, 2 * HD), lambda i: (0, i, 0))
    out_spec = pl.BlockSpec((1, 128, 128), lambda i: (i // 4, 0, 4 + i % 2))
    grad_specs = [
        rows_spec,
        rows_spec,
        out_spec,
        out_spec,
        pl.BlockSpec((16, 16, 512), lambda i: (0, i, 0)),
        pl.BlockSpec((2, 128, 256), lambda i: (i, 0, 2)),
    ]
    anywhere = pl.BlockSpec(memory_space=pl.ANY)
    outs = pl.pallas_call(
        lambda *refs: adamw_kernel(rates, *refs),
        grid=(STEPS,),
        in_specs=[
            pl.BlockSpec(memory_space=pltpu.SMEM),
            gain_spec,
            gain_spec,
            *weight_specs,
            *moment_specs,
            *moment_specs,
            *grad_specs,
        ],
        out_specs=[*weight_specs, *weight_specs, anywhere, anywhere],
        out_shape=[
            *[jax.ShapeDtypeStruct(shape, F32) for shape in shapes],
            *[jax.ShapeDtypeStruct(shape, BF) for shape in shapes],
            *[jax.ShapeDtypeStruct(table.shape, F32) for table in tables],
        ],
        scratch_shapes=[
            pltpu.VMEM((2, sum(STEP_ROWS), 128), F32),
            pltpu.VMEM((2, sum(STEP_ROWS), 128), F32),
            pltpu.SemaphoreType.DMA((2, 14)),
        ],
        compiler_params=pltpu.CompilerParams(
            dimension_semantics=("arbitrary",), vmem_limit_bytes=60 * 1024 * 1024
        ),
        name="adamw",
    )(
        factor.reshape(1, 1),
        gain_one,
        gain_two,
        *masters,
        *[tables[0]] * 7,
        *[tables[1]] * 7,
        part_zero,
        part_one,
        part_zero,
        part_one,
        came,
        came,
    )
    return outs[:7], outs[7:14], outs[14].reshape(-1), outs[15].reshape(-1)


def local(
    tokens,
    block_offsets,
    cotangent,
    w_query,
    w_key,
    w_value,
    w_out,
    w_gate,
    w_up,
    w_down,
    gains,
    moment_one,
    moment_two,
    gain_moment_one,
    gain_moment_two,
):
    lanes = Lanes()
    n_p, h = lanes.n_p, lanes.h
    n_ctx = 4 * n_p
    total_rows = n_ctx * 2 * SUB
    rows = D // n_ctx
    units = FF // (2 * n_ctx)
    chunk = 4 * SUB
    scaling = 1.0 / math.sqrt(HD)
    first_core = h == 0
    gain_low = lowered(gains).astype(F32)
    gain_one, gain_two = gain_low[0][:, None], gain_low[1][:, None]
    in_order = block_offsets[0] >= 0
    fits = rows == 128 and n_p == 4
    own = jnp.stack([lanes.z, lanes.p]).astype(jnp.int32)

    def stage(body):
        shapes = jax.eval_shape(body)
        return lax.cond(
            in_order, body, lambda: jax.tree.map(lambda a: jnp.zeros(a.shape, a.dtype), shapes)
        )

    def both_cores(own):
        other = lanes.swap(own)
        return jnp.where(
            first_core, jnp.concatenate([own, other]), jnp.concatenate([other, own])
        )

    def norm_back(inputs, inverse, incoming):
        inner = jnp.mean(incoming * inputs, axis=-1, keepdims=True)
        return inverse * incoming - inputs * (inverse * inverse * inverse * inner)

    x_own = lax.dynamic_slice_in_dim(tokens, h * SUB, SUB)
    dy_own = lax.dynamic_slice_in_dim(cotangent, h * SUB, SUB)

    query_part = lowered((w_query * gain_one).reshape(rows, 2, QW))
    key_part = lowered((w_key * gain_one).reshape(rows, 2, HD))
    value_part = lowered((w_value * gain_one).reshape(rows, 2, HD))
    out_part = lowered(w_out).T.reshape(rows, 2, QW)
    quarter = QW // 4
    out_parts = [out_part[:, :, k * quarter : (k + 1) * quarter] for k in range(4)]
    blocks = lanes.group_blocks(
        jnp.concatenate(
            [query_part[:, :, :HD], out_parts[0], query_part[:, :, HD:], out_parts[1]], axis=-1
        ),
        jnp.concatenate([key_part, out_parts[2], value_part, out_parts[3]], axis=-1),
    )
    split = rows * 3 * QW // 2 // SUB
    mine = []
    for step in range(4):
        block = pick(blocks, lanes.z ^ step, 0).reshape(2, rows // 2, 3 * QW // 2)
        if rows == 2 * SUB:
            block = jnp.concatenate([block[0], block[1]], axis=-1)
        else:
            block = block.reshape(SUB, split)
        mine.append(jnp.concatenate([block, x_own], axis=-1))
    mine = [mine[0]] + [lanes.over_z(mine[step], step) for step in (1, 2, 3)]
    if fits:
        feed = pack_feed(own, after(gain_two, blocks), w_gate, w_up, w_down, n_p)
    else:
        feed = w_gate * gain_two, w_up * gain_two, w_down.T
        feed = [lowered(matrix).reshape(rows, 4, n_p, units) for matrix in feed]
        feed = jnp.concatenate(feed, axis=-1).transpose(1, 2, 0, 3)
        feed = split_rows(own, feed, 0)
    mine = after(mine, feed[0])
    x_pieces = [piece[:, split:] for piece in mine]
    if rows == 2 * SUB:
        middle = split // 2
        mine = [jnp.concatenate([one[:, :middle], one[:, middle:split]]) for one in mine]
    else:
        mine = [one[:, :split].reshape(rows, 3 * QW // 2) for one in mine]
    mine = lanes.join_z(mine)
    dy_line = lax.all_gather(after(dy_own, mine), "z", axis=0, tiled=True)
    feed = after(list(feed), mine)
    feed = [feed[0]] + [lanes.over_z(feed[step], step) for step in (1, 2, 3)]

    x_chunk = jnp.concatenate(x_pieces).astype(F32)
    inverse_chunk = lax.rsqrt(jnp.mean(x_chunk * x_chunk, axis=-1, keepdims=True) + NORM_EPS)
    normed = lowered(x_chunk * inverse_chunk)

    def in_parts(four):
        here, there = four[:2], four[2:]
        zero = [jnp.where(first_core, a, b) for a, b in zip(here, there)]
        return zero + [jnp.where(first_core, b, a) for a, b in zip(here, there)]

    def quarters_of(pair, which):
        width = HD + quarter
        lanes_of = [(k * width, k * width + HD) if which == 0 else (k * width + HD, (k + 1) * width) for k in (0, 1)]
        return [one[:, low:high] for one in pair for low, high in lanes_of]

    def filled(four, which):
        pads = ((0, 0), (0, quarter)) if which == 0 else ((0, 0), (HD, 0))
        wide = [jnp.pad(one, pads) for one in four]
        return [jnp.concatenate(wide[:2], axis=-1), jnp.concatenate(wide[2:], axis=-1)]

    def project():
        cubes = [
            lanes.gather_cube(half, order) for half, order in zip(lanes.halves(mine), lanes.orders())
        ]
        here = placed(own, cubes, False).reshape(D, 2 * (HD + quarter))
        weights = [here, lanes.swap(here)]
        line = lanes.z ^ jnp.arange(4, dtype=jnp.int32)
        ring = lanes.p ^ jnp.arange(n_p, dtype=jnp.int32)
        cores = h ^ jnp.arange(2, dtype=jnp.int32)
        within = jnp.arange(SUB, dtype=jnp.int32)
        key_blocks = 2 * (line[None, None, :] * n_p + ring[None, :, None]) + cores[:, None, None]
        key_positions = (block_offsets[key_blocks.reshape(-1)][:, None] + within).reshape(-1)
        cosine, sine = rotary_tables(key_positions[:chunk])
        projected = in_parts(quarters_of([product(normed, weight) for weight in weights], 0))
        query_heads = lowered(
            jnp.concatenate([rotate(one, cosine, sine) for one in projected[:SHARE]])
        )
        key_here = lowered(rotate(projected[2], cosine, sine))
        pair_here = jnp.concatenate([key_here, lowered(projected[3])], axis=-1)
        plane = lanes.gather_p(pair_here, lanes.orders()[0], True).reshape(n_p * chunk, 2 * HD)
        pair_all = jnp.concatenate([plane, lanes.swap(plane)])
        return weights, cosine, sine, key_positions, query_heads, pair_all

    weights, cosine, sine, key_positions, query_heads, pair_all = stage(project)
    feed = turned(own, after(feed, pair_all), 0)
    dy_all = lax.all_gather(after(dy_line, feed[0]), "p", axis=0, tiled=True)
    query_heads = after(query_heads, *feed)
    feed = [feed[0]] + [lanes.over_p(feed[e], e) for e in range(1, n_p)]

    def attention_forward():
        keys_all, values_all = pair_all[:, :HD], pair_all[:, HD:]
        my_positions = key_positions[:chunk]
        allowed = key_positions[None, :] <= my_positions[:, None]
        allowed = jnp.concatenate([allowed] * SHARE)
        scores = contract(query_heads, keys_all, 1, 1) * scaling
        scores = jnp.where(allowed, scores, MASKED_SCORE)
        largest = jnp.max(scores, axis=-1, keepdims=True)
        expos = jnp.exp(scores - largest)
        probs = expos / jnp.sum(expos, axis=-1, keepdims=True)
        attended = lowered(product(lowered(probs), values_all))
        mixed = jnp.concatenate([attended[:chunk], attended[chunk:]], axis=-1)
        quarters = in_parts([mixed[:, k * quarter : (k + 1) * quarter] for k in range(4)])
        resid_part = sum(
            contract(part, weight, 1, 1) for part, weight in zip(filled(quarters, 1), weights)
        )
        return probs, mixed, lowered(resid_part).reshape(4, SUB, D)

    probs, mixed, resid_part = stage(attention_forward)
    def second_norm():
        resid = x_own.astype(F32) + lanes.scatter_z(resid_part, True)
        inverse_two = lax.rsqrt(jnp.mean(resid * resid, axis=-1, keepdims=True) + NORM_EPS)
        normed_two = lowered(resid * inverse_two)
        return resid, inverse_two, lanes.absolute(lanes.gather_z(normed_two), lanes.z)

    resid, inverse_two, stacked = stage(second_norm)
    feed = after(feed, stacked)
    if fits:
        here = feed_weights(own, feed)
    else:
        here = joined(own, feed, 1).reshape(D, 3 * units)
        here = [here[:, : 2 * units], here[:, 2 * units :]]

    def gather_normed():
        there = [lanes.swap(weight) for weight in here]
        cubes = [
            lanes.gather_cube(half, order)
            for half, order in zip(lanes.halves(stacked), lanes.orders())
        ]
        normed_all = placed(own, cubes, True).reshape(n_ctx * SUB, D)
        d_hidden = [product(dy_all, weight) for weight in (here[1], there[1])]
        return normed_all, there, d_hidden

    normed_all, there, d_hidden = stage(gather_normed)
    gate_up_weights, down_weights = zip(here, there)

    def feed_forward():
        d_gate_up, hidden = [], []
        for gate_up_weight, incoming in zip(gate_up_weights, d_hidden):
            gate_up = product(normed_all, gate_up_weight)
            gate_values, up_values = gate_up[:, :units], gate_up[:, units:]
            sigmoid_gate = jax.nn.sigmoid(gate_values)
            activated = gate_values * sigmoid_gate
            hidden.append(lowered(activated * up_values))
            slope = sigmoid_gate * (1.0 + gate_values * (1.0 - sigmoid_gate))
            d_gate = lowered(incoming * up_values * slope)
            d_gate_up.append(jnp.concatenate([d_gate, lowered(incoming * activated)], axis=-1))
        cubes = []
        for part in (slice(0, D // 2), slice(D // 2, D)):
            partial = sum(
                contract(one, weight[part], 1, 1)
                for one, weight in zip(d_gate_up, gate_up_weights)
            )
            cubes.append(partial.reshape(lanes.cube + [4, SUB, D // 2]))
        d_normed_parts = [
            lanes.scatter_p(cube, order, False) for cube, order in zip(cubes, lanes.orders())
        ]
        d_gate_up[1] = after(d_gate_up[1], *cubes)
        hidden = after(hidden, *cubes)
        away = jnp.concatenate(
            [
                lowered(contract(normed_all, d_gate_up[1], 0, 0)),
                lowered(contract(dy_all, hidden[1], 0, 0)),
            ],
            axis=-1,
        )
        came = lanes.swap(away)
        home_gate_up = contract(normed_all, after(d_gate_up[0], away), 0, 0)
        home_down = contract(dy_all, hidden[0], 0, 0)
        if fits:
            came = add_split(own, n_p, home_gate_up, home_down, came)
        else:
            home = jnp.concatenate([home_gate_up, home_down], axis=-1)
            came = lowered(home + came.astype(F32)).reshape(4, n_p, rows, 3 * units)
            came = split_rows(own, came, 1)
        out_part = lowered(
            sum(contract(one, weight, 1, 1) for one, weight in zip(hidden, down_weights))
        )
        return jnp.concatenate(d_normed_parts, axis=-1), list(came), out_part

    d_normed_part, came, out_part = stage(feed_forward)
    came = [came[0]] + [lanes.over_p(came[e], e) for e in range(1, n_p)]
    out_line = lax.psum_scatter(out_part, "p", scatter_dimension=0, tiled=True)

    def second_norm_backward():
        d_normed_two = lanes.scatter_z(d_normed_part, False)
        d_resid = dy_own.astype(F32) + norm_back(resid, inverse_two, d_normed_two)
        return d_resid, jnp.concatenate(lanes.gather_z(lowered(d_resid)))

    d_resid, d_resid_chunk = stage(second_norm_backward)
    came = turned(own, after(came, d_resid_chunk), 1)
    d_resid_chunk = after(d_resid_chunk, *came)
    came = [came[0]] + [lanes.over_z(came[step], step) for step in (1, 2, 3)]

    def attention_backward():
        d_mixed = [product(d_resid_chunk, weight) for weight in weights]
        d_mixed = in_parts(quarters_of(d_mixed, 1))
        d_mixed = lowered(jnp.concatenate(d_mixed, axis=-1))
        d_attended = jnp.concatenate([d_mixed[:, :HD], d_mixed[:, HD:]])
        keys_all, values_all = pair_all[:, :HD], pair_all[:, HD:]
        d_probs = contract(d_attended, values_all, 1, 1)
        delta = jnp.sum(probs * d_probs, axis=-1, keepdims=True)
        d_scores = lowered(probs * (d_probs - delta))
        d_query_heads = product(d_scores, keys_all) * scaling
        d_key_all = contract(d_scores, query_heads, 0, 0) * scaling
        d_value_all = contract(lowered(probs), d_attended, 0, 0)
        middle = n_p * chunk
        halves = []
        for whole in (d_key_all, d_value_all):
            halves.append(whole[:middle] + lanes.swap(lowered(whole[middle:])).astype(F32))
        return d_query_heads, halves

    d_query_heads, d_pair_halves = stage(attention_backward)

    def attention_gradients():
        d_key, d_value = [
            lanes.scatter_p(half.reshape(lanes.cube + [chunk, HD]), order, True)
            for half, order in zip(d_pair_halves, lanes.orders())
        ]
        d_key = lowered(rotate(d_key, cosine, -sine))
        d_value = lowered(d_value)
        d_query = [
            lowered(rotate(one, cosine, -sine))
            for one in (d_query_heads[:chunk], d_query_heads[chunk:])
        ]
        lefts = (normed, d_resid_chunk)
        rights = [d_query[0], mixed[:, :quarter], d_query[1], mixed[:, quarter : 2 * quarter]]
        others = [d_key, mixed[:, 2 * quarter : 3 * quarter], d_value, mixed[:, 3 * quarter :]]
        keep, away = [], []
        for k in range(4):
            mine, theirs = jnp.where(first_core, rights[k], others[k]), jnp.where(
                first_core, others[k], rights[k]
            )
            keep.append(contract(lefts[k % 2], mine, 0, 0))
            away.append(lowered(contract(lefts[k % 2], theirs, 0, 0)))
        summed = []
        for at, order in zip((0, 2), lanes.orders()):
            half = jnp.concatenate(keep[at : at + 2], axis=-1)
            half = half + lanes.swap(jnp.concatenate(away[at : at + 2], axis=-1)).astype(F32)
            cube = lowered(half).reshape(4, n_p, rows, half.shape[-1])
            have = list(range(lanes.bits))
            for b in order:
                keep_cube, send = halved(own, cube, have.index(b), b)
                cube = keep_cube.astype(F32) + lanes.over_p(send, 1 << b).astype(F32)
                cube = lowered(cube)
                have.remove(b)
            summed.append(cube.reshape(4, rows, half.shape[-1]))
        in_turn = [half[..., :HD] for half in summed] + [half[..., HD:] for half in summed]
        part_zero, part_one = lanes.group_home(jnp.concatenate(in_turn, axis=-1))

        quarters = after(in_parts(d_query + [d_key, d_value]), summed[1])
        d_normed_part = sum(
            contract(part, weight, 1, 1) for part, weight in zip(filled(quarters, 0), weights)
        )
        return part_zero, part_one, d_normed_part.reshape(4, SUB, D)

    part_zero, part_one, d_normed_part = stage(attention_gradients)

    parts = [
        jnp.concatenate(
            [d_normed_part[s], pick(out_line.reshape(4, SUB, D), lanes.z ^ s, 0).astype(F32)]
        )
        for s in range(4)
    ]
    near = lanes.over_z(lowered(jnp.stack([parts[3], parts[1]])), 1)
    part_zero = after(part_zero, parts[3])
    came = joined(own, after(came, part_zero), 0).reshape(n_ctx, rows, 3 * units)
    masters = (w_query, w_key, w_value, w_out, w_gate, w_up, w_down)
    if fits:
        shared = squares_of(gain_one, gain_two, masters, part_zero, part_one, came)
    else:

        def of_owner(k):
            part = came[:, :, k * units : (k + 1) * units].transpose(1, 0, 2)
            return part.reshape(rows, n_ctx * units).astype(F32)

        inner_gate, inner_up, grad_down = of_owner(0), of_owner(1), of_owner(2).T
        grad_out = jnp.concatenate([part_zero[:, :, QW:], part_one[:, :, QW:]], axis=-1)
        grad_out = grad_out.astype(F32).transpose(0, 2, 1).reshape(2 * QW, rows)
        inner_query = part_zero[:, :, :QW].astype(F32).transpose(1, 0, 2).reshape(rows, 2 * QW)
        inner_pair = part_one[:, :, :QW].astype(F32).transpose(1, 0, 2)
        inner_key = inner_pair[:, :, :HD].reshape(rows, 2 * HD)
        inner_value = inner_pair[:, :, HD:].reshape(rows, 2 * HD)

        def weighed(matrix, inner):
            return jnp.sum(lowered(matrix).astype(F32) * inner, axis=1)

        first = weighed(w_query, inner_query) + weighed(w_key, inner_key)
        grad_gains = jnp.stack(
            [
                first + weighed(w_value, inner_value),
                weighed(w_gate, inner_gate) + weighed(w_up, inner_up),
            ]
        )
        gradients = (
            inner_query * gain_one,
            inner_key * gain_one,
            inner_value * gain_one,
            grad_out,
            inner_gate * gain_two,
            inner_up * gain_two,
            grad_down,
        )
        squares = sum(jnp.sum(gradient * gradient) for gradient in gradients)
        shared = jnp.concatenate([grad_gains, jnp.broadcast_to(squares, (6, rows))])
    shared = shared + lanes.swap(shared)
    grad_gains = shared[:2]
    squares = jnp.broadcast_to(shared[2:3, :1] + jnp.sum(grad_gains * grad_gains), (8, 128))
    for b in range(lanes.bits):
        squares = squares + lanes.over_p(squares, 1 << b)
    for s in (1, 2):
        squares = squares + lanes.over_z(squares, s)
    near = after(near, squares).astype(F32)
    far = lanes.over_z(lowered(parts[2] + near[0]), 2)
    grad_norm = jnp.sqrt(squares[0, 0])
    factor = CLIP_NORM / jnp.maximum(grad_norm, CLIP_NORM)
    wo_fan = min(HQ * HD, max(2, 131072 // total_rows))
    rate_in = 2.0 / math.sqrt(D)
    step_rates = (
        rate_in,
        rate_in,
        rate_in,
        2.0 / math.sqrt(wo_fan),
        rate_in,
        rate_in,
        2.0 / math.sqrt(FF),
    )
    if fits:
        new_weights, copies, moment_first, moment_second = adamw_blocks(
            step_rates,
            factor,
            gain_one,
            gain_two,
            masters,
            (moment_one, moment_two),
            part_zero,
            part_one,
            came,
        )
    else:
        new_weights = []
        firsts = []
        seconds = []
        offset = 0
        for index_now in range(7):
            weight = masters[index_now]
            length = weight.size
            first_moment = moment_one[offset : offset + length].reshape(weight.shape)
            second_moment = moment_two[offset : offset + length].reshape(weight.shape)
            updated, first_new, second_new = adamw_step(
                weight,
                factor * gradients[index_now],
                first_moment,
                second_moment,
                step_rates[index_now],
                WEIGHT_DECAY,
            )
            new_weights.append(updated)
            firsts.append(first_new.reshape(-1))
            seconds.append(second_new.reshape(-1))
            offset = offset + length
        copies = [lowered(weight) for weight in new_weights]
        moment_first, moment_second = jnp.concatenate(firsts), jnp.concatenate(seconds)
    line_sums = parts[0] + near[1] + after(far, new_weights[0]).astype(F32)
    d_normed, out_sum = line_sums[:SUB], line_sums[SUB:]
    x_float = x_own.astype(F32)
    inverse_own = lax.rsqrt(jnp.mean(x_float * x_float, axis=-1, keepdims=True) + NORM_EPS)
    input_grad = lowered(d_resid + norm_back(x_float, inverse_own, d_normed))
    input_grad, layer_out = both_cores(input_grad), both_cores(lowered(resid + out_sum))
    new_gains, gain_first, gain_second = adamw_step(
        gains, factor * grad_gains, gain_moment_one, gain_moment_two, GAIN_RATE, 0.0
    )
    return (
        layer_out,
        input_grad,
        grad_norm,
        *new_weights,
        new_gains,
        *copies,
        lowered(new_gains),
        moment_first,
        moment_second,
        gain_first,
        gain_second,
    )


def solution(mesh):
    n_ctx, n_head = mesh.devices.shape
    lanes_mesh = Mesh(mesh.devices.reshape(4, n_ctx // 4, n_head), ("z", "p", "head"))
    ctx = ("z", "p")
    rows = P(ctx, None)
    wide = P(ctx, "head")
    tall = P("head", ctx)
    flat = P(("z", "p", "head"))
    gain = P(None, ctx)
    weights = (wide, wide, wide, tall, wide, wide, tall, gain)
    return jax.shard_map(
        local,
        mesh=lanes_mesh,
        in_specs=(rows, P(), rows, *weights, flat, flat, gain, gain),
        out_specs=(rows, rows, P(), *weights, *weights, flat, flat, gain, gain),
        check_vma=False,
    )
```

```python
import math

import jax
import jax.numpy as jnp
from jax import lax
from jax.experimental import pallas as pl
from jax.experimental.pallas import tpu as pltpu
from jax.sharding import Mesh
from jax.sharding import PartitionSpec as P

D = 2048
HQ = 8
KV = 4
HD = 256
FF = 8192
SUB = 64
STEP = 10
SHARE = HQ // KV
QW = SHARE * HD


NORM_EPS = 1e-06
ROPE_BASE = 1000042.0
BETA_ONE = 0.9
BETA_TWO = 0.95
ADAM_EPS = 1e-08
WEIGHT_DECAY = 0.1
GAIN_RATE = 0.5
CLIP_NORM = 1.0
MASKED_SCORE = -1e30
BF = jnp.bfloat16
F32 = jnp.float32
SWAP = [(0, 1), (1, 0)]


def lowered(array_in):
    return array_in.astype(BF)


def product(left, right):
    return jnp.dot(left, right, preferred_element_type=F32)


def contract(left, right, left_dim, right_dim):
    return lax.dot_general(
        left, right, (((left_dim,), (right_dim,)), ((), ())), preferred_element_type=F32
    )


def rotary_tables(positions):
    frequency = ROPE_BASE ** (-jnp.arange(0, HD, 2, dtype=F32) / HD)
    angles = positions.astype(F32)[:, None] * frequency[None, :]
    return (jnp.cos(angles), jnp.sin(angles))


def rotate(one_head, cosine, sine):
    half_size = HD // 2
    first_half = one_head[:, :half_size]
    second_half = one_head[:, half_size:]
    return jnp.concatenate(
        [first_half * cosine - second_half * sine, second_half * cosine + first_half * sine],
        axis=-1,
    )


def adamw_step(weight, gradient, first_moment, second_moment, step_rate, decay_rate):
    first_new = BETA_ONE * first_moment + (1.0 - BETA_ONE) * gradient
    second_new = BETA_TWO * second_moment + (1.0 - BETA_TWO) * gradient * gradient
    ratio = (
        first_new
        / (1.0 - BETA_ONE**STEP)
        / (jnp.sqrt(second_new / (1.0 - BETA_TWO**STEP)) + ADAM_EPS)
    )
    return (weight - step_rate * (ratio + decay_rate * weight), first_new, second_new)


def pick(array_in, index, axis):
    return lax.dynamic_index_in_dim(array_in, index, axis, keepdims=False)


def after(arrays, *others):
    listed = arrays if isinstance(arrays, list) else [arrays]
    if not others:
        return arrays
    anywhere = pl.BlockSpec(memory_space=pl.ANY)
    out = pl.pallas_call(
        lambda *refs: None,
        in_specs=[anywhere] * (len(listed) + len(others)),
        out_specs=[anywhere] * len(listed),
        out_shape=[jax.ShapeDtypeStruct(array.shape, array.dtype) for array in listed],
        input_output_aliases={k: k for k in range(len(listed))},
        name="after",
    )(*listed, *others)
    return list(out) if isinstance(arrays, list) else out[0]


class Lanes:
    def __init__(self):
        self.n_p = lax.axis_size("p")
        self.z = lax.axis_index("z")
        self.p = lax.axis_index("p")
        self.h = lax.axis_index("head")
        self.bits = self.n_p.bit_length() - 1
        self.cube = [2] * self.bits

    def swap(self, array_in):
        return lax.ppermute(array_in, "head", SWAP)

    def over_z(self, array_in, step):
        return lax.ppermute(array_in, "z", [(i, i ^ step) for i in range(4)])

    def over_p(self, array_in, step):
        return lax.ppermute(array_in, "p", [(i, i ^ step) for i in range(self.n_p)])

    def orders(self):
        return list(range(self.bits)), list(range(self.bits))[::-1]

    def bit(self, b):
        return (self.p >> b) & 1

    def absolute(self, pieces, index, axis=0):
        for b in range(len(pieces).bit_length() - 1):
            odd = ((index >> b) & 1) == 1
            pieces = [jnp.where(odd, pieces[j ^ (1 << b)], pieces[j]) for j in range(len(pieces))]
        return jnp.stack(pieces, axis)

    def gather_z(self, array_in):
        one, two = self.over_z(array_in, 1), self.over_z(array_in, 2)
        return [array_in, one, two, self.over_z(two, 1)]

    def send_z(self, array_in, axis=0):
        pieces = [pick(array_in, self.z, axis)]
        for s in (1, 2, 3):
            pieces.append(self.over_z(pick(array_in, self.z ^ s, axis), s))
        return pieces

    def join_z(self, pieces, axis=0):
        return self.absolute(pieces, self.z, axis)

    def scatter_z(self, array_in, relative):
        parts = [pick(array_in, s if relative else self.z ^ s, 0).astype(F32) for s in range(4)]
        near = self.over_z(lowered(jnp.stack([parts[3], parts[1]])), 1).astype(F32)
        far = self.over_z(lowered(parts[2] + near[0]), 2).astype(F32)
        return parts[0] + near[1] + far

    def gather_p(self, array_in, order, relative, lead=0):
        have = []
        for b in order:
            other = self.over_p(array_in, 1 << b)
            axis = lead + sum(1 for x in have if x > b)
            mine, other = jnp.expand_dims(array_in, axis), jnp.expand_dims(other, axis)
            array_in = jnp.concatenate([mine, other], axis)
            if not relative:
                array_in = jnp.where(
                    self.bit(b) == 1, jnp.concatenate([other, mine], axis), array_in
                )
            have.append(b)
        return array_in

    def gather_cube(self, array_in, order):
        held = [(array_in[None], [0])]
        for b in order:
            numbers = [j for _, part in held for j in part]
            whole = jnp.concatenate([array for array, _ in held]) if len(held) > 1 else held[0][0]
            held.append((self.over_p(whole, 1 << b), [j ^ (1 << b) for j in numbers]))
        return held

    def scatter_p(self, array_in, order, relative, lead=0):
        have = list(range(self.bits))
        for b in order:
            axis = lead + sum(1 for x in have if x > b)
            bit = 0 if relative else self.bit(b)
            keep, send = pick(array_in, bit, axis), pick(array_in, 1 - bit, axis)
            array_in = keep.astype(F32) + self.over_p(lowered(send), 1 << b).astype(F32)
            have.remove(b)
        return array_in

    def halves(self, array_in):
        middle = array_in.shape[-1] // 2
        return array_in[..., :middle], array_in[..., middle:]

    def group_blocks(self, part_zero, part_one):
        first = self.h == 0
        keep = jnp.where(first, part_zero, part_one).transpose(1, 0, 2)
        other = self.swap(jnp.where(first, part_one, part_zero).transpose(1, 0, 2))
        return jnp.where(
            first, jnp.concatenate([keep, other]), jnp.concatenate([other, keep])
        )

    def group_home(self, blocks):
        first = self.h == 0
        own = jnp.where(first, blocks[:2], blocks[2:])
        other = self.swap(jnp.where(first, blocks[2:], blocks[:2]))
        return jnp.where(first, own, other), jnp.where(first, other, own)


def moved(own, inputs, shapes, plan):
    def kernel(own_ref, *refs):
        ins, outs = refs[: len(inputs)], refs[len(inputs) :]
        for source, target in plan(ins, outs, own_ref[0], own_ref[1]):
            if isinstance(source, tuple):
                total = sum(one[...].astype(F32) for one in source)
                target[...] = total.astype(target.dtype)
            else:
                target[...] = source[...]

    vmem = pl.BlockSpec(memory_space=pltpu.VMEM)
    return pl.pallas_call(
        kernel,
        in_specs=[pl.BlockSpec(memory_space=pltpu.SMEM)] + [vmem] * len(inputs),
        out_specs=[vmem] * len(shapes),
        out_shape=[jax.ShapeDtypeStruct(shape, inputs[0].dtype) for shape in shapes],
        compiler_params=pltpu.CompilerParams(vmem_limit_bytes=60 * 1024 * 1024),
        name="moved",
    )(own, *inputs)


def split_rows(own, array_in, which):
    count = array_in.shape[which]
    shape = array_in.shape[:which] + array_in.shape[which + 1 :]

    def plan(ins, outs, z, p):
        if which == 0:
            return [(ins[0].at[z ^ j], outs[j]) for j in range(count)]
        return [(ins[0].at[:, p ^ j], outs[j]) for j in range(count)]

    return moved(own, [array_in], [shape] * count, plan)


def joined(own, pieces, which):
    count = len(pieces)
    shape = pieces[0].shape
    shape = shape[:which] + (count,) + shape[which:]

    def plan(ins, outs, z, p):
        if which == 0:
            return [(ins[j], outs[0].at[z ^ j]) for j in range(count)]
        return [(ins[j], outs[0].at[:, p ^ j]) for j in range(count)]

    return moved(own, pieces, [shape], plan)[0]


def turned(own, pieces, which):
    count = len(pieces)
    other = pieces[0].shape[0]
    shape = (count,) + pieces[0].shape[1:]

    def plan(ins, outs, z, p):
        mine, theirs = (z, p) if which == 0 else (p, z)
        return [
            (ins[i].at[theirs ^ j], outs[j].at[mine ^ i])
            for i in range(count)
            for j in range(other)
        ]

    return moved(own, pieces, [shape] * other, plan)


def placed(own, halves, in_front):
    arrays = [array for half in halves for array, _ in half]
    n_p = sum(len(numbers) for _, numbers in halves[0])
    block = halves[0][0][0].shape[1:]
    widths = [half[0][0].shape[-1] for half in halves]
    lead = (n_p, block[0]) if in_front else (block[0], n_p)
    shapes = [lead + block[1:-1] + (sum(widths),)]

    def plan(ins, outs, z, p):
        pairs, at = [], 0
        for k, half in enumerate(halves):
            lanes = pl.ds(sum(widths[:k]), widths[k])
            for _, numbers in half:
                for i, j in enumerate(numbers):
                    if in_front:
                        target = outs[0].at[p ^ j, :, :, lanes]
                    else:
                        target = outs[0].at[:, p ^ j, :, lanes]
                    pairs.append((ins[at].at[i], target))
                at = at + 1
        return pairs

    return moved(own, arrays, shapes, plan)[0]


def add_split(own, n_p, home, came):
    rows = home[0].shape[0] // (4 * n_p)

    def kernel(own_ref, gate_up_ref, down_ref, gate_up_came, down_came, *outs):
        sides = (
            (gate_up_ref, gate_up_came, pl.ds(0, 512)),
            (down_ref, down_came, pl.ds(512, 256)),
        )
        for j in range(n_p):
            for z in range(4):
                at = pl.multiple_of((z * n_p + (own_ref[1] ^ j)) * rows, rows)
                at = pl.ds(at, rows)
                for ref, came_ref, lanes in sides:
                    total = ref[at, :].astype(F32) + came_ref[at, :].astype(F32)
                    outs[j][z, :, lanes] = lowered(total)

    vmem = pl.BlockSpec(memory_space=pltpu.VMEM)
    return pl.pallas_call(
        kernel,
        in_specs=[pl.BlockSpec(memory_space=pltpu.SMEM)] + [vmem] * 4,
        out_specs=[vmem] * n_p,
        out_shape=[jax.ShapeDtypeStruct((4, rows, 768), BF)] * n_p,
        compiler_params=pltpu.CompilerParams(vmem_limit_bytes=60 * 1024 * 1024),
        name="add_split",
    )(own, *home, *came)


def half_numbers(count, at, bit):
    return [((k >> at) << (at + 1)) | (k & ((1 << at) - 1)) | (bit << at) for k in range(count // 2)]


def add_halved(own, lead, n_p, keeps, cames, orders):
    rows = cames[0].shape[0] // (lead * n_p)
    counts = [len(keep) for keep in keeps]
    shape = (lead, n_p // 2, rows, cames[0].shape[1])

    def kernel(own_ref, *refs):
        outs = refs[-4:]
        at = 0
        for half, order in enumerate(orders):
            parts, came = refs[at : at + counts[half]], refs[at + counts[half]]
            at = at + counts[half] + 1
            bit = (own_ref[1] >> order[0]) & 1
            for target, value in ((outs[2 * half], bit), (outs[2 * half + 1], 1 - bit)):
                for k, number in enumerate(half_numbers(n_p, order[0], value)):
                    for z in range(lead):
                        from_rows = pl.ds(pl.multiple_of((z * n_p + number) * rows, rows), rows)
                        low = 0
                        for part in parts:
                            lanes = pl.ds(low, part.shape[1])
                            low = low + part.shape[1]
                            total = part[from_rows, :].astype(F32)
                            total = total + came[from_rows, lanes].astype(F32)
                            target[z, k, :, lanes] = lowered(total)

    vmem = pl.BlockSpec(memory_space=pltpu.VMEM)
    inputs = [one for keep, came in zip(keeps, cames) for one in [*keep, came]]
    outs = pl.pallas_call(
        kernel,
        in_specs=[pl.BlockSpec(memory_space=pltpu.SMEM)] + [vmem] * len(inputs),
        out_specs=[vmem] * 4,
        out_shape=[jax.ShapeDtypeStruct(shape, BF)] * 4,
        compiler_params=pltpu.CompilerParams(vmem_limit_bytes=60 * 1024 * 1024),
        name="add_halved",
    )(own, *inputs)
    return outs[:2], outs[2:]


def sum_halved(own, stay, came, at, b):
    count = stay.shape[1]
    shape = (stay.shape[0], count // 2) + stay.shape[2:]

    def plan(ins, outs, z, p):
        bit = (p >> b) & 1
        pairs = []
        for target, value in ((outs[0], bit), (outs[1], 1 - bit)):
            for k, number in enumerate(half_numbers(count, at, value)):
                pairs.append(((ins[0].at[:, number], ins[1].at[:, number]), target.at[:, k]))
        return pairs

    return moved(own, [stay, came], [shape] * 2, plan)


def feed_weights(own, pieces):
    count = len(pieces)

    def plan(ins, outs, z, p):
        pairs = []
        for j in range(count):
            pairs.append((ins[j].at[:, :, pl.ds(0, 512)], outs[0].at[:, p ^ j]))
            pairs.append((ins[j].at[:, :, pl.ds(512, 256)], outs[1].at[:, p ^ j]))
        return pairs

    gate_up, down = moved(own, pieces, [(4, count, 128, 512), (4, count, 128, 256)], plan)
    return [gate_up.reshape(D, 512), down.reshape(D, 256)]


def feed_forward_kernel(
    own_ref, normed_ref, dy_ref, here_ref, there_ref, down_here_ref, down_there_ref,
    hidden_ref, d_zero_ref, d_one_ref, stay_zero_ref, goes_zero_ref, stay_one_ref, goes_one_ref,
):
    step = pl.program_id(0)
    normed = normed_ref[...]
    d_normed = None
    dy = dy_ref[...]
    sides = ((down_here_ref, here_ref, d_zero_ref), (down_there_ref, there_ref, d_one_ref))
    for core, (down_ref, weight_ref, d_ref) in enumerate(sides):
        weight = weight_ref[...]
        gate_up = product(normed, weight)
        gate_values, up_values = gate_up[:, :256], gate_up[:, 256:]
        incoming = product(dy, down_ref[...])
        sigmoid_gate = jax.nn.sigmoid(gate_values)
        activated = gate_values * sigmoid_gate
        hidden_ref[:, pl.ds(core * 256, 256)] = lowered(activated * up_values)
        slope = sigmoid_gate * (1.0 + gate_values * (1.0 - sigmoid_gate))
        d_ref[:, pl.ds(0, 256)] = lowered(incoming * up_values * slope)
        d_ref[:, pl.ds(256, 256)] = lowered(incoming * activated)
        partial = contract(d_ref[...], weight, 1, 1)
        d_normed = partial if d_normed is None else d_normed + partial
    d_normed = lowered(d_normed)
    halves = ((0, stay_zero_ref, goes_zero_ref), (1, stay_one_ref, goes_one_ref))
    for b, stay_ref, goes_ref in halves:
        stays = ((step >> b) & 1) == ((own_ref[1] >> b) & 1)
        place = (step >> 1) if b == 0 else (step & 1)
        part = d_normed[:, b * (D // 2) : (b + 1) * (D // 2)]

        @pl.when(stays)
        def _():
            stay_ref[place] = part

        @pl.when(jnp.logical_not(stays))
        def _():
            goes_ref[place] = part


def feed_forward_blocks(own, normed_all, dy_all, gate_up_weights, down_weights):
    quarter = normed_all.shape[0] // 4

    def of_rows(width):
        return pl.BlockSpec((quarter, width), lambda i: (i, 0))

    def whole(*shape):
        return pl.BlockSpec(shape, lambda i: (0,) * len(shape))

    half = (2, quarter, D // 2)
    return pl.pallas_call(
        feed_forward_kernel,
        grid=(4,),
        in_specs=[
            pl.BlockSpec(memory_space=pltpu.SMEM),
            of_rows(D),
            of_rows(D),
            whole(D, 512),
            whole(D, 512),
            whole(D, 256),
            whole(D, 256),
        ],
        out_specs=[of_rows(512), of_rows(512), of_rows(512)] + [whole(*half)] * 4,
        out_shape=[jax.ShapeDtypeStruct((4 * quarter, 512), BF)] * 3
        + [jax.ShapeDtypeStruct(half, BF)] * 4,
        compiler_params=pltpu.CompilerParams(
            dimension_semantics=("arbitrary",), vmem_limit_bytes=60 * 1024 * 1024
        ),
        name="feed_forward",
    )(own, normed_all, dy_all, *gate_up_weights, *down_weights)


def pack_kernel(n_p, own_ref, gain_ref, gate_ref, up_ref, down_ref, *outs):
    gain = jnp.broadcast_to(gain_ref[...], (128, 256))
    for s in range(4):
        for p in range(n_p):
            at = pl.multiple_of(((own_ref[0] ^ s) * n_p + p) * 256, 256)
            outs[s][p, :, pl.ds(0, 256)] = lowered(gate_ref[:, pl.ds(at, 256)] * gain)
            outs[s][p, :, pl.ds(256, 256)] = lowered(up_ref[:, pl.ds(at, 256)] * gain)
            outs[s][p, :, pl.ds(512, 256)] = lowered(down_ref[pl.ds(at, 256), :].T)


def pack_feed(own, gain, w_gate, w_up, w_down, n_p):
    vmem = pl.BlockSpec(memory_space=pltpu.VMEM)
    return pl.pallas_call(
        lambda *refs: pack_kernel(n_p, *refs),
        in_specs=[pl.BlockSpec(memory_space=pltpu.SMEM), vmem, vmem, vmem, vmem],
        out_specs=[vmem] * 4,
        out_shape=[jax.ShapeDtypeStruct((n_p, 128, 768), BF)] * 4,
        compiler_params=pltpu.CompilerParams(vmem_limit_bytes=60 * 1024 * 1024),
        name="pack_feed",
    )(own, gain, w_gate, w_up, w_down)


def squares_body(gain_ref, blocks, plain, base_ref, row, out_ref, squares_ref, along_ref):
    step = pl.program_id(0)
    height = gain_ref.shape[0]
    here = pl.ds(pl.multiple_of(step * height, height), height)

    @pl.when(step == 0)
    def _():
        squares_ref[...] = jnp.zeros_like(squares_ref)

    nothing = jnp.zeros((height, 128), F32)
    scaled, unscaled, along = nothing, nothing, nothing
    for weight, gradient in blocks:
        gradient = gradient.astype(F32)
        scaled = scaled + gradient * gradient
        along = along + lowered(weight).astype(F32) * gradient
    for gradient in plain:
        gradient = gradient.astype(F32)
        unscaled = unscaled + gradient * gradient
    gain = gain_ref[...]
    along_ref[here, :] = along
    squares_ref[...] += scaled * (gain * gain) + unscaled

    @pl.when(step == pl.num_programs(0) - 1)
    def _():
        total = jnp.sum(squares_ref[...], keepdims=True)
        if base_ref is None:
            out_ref[...] = jnp.broadcast_to(total, (8, 128))
        else:
            out_ref[...] = base_ref[...] + total
            out_ref[1:2, :] = base_ref[1:2, :]
        out_ref[row : row + 1, :] = jnp.sum(along_ref[...].T, axis=0, keepdims=True)


def lanes_of(t):
    return pl.ds(t * 128, 128)


def feed_squares_kernel(gain_ref, gate_ref, up_ref, feed_ref, *outs):
    def column(c, t):
        return feed_ref[c, :, lanes_of(t)]

    blocks = [(gate_ref[:, lanes_of(t)], column(t // 2, t % 2)) for t in range(32)]
    blocks += [(up_ref[:, lanes_of(t)], column(t // 2, t % 2 + 2)) for t in range(32)]
    plain = [column(c, t) for c in range(16) for t in (4, 5)]
    squares_body(gain_ref, blocks, plain, None, 1, *outs)


def attention_squares_kernel(
    gain_ref, query_ref, key_ref, value_ref, zero_ref, one_ref, base_ref, *outs
):
    def column(ref, l, t):
        return ref[l, :, lanes_of(t)]

    blocks = [(query_ref[:, lanes_of(t)], column(zero_ref, t // 4, t % 4)) for t in range(8)]
    blocks += [(key_ref[:, lanes_of(t)], column(one_ref, t // 2, t % 2)) for t in range(4)]
    blocks += [(value_ref[:, lanes_of(t)], column(one_ref, t // 2, t % 2 + 2)) for t in range(4)]
    plain = [column(ref, l, t) for ref in (zero_ref, one_ref) for l in (0, 1) for t in (4, 5)]
    squares_body(gain_ref, blocks, plain, base_ref, 0, *outs)


def squares_call(kernel, arrays, height, name):
    def spec(array):
        if array.ndim == 3:
            return pl.BlockSpec((array.shape[0], height, array.shape[2]), lambda i: (0, i, 0))
        if array.shape[0] == 8:
            return pl.BlockSpec((8, 128), lambda i: (0, 0))
        return pl.BlockSpec((height, array.shape[1]), lambda i: (i, 0))

    return pl.pallas_call(
        kernel,
        grid=(128 // height,),
        in_specs=[spec(array) for array in arrays],
        out_specs=pl.BlockSpec((8, 128), lambda i: (0, 0)),
        out_shape=jax.ShapeDtypeStruct((8, 128), F32),
        scratch_shapes=[pltpu.VMEM((height, 128), F32), pltpu.VMEM((128, 128), F32)],
        compiler_params=pltpu.CompilerParams(
            dimension_semantics=("arbitrary",), vmem_limit_bytes=60 * 1024 * 1024
        ),
        name=name,
    )(*arrays)


def squares_of_feed(gain_two, w_gate, w_up, came):
    return squares_call(feed_squares_kernel, [gain_two, w_gate, w_up, came], 16, "feed_squares")


def squares_of_attention(gain_one, masters, part_zero, part_one, shares):
    arrays = [gain_one, *masters[:3], part_zero, part_one, shares]
    return squares_call(attention_squares_kernel, arrays, 64, "attention_squares")


STEP_ROWS = (128, 64, 64, 128, 512, 512, 512)
STEPS = 8


def adamw_kernel(rates, factor_ref, gain_one_ref, gain_two_ref, *refs):
    masters, firsts, seconds = refs[:7], refs[7:14], refs[14:21]
    query_ref, pair_ref, out_zero_ref, out_one_ref, feed_ref, down_ref = refs[21:27]
    new_refs, copy_refs = refs[27:34], refs[34:41]
    first_hbm, second_hbm, first_buf, second_buf, sems = refs[41:]
    step = pl.program_id(0)
    slot = lax.rem(step, 2)
    factor = factor_ref[0, 0]
    offsets = [sum(STEP_ROWS[:k]) for k in range(7)]

    def moves(of_step, of_slot):
        out = []
        for k in range(7):
            base = STEPS * offsets[k]
            for j, (buf, hbm) in enumerate(((first_buf, first_hbm), (second_buf, second_hbm))):
                out.append(
                    pltpu.make_async_copy(
                        buf.at[of_slot, pl.ds(offsets[k], STEP_ROWS[k])],
                        hbm.at[pl.ds(base + of_step * STEP_ROWS[k], STEP_ROWS[k])],
                        sems.at[of_slot, 2 * k + j],
                    )
                )
        return out

    @pl.when(step >= 2)
    def _():
        for move in moves(step - 2, slot):
            move.wait()

    def update(k, rows, lanes, flat, gradient):
        first = BETA_ONE * firsts[k][flat, :] + (1.0 - BETA_ONE) * gradient
        second = BETA_TWO * seconds[k][flat, :] + (1.0 - BETA_TWO) * gradient * gradient
        ratio = first / (jnp.sqrt(second * (1.0 / (1.0 - BETA_TWO**STEP))) + ADAM_EPS)
        weight = masters[k][rows, lanes]
        weight = weight * (1.0 - rates[k] * WEIGHT_DECAY) - ratio * (
            rates[k] / (1.0 - BETA_ONE**STEP)
        )
        new_refs[k][rows, lanes] = weight
        copy_refs[k][rows, lanes] = lowered(weight)
        return first, second

    def wide(k, gradient_of, scale):
        width = masters[k].shape[1] // 128
        for t in range(width):
            flat = pl.ds(t, 16, stride=width)
            first, second = update(
                k, slice(None), pl.ds(t * 128, 128), flat, gradient_of(t).astype(F32) * scale
            )
            store = pl.ds(offsets[k] + t, 16, stride=width)
            first_buf.at[slot][store, :] = first
            second_buf.at[slot][store, :] = second

    scale_one = jnp.broadcast_to(gain_one_ref[...] * factor, (16, 128))
    scale_two = jnp.broadcast_to(gain_two_ref[...] * factor, (16, 128))
    wide(0, lambda t: query_ref[t // 4, :, pl.ds(t % 4 * 128, 128)], scale_one)
    wide(1, lambda t: pair_ref[t // 2, :, pl.ds(t % 2 * 128, 128)], scale_one)
    wide(2, lambda t: pair_ref[t // 2, :, pl.ds(t % 2 * 128 + HD, 128)], scale_one)
    wide(4, lambda t: feed_ref[t // 2, :, pl.ds(t % 2 * 128, 128)], scale_two)
    wide(5, lambda t: feed_ref[t // 2, :, pl.ds(t % 2 * 128 + 256, 128)], scale_two)

    def tall(k, at, gradient):
        rows = pl.ds(at, 128)
        first, second = update(k, rows, slice(None), rows, gradient.astype(F32).T * factor)
        store = pl.ds(offsets[k] + at, 128)
        first_buf.at[slot][store, :] = first
        second_buf.at[slot][store, :] = second

    part = lax.rem(step // 2, 2) == 0
    tall(3, 0, jnp.where(part, out_zero_ref[0].astype(F32), out_one_ref[0].astype(F32)))
    for c in range(2):
        for t in range(2):
            tall(6, c * 256 + t * 128, down_ref[c, :, pl.ds(t * 128, 128)])

    for move in moves(step, slot):
        move.start()

    @pl.when(step == STEPS - 1)
    def _():
        for move in moves(step - 1, 1 - slot):
            move.wait()
        for move in moves(step, slot):
            move.wait()


def adamw_blocks(rates, factor, gain_one, gain_two, masters, moments, part_zero, part_one, came):
    shapes = [weight.shape for weight in masters]
    tables = [moment.reshape(-1, 128) for moment in moments]
    weight_specs = [
        pl.BlockSpec((shape[0] // STEPS, shape[1]), lambda i: (i, 0)) for shape in shapes
    ]
    starts = [sum(STEP_ROWS[:k]) * STEPS // STEP_ROWS[k] for k in range(7)]
    moment_specs = [
        pl.BlockSpec((STEP_ROWS[k], 128), lambda i, start=starts[k]: (start + i, 0))
        for k in range(7)
    ]
    gain_spec = pl.BlockSpec((16, 1), lambda i: (i, 0))
    rows_spec = pl.BlockSpec((2, 16, 2 * HD), lambda i: (0, i, 0))
    out_spec = pl.BlockSpec((1, 128, 128), lambda i: (i // 4, 0, 4 + i % 2))
    grad_specs = [
        rows_spec,
        rows_spec,
        out_spec,
        out_spec,
        pl.BlockSpec((16, 16, 512), lambda i: (0, i, 0)),
        pl.BlockSpec((2, 128, 256), lambda i: (i, 0, 2)),
    ]
    anywhere = pl.BlockSpec(memory_space=pl.ANY)
    outs = pl.pallas_call(
        lambda *refs: adamw_kernel(rates, *refs),
        grid=(STEPS,),
        in_specs=[
            pl.BlockSpec(memory_space=pltpu.SMEM),
            gain_spec,
            gain_spec,
            *weight_specs,
            *moment_specs,
            *moment_specs,
            *grad_specs,
        ],
        out_specs=[*weight_specs, *weight_specs, anywhere, anywhere],
        out_shape=[
            *[jax.ShapeDtypeStruct(shape, F32) for shape in shapes],
            *[jax.ShapeDtypeStruct(shape, BF) for shape in shapes],
            *[jax.ShapeDtypeStruct(table.shape, F32) for table in tables],
        ],
        scratch_shapes=[
            pltpu.VMEM((2, sum(STEP_ROWS), 128), F32),
            pltpu.VMEM((2, sum(STEP_ROWS), 128), F32),
            pltpu.SemaphoreType.DMA((2, 14)),
        ],
        compiler_params=pltpu.CompilerParams(
            dimension_semantics=("arbitrary",), vmem_limit_bytes=60 * 1024 * 1024
        ),
        name="adamw",
    )(
        factor.reshape(1, 1),
        gain_one,
        gain_two,
        *masters,
        *[tables[0]] * 7,
        *[tables[1]] * 7,
        part_zero,
        part_one,
        part_zero,
        part_one,
        came,
        came,
    )
    return outs[:7], outs[7:14], outs[14].reshape(-1), outs[15].reshape(-1)


def local(
    tokens,
    block_offsets,
    cotangent,
    w_query,
    w_key,
    w_value,
    w_out,
    w_gate,
    w_up,
    w_down,
    gains,
    moment_one,
    moment_two,
    gain_moment_one,
    gain_moment_two,
):
    lanes = Lanes()
    n_p, h = lanes.n_p, lanes.h
    n_ctx = 4 * n_p
    total_rows = n_ctx * 2 * SUB
    rows = D // n_ctx
    units = FF // (2 * n_ctx)
    chunk = 4 * SUB
    scaling = 1.0 / math.sqrt(HD)
    first_core = h == 0
    gain_low = lowered(gains).astype(F32)
    gain_one, gain_two = gain_low[0][:, None], gain_low[1][:, None]
    in_order = block_offsets[0] >= 0
    fits = rows == 128 and n_p == 4
    own = jnp.stack([lanes.z, lanes.p]).astype(jnp.int32)

    def stage(body):
        shapes = jax.eval_shape(body)
        return lax.cond(
            in_order, body, lambda: jax.tree.map(lambda a: jnp.zeros(a.shape, a.dtype), shapes)
        )

    def both_cores(own):
        other = lanes.swap(own)
        return jnp.where(
            first_core, jnp.concatenate([own, other]), jnp.concatenate([other, own])
        )

    def norm_back(inputs, inverse, incoming):
        inner = jnp.mean(incoming * inputs, axis=-1, keepdims=True)
        return inverse * incoming - inputs * (inverse * inverse * inverse * inner)

    x_own = lax.dynamic_slice_in_dim(tokens, h * SUB, SUB)
    dy_own = lax.dynamic_slice_in_dim(cotangent, h * SUB, SUB)

    query_part = lowered((w_query * gain_one).reshape(rows, 2, QW))
    key_part = lowered((w_key * gain_one).reshape(rows, 2, HD))
    value_part = lowered((w_value * gain_one).reshape(rows, 2, HD))
    out_part = lowered(w_out).T.reshape(rows, 2, QW)
    quarter = QW // 4
    out_parts = [out_part[:, :, k * quarter : (k + 1) * quarter] for k in range(4)]
    blocks = lanes.group_blocks(
        jnp.concatenate(
            [query_part[:, :, :HD], out_parts[0], query_part[:, :, HD:], out_parts[1]], axis=-1
        ),
        jnp.concatenate([key_part, out_parts[2], value_part, out_parts[3]], axis=-1),
    )
    split = rows * 3 * QW // 2 // SUB
    mine = []
    for step in range(4):
        block = pick(blocks, lanes.z ^ step, 0).reshape(2, rows // 2, 3 * QW // 2)
        if rows == 2 * SUB:
            block = jnp.concatenate([block[0], block[1]], axis=-1)
        else:
            block = block.reshape(SUB, split)
        mine.append(jnp.concatenate([block, x_own], axis=-1))
    mine = [mine[0]] + [lanes.over_z(mine[step], step) for step in (1, 2, 3)]
    if fits:
        feed = pack_feed(own, after(gain_two, blocks), w_gate, w_up, w_down, n_p)
    else:
        feed = w_gate * gain_two, w_up * gain_two, w_down.T
        feed = [lowered(matrix).reshape(rows, 4, n_p, units) for matrix in feed]
        feed = jnp.concatenate(feed, axis=-1).transpose(1, 2, 0, 3)
        feed = split_rows(own, feed, 0)
    mine = after(mine, feed[0])
    x_pieces = [piece[:, split:] for piece in mine]
    if rows == 2 * SUB:
        middle = split // 2
        mine = [jnp.concatenate([one[:, :middle], one[:, middle:split]]) for one in mine]
    else:
        mine = [one[:, :split].reshape(rows, 3 * QW // 2) for one in mine]
    mine = lanes.join_z(mine)
    dy_line = lax.all_gather(after(dy_own, mine), "z", axis=0, tiled=True)
    feed = after(list(feed), mine)
    feed = [feed[0]] + [lanes.over_z(feed[step], step) for step in (1, 2, 3)]

    x_chunk = jnp.concatenate(x_pieces).astype(F32)
    inverse_chunk = lax.rsqrt(jnp.mean(x_chunk * x_chunk, axis=-1, keepdims=True) + NORM_EPS)
    normed = lowered(x_chunk * inverse_chunk)

    def in_parts(four):
        here, there = four[:2], four[2:]
        zero = [jnp.where(first_core, a, b) for a, b in zip(here, there)]
        return zero + [jnp.where(first_core, b, a) for a, b in zip(here, there)]

    def quarters_of(pair, which):
        width = HD + quarter
        lanes_of = [(k * width, k * width + HD) if which == 0 else (k * width + HD, (k + 1) * width) for k in (0, 1)]
        return [one[:, low:high] for one in pair for low, high in lanes_of]

    def filled(four, which):
        pads = ((0, 0), (0, quarter)) if which == 0 else ((0, 0), (HD, 0))
        wide = [jnp.pad(one, pads) for one in four]
        return [jnp.concatenate(wide[:2], axis=-1), jnp.concatenate(wide[2:], axis=-1)]

    def project():
        cubes = [
            lanes.gather_cube(half, order) for half, order in zip(lanes.halves(mine), lanes.orders())
        ]
        here = placed(own, cubes, False).reshape(D, 2 * (HD + quarter))
        weights = [here, lanes.swap(here)]
        line = lanes.z ^ jnp.arange(4, dtype=jnp.int32)
        ring = lanes.p ^ jnp.arange(n_p, dtype=jnp.int32)
        cores = h ^ jnp.arange(2, dtype=jnp.int32)
        within = jnp.arange(SUB, dtype=jnp.int32)
        key_blocks = 2 * (line[None, None, :] * n_p + ring[None, :, None]) + cores[:, None, None]
        key_positions = (block_offsets[key_blocks.reshape(-1)][:, None] + within).reshape(-1)
        cosine, sine = rotary_tables(key_positions[:chunk])
        projected = in_parts(quarters_of([product(normed, weight) for weight in weights], 0))
        query_heads = lowered(
            jnp.concatenate([rotate(one, cosine, sine) for one in projected[:SHARE]])
        )
        key_here = lowered(rotate(projected[2], cosine, sine))
        pair_here = jnp.concatenate([key_here, lowered(projected[3])], axis=-1)
        plane = lanes.gather_p(pair_here, lanes.orders()[0], True).reshape(n_p * chunk, 2 * HD)
        pair_all = jnp.concatenate([plane, lanes.swap(plane)])
        return weights, cosine, sine, key_positions, query_heads, pair_all

    weights, cosine, sine, key_positions, query_heads, pair_all = stage(project)
    feed = turned(own, after(feed, pair_all), 0)
    dy_all = lax.all_gather(after(dy_line, feed[0]), "p", axis=0, tiled=True)
    query_heads = after(query_heads, *feed)
    feed = [feed[0]] + [lanes.over_p(feed[e], e) for e in range(1, n_p)]

    def attention_forward():
        keys_all, values_all = pair_all[:, :HD], pair_all[:, HD:]
        my_positions = key_positions[:chunk]
        allowed = key_positions[None, :] <= my_positions[:, None]
        allowed = jnp.concatenate([allowed] * SHARE)
        scores = contract(query_heads, keys_all, 1, 1) * scaling
        scores = jnp.where(allowed, scores, MASKED_SCORE)
        largest = jnp.max(scores, axis=-1, keepdims=True)
        expos = jnp.exp(scores - largest)
        probs = expos / jnp.sum(expos, axis=-1, keepdims=True)
        attended = lowered(product(lowered(probs), values_all))
        mixed = jnp.concatenate([attended[:chunk], attended[chunk:]], axis=-1)
        quarters = in_parts([mixed[:, k * quarter : (k + 1) * quarter] for k in range(4)])
        resid_part = sum(
            contract(part, weight, 1, 1) for part, weight in zip(filled(quarters, 1), weights)
        )
        return probs, mixed, lowered(resid_part).reshape(4, SUB, D)

    probs, mixed, resid_part = stage(attention_forward)
    def second_norm():
        resid = x_own.astype(F32) + lanes.scatter_z(resid_part, True)
        inverse_two = lax.rsqrt(jnp.mean(resid * resid, axis=-1, keepdims=True) + NORM_EPS)
        normed_two = lowered(resid * inverse_two)
        return resid, inverse_two, lanes.absolute(lanes.gather_z(normed_two), lanes.z)

    resid, inverse_two, stacked = stage(second_norm)
    feed = after(feed, stacked)
    if fits:
        here = feed_weights(own, feed)
    else:
        here = joined(own, feed, 1).reshape(D, 3 * units)
        here = [here[:, : 2 * units], here[:, 2 * units :]]

    def gather_normed():
        there = [lanes.swap(weight) for weight in here]
        cubes = [
            lanes.gather_cube(half, order)
            for half, order in zip(lanes.halves(stacked), lanes.orders())
        ]
        normed_all = placed(own, cubes, True).reshape(n_ctx * SUB, D)
        return normed_all, there

    normed_all, there = stage(gather_normed)
    gate_up_weights, down_weights = zip(here, there)

    def feed_forward():
        d_gate_up, hidden = [], []
        for gate_up_weight, down_weight in zip(gate_up_weights, down_weights):
            incoming = product(dy_all, down_weight)
            gate_up = product(normed_all, gate_up_weight)
            gate_values, up_values = gate_up[:, :units], gate_up[:, units:]
            sigmoid_gate = jax.nn.sigmoid(gate_values)
            activated = gate_values * sigmoid_gate
            hidden.append(lowered(activated * up_values))
            slope = sigmoid_gate * (1.0 + gate_values * (1.0 - sigmoid_gate))
            d_gate = lowered(incoming * up_values * slope)
            d_gate_up.append(jnp.concatenate([d_gate, lowered(incoming * activated)], axis=-1))
        cubes = []
        for part in (slice(0, D // 2), slice(D // 2, D)):
            partial = sum(
                contract(one, weight[part], 1, 1)
                for one, weight in zip(d_gate_up, gate_up_weights)
            )
            cubes.append(partial.reshape(lanes.cube + [4, SUB, D // 2]))
        d_normed_parts = [
            lanes.scatter_p(cube, order, False) for cube, order in zip(cubes, lanes.orders())
        ]
        return hidden, d_gate_up, jnp.concatenate(d_normed_parts, axis=-1)

    if fits:
        outs = feed_forward_blocks(own, normed_all, dy_all, gate_up_weights, down_weights)
        hidden, d_gate_up = [outs[0][:, :units], outs[0][:, units:]], list(outs[1:3])
        stays, goes = [outs[3], outs[5]], [outs[4], outs[6]]
        comes = [lanes.over_p(goes[b], 1 << b) for b in (0, 1)]
    else:
        hidden, d_gate_up, d_normed_part = stage(feed_forward)
        comes = []

    def feed_gradients(core):
        return [
            lowered(contract(normed_all, d_gate_up[core], 0, 0)),
            lowered(contract(dy_all, hidden[core], 0, 0)),
        ]

    def feed_gradients_away():
        out_part = sum(contract(one, weight, 1, 1) for one, weight in zip(hidden, down_weights))
        return feed_gradients(1), lowered(out_part)

    away, out_part = stage(feed_gradients_away)
    if fits:
        comes = after(comes, out_part)
        totals = [stay.astype(F32) + one.astype(F32) for stay, one in zip(stays, comes)]
        goes = [lowered(pick(totals[b], 1 - lanes.bit(1 - b), 0)) for b in (0, 1)]
        stays = [pick(totals[b], lanes.bit(1 - b), 0) for b in (0, 1)]
        comes = [lanes.over_p(goes[b], 1 << (1 - b)) for b in (0, 1)]

    def feed_gradients_home():
        return [lanes.swap(one) for one in away], feed_gradients(0)

    came, home = stage(feed_gradients_home)
    if fits:
        comes = after(comes, home[1])
        d_normed_part = jnp.concatenate(
            [stay + one.astype(F32) for stay, one in zip(stays, comes)], axis=-1
        ).reshape(4, SUB, D)
    if fits:
        came = add_split(own, n_p, home, came)
    else:
        home, came = [jnp.concatenate(two, axis=-1).astype(F32) for two in (home, came)]
        came = split_rows(own, lowered(home + came).reshape(4, n_p, rows, 3 * units), 1)
    came = [came[0]] + [lanes.over_p(came[e], e) for e in range(1, n_p)]
    out_line = lax.psum_scatter(
        after(out_part, d_normed_part), "p", scatter_dimension=0, tiled=True
    )

    def second_norm_backward():
        d_normed_two = lanes.scatter_z(d_normed_part, False)
        d_resid = dy_own.astype(F32) + norm_back(resid, inverse_two, d_normed_two)
        return d_resid, jnp.concatenate(lanes.gather_z(lowered(d_resid)))

    d_resid, d_resid_chunk = stage(second_norm_backward)
    came = turned(own, after(came, d_resid_chunk), 1)
    d_resid_chunk = after(d_resid_chunk, *came)
    came = [came[0]] + [lanes.over_z(came[step], step) for step in (1, 2, 3)]

    def attention_backward():
        d_mixed = [product(d_resid_chunk, weight) for weight in weights]
        d_mixed = in_parts(quarters_of(d_mixed, 1))
        d_mixed = lowered(jnp.concatenate(d_mixed, axis=-1))
        d_attended = jnp.concatenate([d_mixed[:, :HD], d_mixed[:, HD:]])
        keys_all, values_all = pair_all[:, :HD], pair_all[:, HD:]
        d_probs = contract(d_attended, values_all, 1, 1)
        delta = jnp.sum(probs * d_probs, axis=-1, keepdims=True)
        d_scores = lowered(probs * (d_probs - delta))
        d_query_heads = product(d_scores, keys_all) * scaling
        d_key_all = contract(d_scores, query_heads, 0, 0) * scaling
        d_value_all = contract(lowered(probs), d_attended, 0, 0)
        middle = n_p * chunk
        d_pair = [d_key_all, d_value_all]
        cames = [lanes.swap(lowered(one[middle:])) for one in d_pair]
        return d_query_heads, [lowered(one[:middle]) for one in d_pair], cames

    d_query_heads, d_pair_keeps, d_pair_cames = stage(attention_backward)

    def attention_gradients():
        def summed_over_group(place, lead, keeps, cames):
            halves = add_halved(place, lead, n_p, keeps, cames, lanes.orders())
            done = []
            for (stay, goes), order in zip(halves, lanes.orders()):
                have = list(range(lanes.bits))
                for b, following in zip(order, order[1:] + [None]):
                    other = lanes.over_p(goes, 1 << b)
                    have.remove(b)
                    if following is None:
                        stay = lowered(stay.astype(F32) + other.astype(F32))
                    else:
                        stay, goes = sum_halved(place, stay, other, have.index(following), following)
                done.append(stay.reshape(lead * stay.shape[2], stay.shape[-1]))
            return done

        keeps = [[keep] for keep in d_pair_keeps]
        d_key, d_value = [
            one.astype(F32)
            for one in summed_over_group(jnp.zeros_like(own), 1, keeps, d_pair_cames)
        ]
        d_key = lowered(rotate(d_key, cosine, -sine))
        d_value = lowered(d_value)
        d_query = [
            lowered(rotate(one, cosine, -sine))
            for one in (d_query_heads[:chunk], d_query_heads[chunk:])
        ]
        lefts = (normed, d_resid_chunk)
        rights = [d_query[0], mixed[:, :quarter], d_query[1], mixed[:, quarter : 2 * quarter]]
        others = [d_key, mixed[:, 2 * quarter : 3 * quarter], d_value, mixed[:, 3 * quarter :]]
        keep, away = [], []
        for k in range(4):
            mine, theirs = jnp.where(first_core, rights[k], others[k]), jnp.where(
                first_core, others[k], rights[k]
            )
            keep.append(lowered(contract(lefts[k % 2], mine, 0, 0)))
            away.append(lowered(contract(lefts[k % 2], theirs, 0, 0)))
        cames = [
            lanes.swap(jnp.concatenate(away[at : at + 2], axis=-1)) for at in (0, 2)
        ]
        summed = summed_over_group(own, 4, [keep[:2], keep[2:]], cames)
        in_turn = [half[:, :HD] for half in summed] + [half[:, HD:] for half in summed]
        in_turn = jnp.concatenate(in_turn, axis=-1).reshape(4, rows, 3 * QW // 2)
        return in_turn, in_parts(d_query + [d_key, d_value])

    in_turn, d_projected = stage(attention_gradients)
    homeward = lanes.send_z(in_turn)

    def beside_home():
        joined_came = joined(own, came, 0).reshape(n_ctx, rows, 3 * units)
        shares = squares_of_feed(gain_two, w_gate, w_up, joined_came) if fits else in_turn
        d_normed_part = sum(
            contract(part, weight, 1, 1) for part, weight in zip(filled(d_projected, 0), weights)
        ).reshape(4, SUB, D)
        parts = [
            jnp.concatenate(
                [d_normed_part[s], pick(out_line.reshape(4, SUB, D), lanes.z ^ s, 0).astype(F32)]
            )
            for s in range(4)
        ]
        near = lowered(jnp.stack([parts[3], parts[1]]))
        return joined_came, shares, parts[0], parts[2], near

    came, shares, line_own, line_far, line_near = stage(beside_home)
    part_zero, part_one = lanes.group_home(lanes.join_z(after(homeward, line_near)))
    line_near = after(line_near, part_zero)
    near = lanes.over_z(line_near, 1)
    masters = (w_query, w_key, w_value, w_out, w_gate, w_up, w_down)
    if fits:
        shared = squares_of_attention(gain_one, masters, part_zero, part_one, shares)
    else:

        def of_owner(k):
            part = came[:, :, k * units : (k + 1) * units].transpose(1, 0, 2)
            return part.reshape(rows, n_ctx * units).astype(F32)

        inner_gate, inner_up, grad_down = of_owner(0), of_owner(1), of_owner(2).T
        grad_out = jnp.concatenate([part_zero[:, :, QW:], part_one[:, :, QW:]], axis=-1)
        grad_out = grad_out.astype(F32).transpose(0, 2, 1).reshape(2 * QW, rows)
        inner_query = part_zero[:, :, :QW].astype(F32).transpose(1, 0, 2).reshape(rows, 2 * QW)
        inner_pair = part_one[:, :, :QW].astype(F32).transpose(1, 0, 2)
        inner_key = inner_pair[:, :, :HD].reshape(rows, 2 * HD)
        inner_value = inner_pair[:, :, HD:].reshape(rows, 2 * HD)

        def weighed(matrix, inner):
            return jnp.sum(lowered(matrix).astype(F32) * inner, axis=1)

        first = weighed(w_query, inner_query) + weighed(w_key, inner_key)
        grad_gains = jnp.stack(
            [
                first + weighed(w_value, inner_value),
                weighed(w_gate, inner_gate) + weighed(w_up, inner_up),
            ]
        )
        gradients = (
            inner_query * gain_one,
            inner_key * gain_one,
            inner_value * gain_one,
            grad_out,
            inner_gate * gain_two,
            inner_up * gain_two,
            grad_down,
        )
        squares = sum(jnp.sum(gradient * gradient) for gradient in gradients)
        shared = jnp.concatenate([grad_gains, jnp.broadcast_to(squares, (6, rows))])
    shared = shared + lanes.swap(shared)
    grad_gains = shared[:2]
    squares = jnp.broadcast_to(shared[2:3, :1] + jnp.sum(grad_gains * grad_gains), (8, 128))
    for b in range(lanes.bits):
        squares = squares + lanes.over_p(squares, 1 << b)
    for s in (1, 2):
        squares = squares + lanes.over_z(squares, s)
    near = after(near, squares)
    far = lanes.over_z(lowered(line_far + near[0].astype(F32)), 2)
    grad_norm = jnp.sqrt(squares[0, 0])
    factor = CLIP_NORM / jnp.maximum(grad_norm, CLIP_NORM)
    wo_fan = min(HQ * HD, max(2, 131072 // total_rows))
    rate_in = 2.0 / math.sqrt(D)
    step_rates = (
        rate_in,
        rate_in,
        rate_in,
        2.0 / math.sqrt(wo_fan),
        rate_in,
        rate_in,
        2.0 / math.sqrt(FF),
    )
    if fits:
        new_weights, copies, moment_first, moment_second = adamw_blocks(
            step_rates,
            factor,
            gain_one,
            gain_two,
            masters,
            (moment_one, moment_two),
            part_zero,
            part_one,
            came,
        )
    else:
        new_weights = []
        firsts = []
        seconds = []
        offset = 0
        for index_now in range(7):
            weight = masters[index_now]
            length = weight.size
            first_moment = moment_one[offset : offset + length].reshape(weight.shape)
            second_moment = moment_two[offset : offset + length].reshape(weight.shape)
            updated, first_new, second_new = adamw_step(
                weight,
                factor * gradients[index_now],
                first_moment,
                second_moment,
                step_rates[index_now],
                WEIGHT_DECAY,
            )
            new_weights.append(updated)
            firsts.append(first_new.reshape(-1))
            seconds.append(second_new.reshape(-1))
            offset = offset + length
        copies = [lowered(weight) for weight in new_weights]
        moment_first, moment_second = jnp.concatenate(firsts), jnp.concatenate(seconds)
    line_sums = line_own + near[1].astype(F32) + after(far, new_weights[0]).astype(F32)
    d_normed, out_sum = line_sums[:SUB], line_sums[SUB:]
    x_float = x_own.astype(F32)
    inverse_own = lax.rsqrt(jnp.mean(x_float * x_float, axis=-1, keepdims=True) + NORM_EPS)
    input_grad = lowered(d_resid + norm_back(x_float, inverse_own, d_normed))
    input_grad, layer_out = both_cores(input_grad), both_cores(lowered(resid + out_sum))
    new_gains, gain_first, gain_second = adamw_step(
        gains, factor * grad_gains, gain_moment_one, gain_moment_two, GAIN_RATE, 0.0
    )
    return (
        layer_out,
        input_grad,
        grad_norm,
        *new_weights,
        new_gains,
        *copies,
        lowered(new_gains),
        moment_first,
        moment_second,
        gain_first,
        gain_second,
    )


def solution(mesh):
    n_ctx, n_head = mesh.devices.shape
    lanes_mesh = Mesh(mesh.devices.reshape(4, n_ctx // 4, n_head), ("z", "p", "head"))
    ctx = ("z", "p")
    rows = P(ctx, None)
    wide = P(ctx, "head")
    tall = P("head", ctx)
    flat = P(("z", "p", "head"))
    gain = P(None, ctx)
    weights = (wide, wide, wide, tall, wide, wide, tall, gain)
    return jax.shard_map(
        local,
        mesh=lanes_mesh,
        in_specs=(rows, P(), rows, *weights, flat, flat, gain, gain),
        out_specs=(rows, rows, P(), *weights, *weights, flat, flat, gain, gain),
        check_vma=False,
    )
```

```python
import math

import jax
import jax.numpy as jnp
from jax import lax
from jax.experimental import pallas as pl
from jax.experimental.pallas import tpu as pltpu
from jax.sharding import Mesh
from jax.sharding import PartitionSpec as P

D = 2048
HQ = 8
KV = 4
HD = 256
FF = 8192
SUB = 64
STEP = 10
SHARE = HQ // KV
QW = SHARE * HD


NORM_EPS = 1e-06
ROPE_BASE = 1000042.0
BETA_ONE = 0.9
BETA_TWO = 0.95
ADAM_EPS = 1e-08
WEIGHT_DECAY = 0.1
GAIN_RATE = 0.5
CLIP_NORM = 1.0
MASKED_SCORE = -1e30
BF = jnp.bfloat16
F32 = jnp.float32
SWAP = [(0, 1), (1, 0)]


def lowered(array_in):
    return array_in.astype(BF)


def product(left, right):
    return jnp.dot(left, right, preferred_element_type=F32)


def contract(left, right, left_dim, right_dim):
    return lax.dot_general(
        left, right, (((left_dim,), (right_dim,)), ((), ())), preferred_element_type=F32
    )


def rotary_tables(positions):
    frequency = ROPE_BASE ** (-jnp.arange(0, HD, 2, dtype=F32) / HD)
    angles = positions.astype(F32)[:, None] * frequency[None, :]
    return (jnp.cos(angles), jnp.sin(angles))


def rotate(one_head, cosine, sine):
    half_size = HD // 2
    first_half = one_head[:, :half_size]
    second_half = one_head[:, half_size:]
    return jnp.concatenate(
        [first_half * cosine - second_half * sine, second_half * cosine + first_half * sine],
        axis=-1,
    )


def adamw_step(weight, gradient, first_moment, second_moment, step_rate, decay_rate):
    first_new = BETA_ONE * first_moment + (1.0 - BETA_ONE) * gradient
    second_new = BETA_TWO * second_moment + (1.0 - BETA_TWO) * gradient * gradient
    ratio = (
        first_new
        / (1.0 - BETA_ONE**STEP)
        / (jnp.sqrt(second_new / (1.0 - BETA_TWO**STEP)) + ADAM_EPS)
    )
    return (weight - step_rate * (ratio + decay_rate * weight), first_new, second_new)


def pick(array_in, index, axis):
    return lax.dynamic_index_in_dim(array_in, index, axis, keepdims=False)


def after(arrays, *others):
    listed = arrays if isinstance(arrays, list) else [arrays]
    if not others:
        return arrays
    anywhere = pl.BlockSpec(memory_space=pl.ANY)
    out = pl.pallas_call(
        lambda *refs: None,
        in_specs=[anywhere] * (len(listed) + len(others)),
        out_specs=[anywhere] * len(listed),
        out_shape=[jax.ShapeDtypeStruct(array.shape, array.dtype) for array in listed],
        input_output_aliases={k: k for k in range(len(listed))},
        name="after",
    )(*listed, *others)
    return list(out) if isinstance(arrays, list) else out[0]


class Lanes:
    def __init__(self):
        self.n_p = lax.axis_size("p")
        self.z = lax.axis_index("z")
        self.p = lax.axis_index("p")
        self.h = lax.axis_index("head")
        self.bits = self.n_p.bit_length() - 1
        self.cube = [2] * self.bits

    def swap(self, array_in):
        return lax.ppermute(array_in, "head", SWAP)

    def over_z(self, array_in, step):
        return lax.ppermute(array_in, "z", [(i, i ^ step) for i in range(4)])

    def over_p(self, array_in, step):
        return lax.ppermute(array_in, "p", [(i, i ^ step) for i in range(self.n_p)])

    def orders(self):
        return list(range(self.bits)), list(range(self.bits))[::-1]

    def bit(self, b):
        return (self.p >> b) & 1

    def absolute(self, pieces, index, axis=0):
        for b in range(len(pieces).bit_length() - 1):
            odd = ((index >> b) & 1) == 1
            pieces = [jnp.where(odd, pieces[j ^ (1 << b)], pieces[j]) for j in range(len(pieces))]
        return jnp.stack(pieces, axis)

    def gather_z(self, array_in):
        one, two = self.over_z(array_in, 1), self.over_z(array_in, 2)
        return [array_in, one, two, self.over_z(two, 1)]

    def send_z(self, array_in, axis=0):
        pieces = [pick(array_in, self.z, axis)]
        for s in (1, 2, 3):
            pieces.append(self.over_z(pick(array_in, self.z ^ s, axis), s))
        return pieces

    def join_z(self, pieces, axis=0):
        return self.absolute(pieces, self.z, axis)

    def scatter_z(self, array_in, relative):
        parts = [pick(array_in, s if relative else self.z ^ s, 0).astype(F32) for s in range(4)]
        near = self.over_z(lowered(jnp.stack([parts[3], parts[1]])), 1).astype(F32)
        far = self.over_z(lowered(parts[2] + near[0]), 2).astype(F32)
        return parts[0] + near[1] + far

    def gather_p(self, array_in, order, relative, lead=0):
        have = []
        for b in order:
            other = self.over_p(array_in, 1 << b)
            axis = lead + sum(1 for x in have if x > b)
            mine, other = jnp.expand_dims(array_in, axis), jnp.expand_dims(other, axis)
            array_in = jnp.concatenate([mine, other], axis)
            if not relative:
                array_in = jnp.where(
                    self.bit(b) == 1, jnp.concatenate([other, mine], axis), array_in
                )
            have.append(b)
        return array_in

    def gather_cube(self, array_in, order):
        held = [(array_in[None], [0])]
        for b in order:
            numbers = [j for _, part in held for j in part]
            whole = jnp.concatenate([array for array, _ in held]) if len(held) > 1 else held[0][0]
            held.append((self.over_p(whole, 1 << b), [j ^ (1 << b) for j in numbers]))
        return held

    def scatter_p(self, array_in, order, relative, lead=0):
        have = list(range(self.bits))
        for b in order:
            axis = lead + sum(1 for x in have if x > b)
            bit = 0 if relative else self.bit(b)
            keep, send = pick(array_in, bit, axis), pick(array_in, 1 - bit, axis)
            array_in = keep.astype(F32) + self.over_p(lowered(send), 1 << b).astype(F32)
            have.remove(b)
        return array_in

    def halves(self, array_in):
        middle = array_in.shape[-1] // 2
        return array_in[..., :middle], array_in[..., middle:]

    def group_blocks(self, part_zero, part_one):
        first = self.h == 0
        keep = jnp.where(first, part_zero, part_one).transpose(1, 0, 2)
        other = self.swap(jnp.where(first, part_one, part_zero).transpose(1, 0, 2))
        return jnp.where(
            first, jnp.concatenate([keep, other]), jnp.concatenate([other, keep])
        )

    def group_home(self, blocks):
        first = self.h == 0
        own = jnp.where(first, blocks[:2], blocks[2:])
        other = self.swap(jnp.where(first, blocks[2:], blocks[:2]))
        return jnp.where(first, own, other), jnp.where(first, other, own)


def moved(own, inputs, shapes, plan):
    def kernel(own_ref, *refs):
        ins, outs = refs[: len(inputs)], refs[len(inputs) :]
        for source, target in plan(ins, outs, own_ref[0], own_ref[1]):
            if isinstance(source, tuple):
                total = sum(one[...].astype(F32) for one in source)
                target[...] = total.astype(target.dtype)
            else:
                target[...] = source[...]

    vmem = pl.BlockSpec(memory_space=pltpu.VMEM)
    return pl.pallas_call(
        kernel,
        in_specs=[pl.BlockSpec(memory_space=pltpu.SMEM)] + [vmem] * len(inputs),
        out_specs=[vmem] * len(shapes),
        out_shape=[jax.ShapeDtypeStruct(shape, inputs[0].dtype) for shape in shapes],
        compiler_params=pltpu.CompilerParams(vmem_limit_bytes=60 * 1024 * 1024),
        name="moved",
    )(own, *inputs)


def split_rows(own, array_in, which):
    count = array_in.shape[which]
    shape = array_in.shape[:which] + array_in.shape[which + 1 :]

    def plan(ins, outs, z, p):
        if which == 0:
            return [(ins[0].at[z ^ j], outs[j]) for j in range(count)]
        return [(ins[0].at[:, p ^ j], outs[j]) for j in range(count)]

    return moved(own, [array_in], [shape] * count, plan)


def joined(own, pieces, which):
    count = len(pieces)
    shape = pieces[0].shape
    shape = shape[:which] + (count,) + shape[which:]

    def plan(ins, outs, z, p):
        if which == 0:
            return [(ins[j], outs[0].at[z ^ j]) for j in range(count)]
        return [(ins[j], outs[0].at[:, p ^ j]) for j in range(count)]

    return moved(own, pieces, [shape], plan)[0]


def turned(own, pieces, which):
    count = len(pieces)
    other = pieces[0].shape[0]
    shape = (count,) + pieces[0].shape[1:]

    def plan(ins, outs, z, p):
        mine, theirs = (z, p) if which == 0 else (p, z)
        return [
            (ins[i].at[theirs ^ j], outs[j].at[mine ^ i])
            for i in range(count)
            for j in range(other)
        ]

    return moved(own, pieces, [shape] * other, plan)


def placed(own, halves, in_front):
    arrays = [array for half in halves for array, _ in half]
    n_p = sum(len(numbers) for _, numbers in halves[0])
    block = halves[0][0][0].shape[1:]
    widths = [half[0][0].shape[-1] for half in halves]
    lead = (n_p, block[0]) if in_front else (block[0], n_p)
    shapes = [lead + block[1:-1] + (sum(widths),)]

    def plan(ins, outs, z, p):
        pairs, at = [], 0
        for k, half in enumerate(halves):
            lanes = pl.ds(sum(widths[:k]), widths[k])
            for _, numbers in half:
                for i, j in enumerate(numbers):
                    if in_front:
                        target = outs[0].at[p ^ j, :, :, lanes]
                    else:
                        target = outs[0].at[:, p ^ j, :, lanes]
                    pairs.append((ins[at].at[i], target))
                at = at + 1
        return pairs

    return moved(own, arrays, shapes, plan)[0]


def add_split(own, n_p, home, came):
    rows = home[0].shape[0] // (4 * n_p)

    def kernel(own_ref, gate_up_ref, down_ref, gate_up_came, down_came, *outs):
        sides = (
            (gate_up_ref, gate_up_came, pl.ds(0, 512)),
            (down_ref, down_came, pl.ds(512, 256)),
        )
        for j in range(n_p):
            for z in range(4):
                at = pl.multiple_of((z * n_p + (own_ref[1] ^ j)) * rows, rows)
                at = pl.ds(at, rows)
                for ref, came_ref, lanes in sides:
                    total = ref[at, :].astype(F32) + came_ref[at, :].astype(F32)
                    outs[j][z, :, lanes] = lowered(total)

    vmem = pl.BlockSpec(memory_space=pltpu.VMEM)
    return pl.pallas_call(
        kernel,
        in_specs=[pl.BlockSpec(memory_space=pltpu.SMEM)] + [vmem] * 4,
        out_specs=[vmem] * n_p,
        out_shape=[jax.ShapeDtypeStruct((4, rows, 768), BF)] * n_p,
        compiler_params=pltpu.CompilerParams(vmem_limit_bytes=60 * 1024 * 1024),
        name="add_split",
    )(own, *home, *came)


def half_numbers(count, at, bit):
    return [((k >> at) << (at + 1)) | (k & ((1 << at) - 1)) | (bit << at) for k in range(count // 2)]


def add_halved(own, lead, n_p, keeps, cames, orders):
    rows = cames[0].shape[0] // (lead * n_p)
    counts = [len(keep) for keep in keeps]
    shape = (lead, n_p // 2, rows, cames[0].shape[1])

    def kernel(own_ref, *refs):
        outs = refs[-4:]
        at = 0
        for half, order in enumerate(orders):
            parts, came = refs[at : at + counts[half]], refs[at + counts[half]]
            at = at + counts[half] + 1
            bit = (own_ref[1] >> order[0]) & 1
            for target, value in ((outs[2 * half], bit), (outs[2 * half + 1], 1 - bit)):
                for k, number in enumerate(half_numbers(n_p, order[0], value)):
                    for z in range(lead):
                        from_rows = pl.ds(pl.multiple_of((z * n_p + number) * rows, rows), rows)
                        low = 0
                        for part in parts:
                            lanes = pl.ds(low, part.shape[1])
                            low = low + part.shape[1]
                            total = part[from_rows, :].astype(F32)
                            total = total + came[from_rows, lanes].astype(F32)
                            target[z, k, :, lanes] = lowered(total)

    vmem = pl.BlockSpec(memory_space=pltpu.VMEM)
    inputs = [one for keep, came in zip(keeps, cames) for one in [*keep, came]]
    outs = pl.pallas_call(
        kernel,
        in_specs=[pl.BlockSpec(memory_space=pltpu.SMEM)] + [vmem] * len(inputs),
        out_specs=[vmem] * 4,
        out_shape=[jax.ShapeDtypeStruct(shape, BF)] * 4,
        compiler_params=pltpu.CompilerParams(vmem_limit_bytes=60 * 1024 * 1024),
        name="add_halved",
    )(own, *inputs)
    return outs[:2], outs[2:]


def sum_halved(own, stay, came, at, b):
    count = stay.shape[1]
    shape = (stay.shape[0], count // 2) + stay.shape[2:]

    def plan(ins, outs, z, p):
        bit = (p >> b) & 1
        pairs = []
        for target, value in ((outs[0], bit), (outs[1], 1 - bit)):
            for k, number in enumerate(half_numbers(count, at, value)):
                pairs.append(((ins[0].at[:, number], ins[1].at[:, number]), target.at[:, k]))
        return pairs

    return moved(own, [stay, came], [shape] * 2, plan)


def feed_weights(own, pieces):
    count = len(pieces)

    def plan(ins, outs, z, p):
        pairs = []
        for j in range(count):
            pairs.append((ins[j].at[:, :, pl.ds(0, 512)], outs[0].at[:, p ^ j]))
            pairs.append((ins[j].at[:, :, pl.ds(512, 256)], outs[1].at[:, p ^ j]))
        return pairs

    gate_up, down = moved(own, pieces, [(4, count, 128, 512), (4, count, 128, 256)], plan)
    return [gate_up.reshape(D, 512), down.reshape(D, 256)]


def feed_forward_kernel(
    own_ref, normed_ref, dy_ref, here_ref, there_ref, down_here_ref, down_there_ref,
    hidden_ref, d_zero_ref, d_one_ref, stay_zero_ref, goes_zero_ref, stay_one_ref, goes_one_ref,
):
    step = pl.program_id(0)
    normed = normed_ref[...]
    d_normed = None
    dy = dy_ref[...]
    sides = ((down_here_ref, here_ref, d_zero_ref), (down_there_ref, there_ref, d_one_ref))
    for core, (down_ref, weight_ref, d_ref) in enumerate(sides):
        weight = weight_ref[...]
        gate_up = product(normed, weight)
        gate_values, up_values = gate_up[:, :256], gate_up[:, 256:]
        incoming = product(dy, down_ref[...])
        sigmoid_gate = jax.nn.sigmoid(gate_values)
        activated = gate_values * sigmoid_gate
        hidden_ref[:, pl.ds(core * 256, 256)] = lowered(activated * up_values)
        slope = sigmoid_gate * (1.0 + gate_values * (1.0 - sigmoid_gate))
        d_ref[:, pl.ds(0, 256)] = lowered(incoming * up_values * slope)
        d_ref[:, pl.ds(256, 256)] = lowered(incoming * activated)
        partial = contract(d_ref[...], weight, 1, 1)
        d_normed = partial if d_normed is None else d_normed + partial
    d_normed = lowered(d_normed)
    halves = ((0, stay_zero_ref, goes_zero_ref), (1, stay_one_ref, goes_one_ref))
    for b, stay_ref, goes_ref in halves:
        stays = ((step >> b) & 1) == ((own_ref[1] >> b) & 1)
        place = (step >> 1) if b == 0 else (step & 1)
        part = d_normed[:, b * (D // 2) : (b + 1) * (D // 2)]

        @pl.when(stays)
        def _():
            stay_ref[place] = part

        @pl.when(jnp.logical_not(stays))
        def _():
            goes_ref[place] = part


def feed_forward_blocks(own, normed_all, dy_all, gate_up_weights, down_weights):
    quarter = normed_all.shape[0] // 4

    def of_rows(width):
        return pl.BlockSpec((quarter, width), lambda i: (i, 0))

    def whole(*shape):
        return pl.BlockSpec(shape, lambda i: (0,) * len(shape))

    half = (2, quarter, D // 2)
    return pl.pallas_call(
        feed_forward_kernel,
        grid=(4,),
        in_specs=[
            pl.BlockSpec(memory_space=pltpu.SMEM),
            of_rows(D),
            of_rows(D),
            whole(D, 512),
            whole(D, 512),
            whole(D, 256),
            whole(D, 256),
        ],
        out_specs=[of_rows(512), of_rows(512), of_rows(512)] + [whole(*half)] * 4,
        out_shape=[jax.ShapeDtypeStruct((4 * quarter, 512), BF)] * 3
        + [jax.ShapeDtypeStruct(half, BF)] * 4,
        compiler_params=pltpu.CompilerParams(
            dimension_semantics=("arbitrary",), vmem_limit_bytes=60 * 1024 * 1024
        ),
        name="feed_forward",
    )(own, normed_all, dy_all, *gate_up_weights, *down_weights)


def pack_kernel(n_p, own_ref, gain_ref, gate_ref, up_ref, down_ref, *outs):
    gain = jnp.broadcast_to(gain_ref[...], (128, 256))
    for s in range(4):
        for p in range(n_p):
            at = pl.multiple_of(((own_ref[0] ^ s) * n_p + p) * 256, 256)
            outs[s][p, :, pl.ds(0, 256)] = lowered(gate_ref[:, pl.ds(at, 256)] * gain)
            outs[s][p, :, pl.ds(256, 256)] = lowered(up_ref[:, pl.ds(at, 256)] * gain)
            outs[s][p, :, pl.ds(512, 256)] = lowered(down_ref[pl.ds(at, 256), :].T)


def pack_feed(own, gain, w_gate, w_up, w_down, n_p):
    vmem = pl.BlockSpec(memory_space=pltpu.VMEM)
    return pl.pallas_call(
        lambda *refs: pack_kernel(n_p, *refs),
        in_specs=[pl.BlockSpec(memory_space=pltpu.SMEM), vmem, vmem, vmem, vmem],
        out_specs=[vmem] * 4,
        out_shape=[jax.ShapeDtypeStruct((n_p, 128, 768), BF)] * 4,
        compiler_params=pltpu.CompilerParams(vmem_limit_bytes=60 * 1024 * 1024),
        name="pack_feed",
    )(own, gain, w_gate, w_up, w_down)


def squares_body(gain_ref, blocks, plain, base_ref, row, out_ref, squares_ref, along_ref):
    step = pl.program_id(0)
    height = gain_ref.shape[0]
    here = pl.ds(pl.multiple_of(step * height, height), height)

    @pl.when(step == 0)
    def _():
        squares_ref[...] = jnp.zeros_like(squares_ref)

    nothing = jnp.zeros((height, 128), F32)
    scaled, unscaled, along = nothing, nothing, nothing
    for weight, gradient in blocks:
        gradient = gradient.astype(F32)
        scaled = scaled + gradient * gradient
        along = along + lowered(weight).astype(F32) * gradient
    for gradient in plain:
        gradient = gradient.astype(F32)
        unscaled = unscaled + gradient * gradient
    gain = gain_ref[...]
    along_ref[here, :] = along
    squares_ref[...] += scaled * (gain * gain) + unscaled

    @pl.when(step == pl.num_programs(0) - 1)
    def _():
        total = jnp.sum(squares_ref[...], keepdims=True)
        if base_ref is None:
            out_ref[...] = jnp.broadcast_to(total, (8, 128))
        else:
            out_ref[...] = base_ref[...] + total
            out_ref[1:2, :] = base_ref[1:2, :]
        out_ref[row : row + 1, :] = jnp.sum(along_ref[...].T, axis=0, keepdims=True)


def lanes_of(t):
    return pl.ds(t * 128, 128)


def feed_squares_kernel(gain_ref, gate_ref, up_ref, feed_ref, *outs):
    def column(c, t):
        return feed_ref[c, :, lanes_of(t)]

    blocks = [(gate_ref[:, lanes_of(t)], column(t // 2, t % 2)) for t in range(32)]
    blocks += [(up_ref[:, lanes_of(t)], column(t // 2, t % 2 + 2)) for t in range(32)]
    plain = [column(c, t) for c in range(16) for t in (4, 5)]
    squares_body(gain_ref, blocks, plain, None, 1, *outs)


def attention_squares_kernel(
    gain_ref, query_ref, key_ref, value_ref, zero_ref, one_ref, base_ref, *outs
):
    def column(ref, l, t):
        return ref[l, :, lanes_of(t)]

    blocks = [(query_ref[:, lanes_of(t)], column(zero_ref, t // 4, t % 4)) for t in range(8)]
    blocks += [(key_ref[:, lanes_of(t)], column(one_ref, t // 2, t % 2)) for t in range(4)]
    blocks += [(value_ref[:, lanes_of(t)], column(one_ref, t // 2, t % 2 + 2)) for t in range(4)]
    plain = [column(ref, l, t) for ref in (zero_ref, one_ref) for l in (0, 1) for t in (4, 5)]
    squares_body(gain_ref, blocks, plain, base_ref, 0, *outs)


def squares_call(kernel, arrays, height, name):
    def spec(array):
        if array.ndim == 3:
            return pl.BlockSpec((array.shape[0], height, array.shape[2]), lambda i: (0, i, 0))
        if array.shape[0] == 8:
            return pl.BlockSpec((8, 128), lambda i: (0, 0))
        return pl.BlockSpec((height, array.shape[1]), lambda i: (i, 0))

    return pl.pallas_call(
        kernel,
        grid=(128 // height,),
        in_specs=[spec(array) for array in arrays],
        out_specs=pl.BlockSpec((8, 128), lambda i: (0, 0)),
        out_shape=jax.ShapeDtypeStruct((8, 128), F32),
        scratch_shapes=[pltpu.VMEM((height, 128), F32), pltpu.VMEM((128, 128), F32)],
        compiler_params=pltpu.CompilerParams(
            dimension_semantics=("arbitrary",), vmem_limit_bytes=60 * 1024 * 1024
        ),
        name=name,
    )(*arrays)


def squares_of_feed(gain_two, w_gate, w_up, came):
    return squares_call(feed_squares_kernel, [gain_two, w_gate, w_up, came], 16, "feed_squares")


def squares_of_attention(gain_one, masters, part_zero, part_one, shares):
    arrays = [gain_one, *masters[:3], part_zero, part_one, shares]
    return squares_call(attention_squares_kernel, arrays, 64, "attention_squares")


STEP_ROWS = (128, 64, 64, 128, 512, 512, 512)
STEPS = 8


def adamw_kernel(rates, factor_ref, gain_one_ref, gain_two_ref, *refs):
    masters, firsts, seconds = refs[:7], refs[7:14], refs[14:21]
    query_ref, pair_ref, out_zero_ref, out_one_ref, feed_ref, down_ref = refs[21:27]
    new_refs, copy_refs = refs[27:34], refs[34:41]
    first_hbm, second_hbm, first_buf, second_buf, sems = refs[41:]
    step = pl.program_id(0)
    slot = lax.rem(step, 2)
    factor = factor_ref[0, 0]
    offsets = [sum(STEP_ROWS[:k]) for k in range(7)]

    def moves(of_step, of_slot):
        out = []
        for k in range(7):
            base = STEPS * offsets[k]
            for j, (buf, hbm) in enumerate(((first_buf, first_hbm), (second_buf, second_hbm))):
                out.append(
                    pltpu.make_async_copy(
                        buf.at[of_slot, pl.ds(offsets[k], STEP_ROWS[k])],
                        hbm.at[pl.ds(base + of_step * STEP_ROWS[k], STEP_ROWS[k])],
                        sems.at[of_slot, 2 * k + j],
                    )
                )
        return out

    @pl.when(step >= 2)
    def _():
        for move in moves(step - 2, slot):
            move.wait()

    def update(k, rows, lanes, flat, gradient):
        first = BETA_ONE * firsts[k][flat, :] + (1.0 - BETA_ONE) * gradient
        second = BETA_TWO * seconds[k][flat, :] + (1.0 - BETA_TWO) * gradient * gradient
        ratio = first / (jnp.sqrt(second * (1.0 / (1.0 - BETA_TWO**STEP))) + ADAM_EPS)
        weight = masters[k][rows, lanes]
        weight = weight * (1.0 - rates[k] * WEIGHT_DECAY) - ratio * (
            rates[k] / (1.0 - BETA_ONE**STEP)
        )
        new_refs[k][rows, lanes] = weight
        copy_refs[k][rows, lanes] = lowered(weight)
        return first, second

    def wide(k, gradient_of, scale):
        width = masters[k].shape[1] // 128
        for t in range(width):
            flat = pl.ds(t, 16, stride=width)
            first, second = update(
                k, slice(None), pl.ds(t * 128, 128), flat, gradient_of(t).astype(F32) * scale
            )
            store = pl.ds(offsets[k] + t, 16, stride=width)
            first_buf.at[slot][store, :] = first
            second_buf.at[slot][store, :] = second

    scale_one = jnp.broadcast_to(gain_one_ref[...] * factor, (16, 128))
    scale_two = jnp.broadcast_to(gain_two_ref[...] * factor, (16, 128))
    wide(0, lambda t: query_ref[t // 4, :, pl.ds(t % 4 * 128, 128)], scale_one)
    wide(1, lambda t: pair_ref[t // 2, :, pl.ds(t % 2 * 128, 128)], scale_one)
    wide(2, lambda t: pair_ref[t // 2, :, pl.ds(t % 2 * 128 + HD, 128)], scale_one)
    wide(4, lambda t: feed_ref[t // 2, :, pl.ds(t % 2 * 128, 128)], scale_two)
    wide(5, lambda t: feed_ref[t // 2, :, pl.ds(t % 2 * 128 + 256, 128)], scale_two)

    def tall(k, at, gradient):
        rows = pl.ds(at, 128)
        first, second = update(k, rows, slice(None), rows, gradient.astype(F32).T * factor)
        store = pl.ds(offsets[k] + at, 128)
        first_buf.at[slot][store, :] = first
        second_buf.at[slot][store, :] = second

    part = lax.rem(step // 2, 2) == 0
    tall(3, 0, jnp.where(part, out_zero_ref[0].astype(F32), out_one_ref[0].astype(F32)))
    for c in range(2):
        for t in range(2):
            tall(6, c * 256 + t * 128, down_ref[c, :, pl.ds(t * 128, 128)])

    for move in moves(step, slot):
        move.start()

    @pl.when(step == STEPS - 1)
    def _():
        for move in moves(step - 1, 1 - slot):
            move.wait()
        for move in moves(step, slot):
            move.wait()


def adamw_blocks(rates, factor, gain_one, gain_two, masters, moments, part_zero, part_one, came):
    shapes = [weight.shape for weight in masters]
    tables = [moment.reshape(-1, 128) for moment in moments]
    weight_specs = [
        pl.BlockSpec((shape[0] // STEPS, shape[1]), lambda i: (i, 0)) for shape in shapes
    ]
    starts = [sum(STEP_ROWS[:k]) * STEPS // STEP_ROWS[k] for k in range(7)]
    moment_specs = [
        pl.BlockSpec((STEP_ROWS[k], 128), lambda i, start=starts[k]: (start + i, 0))
        for k in range(7)
    ]
    gain_spec = pl.BlockSpec((16, 1), lambda i: (i, 0))
    rows_spec = pl.BlockSpec((2, 16, 2 * HD), lambda i: (0, i, 0))
    out_spec = pl.BlockSpec((1, 128, 128), lambda i: (i // 4, 0, 4 + i % 2))
    grad_specs = [
        rows_spec,
        rows_spec,
        out_spec,
        out_spec,
        pl.BlockSpec((16, 16, 512), lambda i: (0, i, 0)),
        pl.BlockSpec((2, 128, 256), lambda i: (i, 0, 2)),
    ]
    anywhere = pl.BlockSpec(memory_space=pl.ANY)
    outs = pl.pallas_call(
        lambda *refs: adamw_kernel(rates, *refs),
        grid=(STEPS,),
        in_specs=[
            pl.BlockSpec(memory_space=pltpu.SMEM),
            gain_spec,
            gain_spec,
            *weight_specs,
            *moment_specs,
            *moment_specs,
            *grad_specs,
        ],
        out_specs=[*weight_specs, *weight_specs, anywhere, anywhere],
        out_shape=[
            *[jax.ShapeDtypeStruct(shape, F32) for shape in shapes],
            *[jax.ShapeDtypeStruct(shape, BF) for shape in shapes],
            *[jax.ShapeDtypeStruct(table.shape, F32) for table in tables],
        ],
        scratch_shapes=[
            pltpu.VMEM((2, sum(STEP_ROWS), 128), F32),
            pltpu.VMEM((2, sum(STEP_ROWS), 128), F32),
            pltpu.SemaphoreType.DMA((2, 14)),
        ],
        compiler_params=pltpu.CompilerParams(
            dimension_semantics=("arbitrary",), vmem_limit_bytes=60 * 1024 * 1024
        ),
        name="adamw",
    )(
        factor.reshape(1, 1),
        gain_one,
        gain_two,
        *masters,
        *[tables[0]] * 7,
        *[tables[1]] * 7,
        part_zero,
        part_one,
        part_zero,
        part_one,
        came,
        came,
    )
    return outs[:7], outs[7:14], outs[14].reshape(-1), outs[15].reshape(-1)


def local(
    tokens,
    block_offsets,
    cotangent,
    w_query,
    w_key,
    w_value,
    w_out,
    w_gate,
    w_up,
    w_down,
    gains,
    moment_one,
    moment_two,
    gain_moment_one,
    gain_moment_two,
):
    lanes = Lanes()
    n_p, h = lanes.n_p, lanes.h
    n_ctx = 4 * n_p
    total_rows = n_ctx * 2 * SUB
    rows = D // n_ctx
    units = FF // (2 * n_ctx)
    chunk = 4 * SUB
    scaling = 1.0 / math.sqrt(HD)
    first_core = h == 0
    gain_low = lowered(gains).astype(F32)
    gain_one, gain_two = gain_low[0][:, None], gain_low[1][:, None]
    in_order = block_offsets[0] >= 0
    fits = rows == 128 and n_p == 4
    own = jnp.stack([lanes.z, lanes.p]).astype(jnp.int32)

    def stage(body):
        shapes = jax.eval_shape(body)
        return lax.cond(
            in_order, body, lambda: jax.tree.map(lambda a: jnp.zeros(a.shape, a.dtype), shapes)
        )

    def both_cores(own):
        other = lanes.swap(own)
        return jnp.where(
            first_core, jnp.concatenate([own, other]), jnp.concatenate([other, own])
        )

    def norm_back(inputs, inverse, incoming):
        inner = jnp.mean(incoming * inputs, axis=-1, keepdims=True)
        return inverse * incoming - inputs * (inverse * inverse * inverse * inner)

    x_own = lax.dynamic_slice_in_dim(tokens, h * SUB, SUB)
    dy_own = lax.dynamic_slice_in_dim(cotangent, h * SUB, SUB)

    query_part = lowered((w_query * gain_one).reshape(rows, 2, QW))
    key_part = lowered((w_key * gain_one).reshape(rows, 2, HD))
    value_part = lowered((w_value * gain_one).reshape(rows, 2, HD))
    out_part = lowered(w_out).T.reshape(rows, 2, QW)
    quarter = QW // 4
    out_parts = [out_part[:, :, k * quarter : (k + 1) * quarter] for k in range(4)]
    blocks = lanes.group_blocks(
        jnp.concatenate(
            [query_part[:, :, :HD], out_parts[0], query_part[:, :, HD:], out_parts[1]], axis=-1
        ),
        jnp.concatenate([key_part, out_parts[2], value_part, out_parts[3]], axis=-1),
    )
    split = rows * 3 * QW // 2 // SUB
    mine = []
    for step in range(4):
        block = pick(blocks, lanes.z ^ step, 0).reshape(2, rows // 2, 3 * QW // 2)
        if rows == 2 * SUB:
            block = jnp.concatenate([block[0], block[1]], axis=-1)
        else:
            block = block.reshape(SUB, split)
        mine.append(jnp.concatenate([block, x_own], axis=-1))
    mine = [mine[0]] + [lanes.over_z(mine[step], step) for step in (1, 2, 3)]
    if fits:
        feed = pack_feed(own, after(gain_two, blocks), w_gate, w_up, w_down, n_p)
    else:
        feed = w_gate * gain_two, w_up * gain_two, w_down.T
        feed = [lowered(matrix).reshape(rows, 4, n_p, units) for matrix in feed]
        feed = jnp.concatenate(feed, axis=-1).transpose(1, 2, 0, 3)
        feed = split_rows(own, feed, 0)
    mine = after(mine, feed[0])
    x_pieces = [piece[:, split:] for piece in mine]
    if rows == 2 * SUB:
        middle = split // 2
        mine = [jnp.concatenate([one[:, :middle], one[:, middle:split]]) for one in mine]
    else:
        mine = [one[:, :split].reshape(rows, 3 * QW // 2) for one in mine]
    mine = lanes.join_z(mine)
    dy_line = lax.all_gather(after(dy_own, mine), "z", axis=0, tiled=True)
    feed = after(list(feed), mine)
    feed = [feed[0]] + [lanes.over_z(feed[step], step) for step in (1, 2, 3)]

    x_chunk = jnp.concatenate(x_pieces).astype(F32)
    inverse_chunk = lax.rsqrt(jnp.mean(x_chunk * x_chunk, axis=-1, keepdims=True) + NORM_EPS)
    normed = lowered(x_chunk * inverse_chunk)

    def in_parts(four):
        here, there = four[:2], four[2:]
        zero = [jnp.where(first_core, a, b) for a, b in zip(here, there)]
        return zero + [jnp.where(first_core, b, a) for a, b in zip(here, there)]

    def quarters_of(pair, which):
        width = HD + quarter
        lanes_of = [(k * width, k * width + HD) if which == 0 else (k * width + HD, (k + 1) * width) for k in (0, 1)]
        return [one[:, low:high] for one in pair for low, high in lanes_of]

    def filled(four, which):
        pads = ((0, 0), (0, quarter)) if which == 0 else ((0, 0), (HD, 0))
        wide = [jnp.pad(one, pads) for one in four]
        return [jnp.concatenate(wide[:2], axis=-1), jnp.concatenate(wide[2:], axis=-1)]

    def project():
        cubes = [
            lanes.gather_cube(half, order) for half, order in zip(lanes.halves(mine), lanes.orders())
        ]
        here = placed(own, cubes, False).reshape(D, 2 * (HD + quarter))
        weights = [here, lanes.swap(here)]
        line = lanes.z ^ jnp.arange(4, dtype=jnp.int32)
        ring = lanes.p ^ jnp.arange(n_p, dtype=jnp.int32)
        cores = h ^ jnp.arange(2, dtype=jnp.int32)
        within = jnp.arange(SUB, dtype=jnp.int32)
        key_blocks = 2 * (line[None, None, :] * n_p + ring[None, :, None]) + cores[:, None, None]
        key_positions = (block_offsets[key_blocks.reshape(-1)][:, None] + within).reshape(-1)
        cosine, sine = rotary_tables(key_positions[:chunk])
        projected = in_parts(quarters_of([product(normed, weight) for weight in weights], 0))
        query_heads = lowered(
            jnp.concatenate([rotate(one, cosine, sine) for one in projected[:SHARE]])
        )
        key_here = lowered(rotate(projected[2], cosine, sine))
        cubes = [
            lanes.gather_cube(one.reshape(4, SUB, HD), order)
            for one, order in zip((key_here, lowered(projected[3])), lanes.orders())
        ]
        plane = placed(jnp.zeros_like(own), cubes, True).reshape(n_p * chunk, 2 * HD)
        pair_all = jnp.concatenate([plane, lanes.swap(plane)])
        return weights, cosine, sine, key_positions, query_heads, pair_all

    weights, cosine, sine, key_positions, query_heads, pair_all = stage(project)
    feed = turned(own, after(feed, pair_all), 0)
    dy_all = lax.all_gather(after(dy_line, feed[0]), "p", axis=0, tiled=True)
    query_heads = after(query_heads, *feed)
    feed = [feed[0]] + [lanes.over_p(feed[e], e) for e in range(1, n_p)]

    def attention_forward():
        keys_all, values_all = pair_all[:, :HD], pair_all[:, HD:]
        my_positions = key_positions[:chunk]
        allowed = key_positions[None, :] <= my_positions[:, None]
        allowed = jnp.concatenate([allowed] * SHARE)
        scores = contract(query_heads, keys_all, 1, 1) * scaling
        scores = jnp.where(allowed, scores, MASKED_SCORE)
        largest = jnp.max(scores, axis=-1, keepdims=True)
        expos = jnp.exp(scores - largest)
        probs = expos / jnp.sum(expos, axis=-1, keepdims=True)
        attended = lowered(product(lowered(probs), values_all))
        mixed = jnp.concatenate([attended[:chunk], attended[chunk:]], axis=-1)
        quarters = in_parts([mixed[:, k * quarter : (k + 1) * quarter] for k in range(4)])
        resid_part = sum(
            contract(part, weight, 1, 1) for part, weight in zip(filled(quarters, 1), weights)
        )
        return probs, mixed, lowered(resid_part).reshape(4, SUB, D)

    probs, mixed, resid_part = stage(attention_forward)
    def second_norm():
        resid = x_own.astype(F32) + lanes.scatter_z(resid_part, True)
        inverse_two = lax.rsqrt(jnp.mean(resid * resid, axis=-1, keepdims=True) + NORM_EPS)
        normed_two = lowered(resid * inverse_two)
        return resid, inverse_two, lanes.absolute(lanes.gather_z(normed_two), lanes.z)

    resid, inverse_two, stacked = stage(second_norm)
    feed = after(feed, stacked)
    if fits:
        here = feed_weights(own, feed)
    else:
        here = joined(own, feed, 1).reshape(D, 3 * units)
        here = [here[:, : 2 * units], here[:, 2 * units :]]

    def gather_normed():
        there = [lanes.swap(weight) for weight in here]
        cubes = [
            lanes.gather_cube(half, order)
            for half, order in zip(lanes.halves(stacked), lanes.orders())
        ]
        normed_all = placed(own, cubes, True).reshape(n_ctx * SUB, D)
        return normed_all, there

    normed_all, there = stage(gather_normed)
    gate_up_weights, down_weights = zip(here, there)

    def feed_forward():
        d_gate_up, hidden = [], []
        for gate_up_weight, down_weight in zip(gate_up_weights, down_weights):
            incoming = product(dy_all, down_weight)
            gate_up = product(normed_all, gate_up_weight)
            gate_values, up_values = gate_up[:, :units], gate_up[:, units:]
            sigmoid_gate = jax.nn.sigmoid(gate_values)
            activated = gate_values * sigmoid_gate
            hidden.append(lowered(activated * up_values))
            slope = sigmoid_gate * (1.0 + gate_values * (1.0 - sigmoid_gate))
            d_gate = lowered(incoming * up_values * slope)
            d_gate_up.append(jnp.concatenate([d_gate, lowered(incoming * activated)], axis=-1))
        cubes = []
        for part in (slice(0, D // 2), slice(D // 2, D)):
            partial = sum(
                contract(one, weight[part], 1, 1)
                for one, weight in zip(d_gate_up, gate_up_weights)
            )
            cubes.append(partial.reshape(lanes.cube + [4, SUB, D // 2]))
        d_normed_parts = [
            lanes.scatter_p(cube, order, False) for cube, order in zip(cubes, lanes.orders())
        ]
        return hidden, d_gate_up, jnp.concatenate(d_normed_parts, axis=-1)

    if fits:
        outs = feed_forward_blocks(own, normed_all, dy_all, gate_up_weights, down_weights)
        hidden, d_gate_up = [outs[0][:, :units], outs[0][:, units:]], list(outs[1:3])
        stays, goes = [outs[3], outs[5]], [outs[4], outs[6]]
        comes = [lanes.over_p(goes[b], 1 << b) for b in (0, 1)]
    else:
        hidden, d_gate_up, d_normed_part = stage(feed_forward)
        comes = []

    def feed_gradients(core):
        return [
            lowered(contract(normed_all, d_gate_up[core], 0, 0)),
            lowered(contract(dy_all, hidden[core], 0, 0)),
        ]

    def feed_gradients_both():
        came = [lanes.swap(one) for one in feed_gradients(1)]
        out_part = sum(contract(one, weight, 1, 1) for one, weight in zip(hidden, down_weights))
        return came, feed_gradients(0), lowered(out_part)

    came, home, out_part = stage(feed_gradients_both)
    if fits:
        comes = after(comes, out_part)
        totals = [stay.astype(F32) + one.astype(F32) for stay, one in zip(stays, comes)]
        goes = [lowered(pick(totals[b], 1 - lanes.bit(1 - b), 0)) for b in (0, 1)]
        stays = [pick(totals[b], lanes.bit(1 - b), 0) for b in (0, 1)]
        comes = [lanes.over_p(goes[b], 1 << (1 - b)) for b in (0, 1)]
        came = add_split(own, n_p, after(home, *goes), came)
        comes = after(comes, came[0])
        d_normed_part = jnp.concatenate(
            [stay + one.astype(F32) for stay, one in zip(stays, comes)], axis=-1
        ).reshape(4, SUB, D)
    else:
        home, came = [jnp.concatenate(two, axis=-1).astype(F32) for two in (home, came)]
        came = split_rows(own, lowered(home + came).reshape(4, n_p, rows, 3 * units), 1)
    came = [came[0]] + [lanes.over_p(came[e], e) for e in range(1, n_p)]
    out_line = lax.psum_scatter(
        after(out_part, d_normed_part), "p", scatter_dimension=0, tiled=True
    )

    def second_norm_backward():
        d_normed_two = lanes.scatter_z(d_normed_part, False)
        d_resid = dy_own.astype(F32) + norm_back(resid, inverse_two, d_normed_two)
        return d_resid, jnp.concatenate(lanes.gather_z(lowered(d_resid)))

    d_resid, d_resid_chunk = stage(second_norm_backward)
    came = turned(own, after(came, d_resid_chunk), 1)
    d_resid_chunk = after(d_resid_chunk, *came)
    came = [came[0]] + [lanes.over_z(came[step], step) for step in (1, 2, 3)]

    def attention_backward():
        d_mixed = [product(d_resid_chunk, weight) for weight in weights]
        d_mixed = in_parts(quarters_of(d_mixed, 1))
        d_mixed = lowered(jnp.concatenate(d_mixed, axis=-1))
        d_attended = jnp.concatenate([d_mixed[:, :HD], d_mixed[:, HD:]])
        keys_all, values_all = pair_all[:, :HD], pair_all[:, HD:]
        d_probs = contract(d_attended, values_all, 1, 1)
        delta = jnp.sum(probs * d_probs, axis=-1, keepdims=True)
        d_scores = lowered(probs * (d_probs - delta))
        d_query_heads = product(d_scores, keys_all) * scaling
        d_key_all = contract(d_scores, query_heads, 0, 0) * scaling
        d_value_all = contract(lowered(probs), d_attended, 0, 0)
        middle = n_p * chunk
        d_pair = [d_key_all, d_value_all]
        cames = [lanes.swap(lowered(one[middle:])) for one in d_pair]
        d_pair_keeps = [lowered(one[:middle]) for one in d_pair]

        def summed_over_group(place, lead, keeps, cames):
            halves = add_halved(place, lead, n_p, keeps, cames, lanes.orders())
            done = []
            for (stay, goes), order in zip(halves, lanes.orders()):
                have = list(range(lanes.bits))
                for b, following in zip(order, order[1:] + [None]):
                    other = lanes.over_p(goes, 1 << b)
                    have.remove(b)
                    if following is None:
                        stay = lowered(stay.astype(F32) + other.astype(F32))
                    else:
                        stay, goes = sum_halved(place, stay, other, have.index(following), following)
                done.append(stay.reshape(lead * stay.shape[2], stay.shape[-1]))
            return done

        keeps = [[keep] for keep in d_pair_keeps]
        d_key, d_value = [
            one.astype(F32)
            for one in summed_over_group(jnp.zeros_like(own), 1, keeps, cames)
        ]
        d_key = lowered(rotate(d_key, cosine, -sine))
        d_value = lowered(d_value)
        d_query = [
            lowered(rotate(one, cosine, -sine))
            for one in (d_query_heads[:chunk], d_query_heads[chunk:])
        ]
        lefts = (normed, d_resid_chunk)
        rights = [d_query[0], mixed[:, :quarter], d_query[1], mixed[:, quarter : 2 * quarter]]
        others = [d_key, mixed[:, 2 * quarter : 3 * quarter], d_value, mixed[:, 3 * quarter :]]
        keep, away = [], []
        for k in range(4):
            mine, theirs = jnp.where(first_core, rights[k], others[k]), jnp.where(
                first_core, others[k], rights[k]
            )
            keep.append(lowered(contract(lefts[k % 2], mine, 0, 0)))
            away.append(lowered(contract(lefts[k % 2], theirs, 0, 0)))
        cames = [
            lanes.swap(jnp.concatenate(away[at : at + 2], axis=-1)) for at in (0, 2)
        ]
        summed = summed_over_group(own, 4, [keep[:2], keep[2:]], cames)
        in_turn = [half[:, :HD] for half in summed] + [half[:, HD:] for half in summed]
        in_turn = jnp.concatenate(in_turn, axis=-1).reshape(4, rows, 3 * QW // 2)
        return in_turn, in_parts(d_query + [d_key, d_value])

    in_turn, d_projected = stage(attention_backward)
    homeward = lanes.send_z(in_turn)

    def beside_home():
        joined_came = joined(own, came, 0).reshape(n_ctx, rows, 3 * units)
        shares = squares_of_feed(gain_two, w_gate, w_up, joined_came) if fits else in_turn
        d_normed_part = sum(
            contract(part, weight, 1, 1) for part, weight in zip(filled(d_projected, 0), weights)
        ).reshape(4, SUB, D)
        parts = [
            jnp.concatenate(
                [d_normed_part[s], pick(out_line.reshape(4, SUB, D), lanes.z ^ s, 0).astype(F32)]
            )
            for s in range(4)
        ]
        near = lowered(jnp.stack([parts[3], parts[1]]))
        return joined_came, shares, parts[0], parts[2], near

    came, shares, line_own, line_far, line_near = stage(beside_home)
    part_zero, part_one = lanes.group_home(lanes.join_z(after(homeward, line_near)))
    line_near = after(line_near, part_zero)
    near = lanes.over_z(line_near, 1)
    masters = (w_query, w_key, w_value, w_out, w_gate, w_up, w_down)
    if fits:
        shared = squares_of_attention(gain_one, masters, part_zero, part_one, shares)
    else:

        def of_owner(k):
            part = came[:, :, k * units : (k + 1) * units].transpose(1, 0, 2)
            return part.reshape(rows, n_ctx * units).astype(F32)

        inner_gate, inner_up, grad_down = of_owner(0), of_owner(1), of_owner(2).T
        grad_out = jnp.concatenate([part_zero[:, :, QW:], part_one[:, :, QW:]], axis=-1)
        grad_out = grad_out.astype(F32).transpose(0, 2, 1).reshape(2 * QW, rows)
        inner_query = part_zero[:, :, :QW].astype(F32).transpose(1, 0, 2).reshape(rows, 2 * QW)
        inner_pair = part_one[:, :, :QW].astype(F32).transpose(1, 0, 2)
        inner_key = inner_pair[:, :, :HD].reshape(rows, 2 * HD)
        inner_value = inner_pair[:, :, HD:].reshape(rows, 2 * HD)

        def weighed(matrix, inner):
            return jnp.sum(lowered(matrix).astype(F32) * inner, axis=1)

        first = weighed(w_query, inner_query) + weighed(w_key, inner_key)
        grad_gains = jnp.stack(
            [
                first + weighed(w_value, inner_value),
                weighed(w_gate, inner_gate) + weighed(w_up, inner_up),
            ]
        )
        gradients = (
            inner_query * gain_one,
            inner_key * gain_one,
            inner_value * gain_one,
            grad_out,
            inner_gate * gain_two,
            inner_up * gain_two,
            grad_down,
        )
        squares = sum(jnp.sum(gradient * gradient) for gradient in gradients)
        shared = jnp.concatenate([grad_gains, jnp.broadcast_to(squares, (6, rows))])
    shared = shared + lanes.swap(shared)
    grad_gains = shared[:2]
    squares = jnp.broadcast_to(shared[2:3, :1] + jnp.sum(grad_gains * grad_gains), (8, 128))
    for b in range(lanes.bits):
        squares = squares + lanes.over_p(squares, 1 << b)
    for s in (1, 2):
        squares = squares + lanes.over_z(squares, s)
    near = after(near, squares)
    far = lanes.over_z(lowered(line_far + near[0].astype(F32)), 2)
    grad_norm = jnp.sqrt(squares[0, 0])
    factor = CLIP_NORM / jnp.maximum(grad_norm, CLIP_NORM)
    wo_fan = min(HQ * HD, max(2, 131072 // total_rows))
    rate_in = 2.0 / math.sqrt(D)
    step_rates = (
        rate_in,
        rate_in,
        rate_in,
        2.0 / math.sqrt(wo_fan),
        rate_in,
        rate_in,
        2.0 / math.sqrt(FF),
    )
    if fits:
        new_weights, copies, moment_first, moment_second = adamw_blocks(
            step_rates,
            factor,
            gain_one,
            gain_two,
            masters,
            (moment_one, moment_two),
            part_zero,
            part_one,
            came,
        )
    else:
        new_weights = []
        firsts = []
        seconds = []
        offset = 0
        for index_now in range(7):
            weight = masters[index_now]
            length = weight.size
            first_moment = moment_one[offset : offset + length].reshape(weight.shape)
            second_moment = moment_two[offset : offset + length].reshape(weight.shape)
            updated, first_new, second_new = adamw_step(
                weight,
                factor * gradients[index_now],
                first_moment,
                second_moment,
                step_rates[index_now],
                WEIGHT_DECAY,
            )
            new_weights.append(updated)
            firsts.append(first_new.reshape(-1))
            seconds.append(second_new.reshape(-1))
            offset = offset + length
        copies = [lowered(weight) for weight in new_weights]
        moment_first, moment_second = jnp.concatenate(firsts), jnp.concatenate(seconds)
    line_sums = line_own + near[1].astype(F32) + after(far, new_weights[0]).astype(F32)
    d_normed, out_sum = line_sums[:SUB], line_sums[SUB:]
    x_float = x_own.astype(F32)
    inverse_own = lax.rsqrt(jnp.mean(x_float * x_float, axis=-1, keepdims=True) + NORM_EPS)
    input_grad = lowered(d_resid + norm_back(x_float, inverse_own, d_normed))
    input_grad, layer_out = both_cores(input_grad), both_cores(lowered(resid + out_sum))
    new_gains, gain_first, gain_second = adamw_step(
        gains, factor * grad_gains, gain_moment_one, gain_moment_two, GAIN_RATE, 0.0
    )
    return (
        layer_out,
        input_grad,
        grad_norm,
        *new_weights,
        new_gains,
        *copies,
        lowered(new_gains),
        moment_first,
        moment_second,
        gain_first,
        gain_second,
    )


def solution(mesh):
    n_ctx, n_head = mesh.devices.shape
    lanes_mesh = Mesh(mesh.devices.reshape(4, n_ctx // 4, n_head), ("z", "p", "head"))
    ctx = ("z", "p")
    rows = P(ctx, None)
    wide = P(ctx, "head")
    tall = P("head", ctx)
    flat = P(("z", "p", "head"))
    gain = P(None, ctx)
    weights = (wide, wide, wide, tall, wide, wide, tall, gain)
    return jax.shard_map(
        local,
        mesh=lanes_mesh,
        in_specs=(rows, P(), rows, *weights, flat, flat, gain, gain),
        out_specs=(rows, rows, P(), *weights, *weights, flat, flat, gain, gain),
        check_vma=False,
    )
```

```python
import math

import jax
import jax.numpy as jnp
from jax import lax
from jax.experimental import pallas as pl
from jax.experimental.pallas import tpu as pltpu
from jax.sharding import Mesh
from jax.sharding import PartitionSpec as P

D = 2048
HQ = 8
KV = 4
HD = 256
FF = 8192
SUB = 64
STEP = 10
SHARE = HQ // KV
QW = SHARE * HD


NORM_EPS = 1e-06
ROPE_BASE = 1000042.0
BETA_ONE = 0.9
BETA_TWO = 0.95
ADAM_EPS = 1e-08
WEIGHT_DECAY = 0.1
GAIN_RATE = 0.5
CLIP_NORM = 1.0
MASKED_SCORE = -1e30
BF = jnp.bfloat16
F32 = jnp.float32
SWAP = [(0, 1), (1, 0)]


def lowered(array_in):
    return array_in.astype(BF)


def product(left, right):
    return jnp.dot(left, right, preferred_element_type=F32)


def contract(left, right, left_dim, right_dim):
    return lax.dot_general(
        left, right, (((left_dim,), (right_dim,)), ((), ())), preferred_element_type=F32
    )


def rotary_tables(positions):
    frequency = ROPE_BASE ** (-jnp.arange(0, HD, 2, dtype=F32) / HD)
    angles = positions.astype(F32)[:, None] * frequency[None, :]
    return (jnp.cos(angles), jnp.sin(angles))


def rotate(one_head, cosine, sine):
    half_size = HD // 2
    first_half = one_head[:, :half_size]
    second_half = one_head[:, half_size:]
    return jnp.concatenate(
        [first_half * cosine - second_half * sine, second_half * cosine + first_half * sine],
        axis=-1,
    )


def adamw_step(weight, gradient, first_moment, second_moment, step_rate, decay_rate):
    first_new = BETA_ONE * first_moment + (1.0 - BETA_ONE) * gradient
    second_new = BETA_TWO * second_moment + (1.0 - BETA_TWO) * gradient * gradient
    ratio = (
        first_new
        / (1.0 - BETA_ONE**STEP)
        / (jnp.sqrt(second_new / (1.0 - BETA_TWO**STEP)) + ADAM_EPS)
    )
    return (weight - step_rate * (ratio + decay_rate * weight), first_new, second_new)


def pick(array_in, index, axis):
    return lax.dynamic_index_in_dim(array_in, index, axis, keepdims=False)


def after(arrays, *others):
    listed = arrays if isinstance(arrays, list) else [arrays]
    if not others:
        return arrays
    anywhere = pl.BlockSpec(memory_space=pl.ANY)
    out = pl.pallas_call(
        lambda *refs: None,
        in_specs=[anywhere] * (len(listed) + len(others)),
        out_specs=[anywhere] * len(listed),
        out_shape=[jax.ShapeDtypeStruct(array.shape, array.dtype) for array in listed],
        input_output_aliases={k: k for k in range(len(listed))},
        name="after",
    )(*listed, *others)
    return list(out) if isinstance(arrays, list) else out[0]


class Lanes:
    def __init__(self):
        self.n_p = lax.axis_size("p")
        self.z = lax.axis_index("z")
        self.p = lax.axis_index("p")
        self.h = lax.axis_index("head")
        self.bits = self.n_p.bit_length() - 1
        self.cube = [2] * self.bits

    def swap(self, array_in):
        return lax.ppermute(array_in, "head", SWAP)

    def over_z(self, array_in, step):
        return lax.ppermute(array_in, "z", [(i, i ^ step) for i in range(4)])

    def over_p(self, array_in, step):
        return lax.ppermute(array_in, "p", [(i, i ^ step) for i in range(self.n_p)])

    def orders(self):
        return list(range(self.bits)), list(range(self.bits))[::-1]

    def bit(self, b):
        return (self.p >> b) & 1

    def absolute(self, pieces, index, axis=0):
        for b in range(len(pieces).bit_length() - 1):
            odd = ((index >> b) & 1) == 1
            pieces = [jnp.where(odd, pieces[j ^ (1 << b)], pieces[j]) for j in range(len(pieces))]
        return jnp.stack(pieces, axis)

    def gather_z(self, array_in):
        one, two = self.over_z(array_in, 1), self.over_z(array_in, 2)
        return [array_in, one, two, self.over_z(two, 1)]

    def send_z(self, array_in, axis=0):
        pieces = [pick(array_in, self.z, axis)]
        for s in (1, 2, 3):
            pieces.append(self.over_z(pick(array_in, self.z ^ s, axis), s))
        return pieces

    def join_z(self, pieces, axis=0):
        return self.absolute(pieces, self.z, axis)

    def scatter_z(self, array_in, relative):
        parts = [pick(array_in, s if relative else self.z ^ s, 0).astype(F32) for s in range(4)]
        near = self.over_z(lowered(jnp.stack([parts[3], parts[1]])), 1)
        far = self.over_z(lowered(parts[2] + near[0].astype(F32)), 2)
        return parts[0] + near[1].astype(F32) + far.astype(F32)

    def gather_p(self, array_in, order, relative, lead=0):
        have = []
        for b in order:
            other = self.over_p(array_in, 1 << b)
            axis = lead + sum(1 for x in have if x > b)
            mine, other = jnp.expand_dims(array_in, axis), jnp.expand_dims(other, axis)
            array_in = jnp.concatenate([mine, other], axis)
            if not relative:
                array_in = jnp.where(
                    self.bit(b) == 1, jnp.concatenate([other, mine], axis), array_in
                )
            have.append(b)
        return array_in

    def gather_cube(self, array_in, order):
        held = [(array_in[None], [0])]
        for b in order:
            numbers = [j for _, part in held for j in part]
            whole = jnp.concatenate([array for array, _ in held]) if len(held) > 1 else held[0][0]
            held.append((self.over_p(whole, 1 << b), [j ^ (1 << b) for j in numbers]))
        return held

    def scatter_p(self, array_in, order, relative, lead=0):
        have = list(range(self.bits))
        for b in order:
            axis = lead + sum(1 for x in have if x > b)
            bit = 0 if relative else self.bit(b)
            keep, send = pick(array_in, bit, axis), pick(array_in, 1 - bit, axis)
            array_in = keep.astype(F32) + self.over_p(lowered(send), 1 << b).astype(F32)
            have.remove(b)
        return array_in

    def halves(self, array_in):
        middle = array_in.shape[-1] // 2
        return array_in[..., :middle], array_in[..., middle:]

    def group_blocks(self, part_zero, part_one):
        first = self.h == 0
        keep = jnp.where(first, part_zero, part_one).transpose(1, 0, 2)
        other = self.swap(jnp.where(first, part_one, part_zero).transpose(1, 0, 2))
        return jnp.where(
            first, jnp.concatenate([keep, other]), jnp.concatenate([other, keep])
        )

    def group_home(self, blocks):
        first = self.h == 0
        own = jnp.where(first, blocks[:2], blocks[2:])
        other = self.swap(jnp.where(first, blocks[2:], blocks[:2]))
        return jnp.where(first, own, other), jnp.where(first, other, own)


def moved(own, inputs, shapes, plan):
    def kernel(own_ref, *refs):
        ins, outs = refs[: len(inputs)], refs[len(inputs) :]
        for source, target in plan(ins, outs, own_ref[0], own_ref[1]):
            if isinstance(source, tuple):
                total = sum(one[...].astype(F32) for one in source)
                target[...] = total.astype(target.dtype)
            else:
                target[...] = source[...]

    vmem = pl.BlockSpec(memory_space=pltpu.VMEM)
    return pl.pallas_call(
        kernel,
        in_specs=[pl.BlockSpec(memory_space=pltpu.SMEM)] + [vmem] * len(inputs),
        out_specs=[vmem] * len(shapes),
        out_shape=[jax.ShapeDtypeStruct(shape, inputs[0].dtype) for shape in shapes],
        compiler_params=pltpu.CompilerParams(vmem_limit_bytes=60 * 1024 * 1024),
        name="moved",
    )(own, *inputs)


def split_rows(own, array_in, which):
    count = array_in.shape[which]
    shape = array_in.shape[:which] + array_in.shape[which + 1 :]

    def plan(ins, outs, z, p):
        if which == 0:
            return [(ins[0].at[z ^ j], outs[j]) for j in range(count)]
        return [(ins[0].at[:, p ^ j], outs[j]) for j in range(count)]

    return moved(own, [array_in], [shape] * count, plan)


def joined(own, pieces, which):
    count = len(pieces)
    shape = pieces[0].shape
    shape = shape[:which] + (count,) + shape[which:]

    def plan(ins, outs, z, p):
        if which == 0:
            return [(ins[j], outs[0].at[z ^ j]) for j in range(count)]
        return [(ins[j], outs[0].at[:, p ^ j]) for j in range(count)]

    return moved(own, pieces, [shape], plan)[0]


def turned(own, pieces, which):
    count = len(pieces)
    other = pieces[0].shape[0]
    shape = (count,) + pieces[0].shape[1:]

    def plan(ins, outs, z, p):
        mine, theirs = (z, p) if which == 0 else (p, z)
        return [
            (ins[i].at[theirs ^ j], outs[j].at[mine ^ i])
            for i in range(count)
            for j in range(other)
        ]

    return moved(own, pieces, [shape] * other, plan)


def placed(own, halves, in_front):
    arrays = [array for half in halves for array, _ in half]
    n_p = sum(len(numbers) for _, numbers in halves[0])
    block = halves[0][0][0].shape[1:]
    widths = [half[0][0].shape[-1] for half in halves]
    lead = (n_p, block[0]) if in_front else (block[0], n_p)
    shapes = [lead + block[1:-1] + (sum(widths),)]

    def plan(ins, outs, z, p):
        pairs, at = [], 0
        for k, half in enumerate(halves):
            lanes = pl.ds(sum(widths[:k]), widths[k])
            for _, numbers in half:
                for i, j in enumerate(numbers):
                    if in_front:
                        target = outs[0].at[p ^ j, :, :, lanes]
                    else:
                        target = outs[0].at[:, p ^ j, :, lanes]
                    pairs.append((ins[at].at[i], target))
                at = at + 1
        return pairs

    return moved(own, arrays, shapes, plan)[0]


def add_split(own, n_p, home, came):
    rows = home[0].shape[0] // (4 * n_p)

    def kernel(own_ref, gate_up_ref, down_ref, gate_up_came, down_came, *outs):
        sides = (
            (gate_up_ref, gate_up_came, pl.ds(0, 512)),
            (down_ref, down_came, pl.ds(512, 256)),
        )
        for j in range(n_p):
            for z in range(4):
                at = pl.multiple_of((z * n_p + (own_ref[1] ^ j)) * rows, rows)
                at = pl.ds(at, rows)
                for ref, came_ref, lanes in sides:
                    total = ref[at, :].astype(F32) + came_ref[at, :].astype(F32)
                    outs[j][z, :, lanes] = lowered(total)

    vmem = pl.BlockSpec(memory_space=pltpu.VMEM)
    return pl.pallas_call(
        kernel,
        in_specs=[pl.BlockSpec(memory_space=pltpu.SMEM)] + [vmem] * 4,
        out_specs=[vmem] * n_p,
        out_shape=[jax.ShapeDtypeStruct((4, rows, 768), BF)] * n_p,
        compiler_params=pltpu.CompilerParams(vmem_limit_bytes=60 * 1024 * 1024),
        name="add_split",
    )(own, *home, *came)


def half_numbers(count, at, bit):
    return [((k >> at) << (at + 1)) | (k & ((1 << at) - 1)) | (bit << at) for k in range(count // 2)]


def add_halved(own, lead, n_p, keeps, cames, orders):
    rows = cames[0].shape[0] // (lead * n_p)
    counts = [len(keep) for keep in keeps]
    shape = (lead, n_p // 2, rows, cames[0].shape[1])

    def kernel(own_ref, *refs):
        outs = refs[-4:]
        at = 0
        for half, order in enumerate(orders):
            parts, came = refs[at : at + counts[half]], refs[at + counts[half]]
            at = at + counts[half] + 1
            bit = (own_ref[1] >> order[0]) & 1
            for target, value in ((outs[2 * half], bit), (outs[2 * half + 1], 1 - bit)):
                for k, number in enumerate(half_numbers(n_p, order[0], value)):
                    for z in range(lead):
                        from_rows = pl.ds(pl.multiple_of((z * n_p + number) * rows, rows), rows)
                        low = 0
                        for part in parts:
                            lanes = pl.ds(low, part.shape[1])
                            low = low + part.shape[1]
                            total = part[from_rows, :].astype(F32)
                            total = total + came[from_rows, lanes].astype(F32)
                            target[z, k, :, lanes] = lowered(total)

    vmem = pl.BlockSpec(memory_space=pltpu.VMEM)
    inputs = [one for keep, came in zip(keeps, cames) for one in [*keep, came]]
    outs = pl.pallas_call(
        kernel,
        in_specs=[pl.BlockSpec(memory_space=pltpu.SMEM)] + [vmem] * len(inputs),
        out_specs=[vmem] * 4,
        out_shape=[jax.ShapeDtypeStruct(shape, BF)] * 4,
        compiler_params=pltpu.CompilerParams(vmem_limit_bytes=60 * 1024 * 1024),
        name="add_halved",
    )(own, *inputs)
    return outs[:2], outs[2:]


def sum_halved(own, stay, came, at, b):
    count = stay.shape[1]
    shape = (stay.shape[0], count // 2) + stay.shape[2:]

    def plan(ins, outs, z, p):
        bit = (p >> b) & 1
        pairs = []
        for target, value in ((outs[0], bit), (outs[1], 1 - bit)):
            for k, number in enumerate(half_numbers(count, at, value)):
                pairs.append(((ins[0].at[:, number], ins[1].at[:, number]), target.at[:, k]))
        return pairs

    return moved(own, [stay, came], [shape] * 2, plan)


def feed_weights(own, pieces):
    count = len(pieces)

    def plan(ins, outs, z, p):
        pairs = []
        for j in range(count):
            pairs.append((ins[j].at[:, :, pl.ds(0, 512)], outs[0].at[:, p ^ j]))
            pairs.append((ins[j].at[:, :, pl.ds(512, 256)], outs[1].at[:, p ^ j]))
        return pairs

    gate_up, down = moved(own, pieces, [(4, count, 128, 512), (4, count, 128, 256)], plan)
    return [gate_up.reshape(D, 512), down.reshape(D, 256)]


def feed_forward_kernel(
    own_ref, normed_ref, dy_ref, here_ref, there_ref, down_here_ref, down_there_ref,
    hidden_ref, d_zero_ref, d_one_ref, stay_zero_ref, goes_zero_ref, stay_one_ref, goes_one_ref,
):
    step = pl.program_id(0)
    normed = normed_ref[...]
    d_normed = None
    dy = dy_ref[...]
    sides = ((down_here_ref, here_ref, d_zero_ref), (down_there_ref, there_ref, d_one_ref))
    for core, (down_ref, weight_ref, d_ref) in enumerate(sides):
        weight = weight_ref[...]
        gate_up = product(normed, weight)
        gate_values, up_values = gate_up[:, :256], gate_up[:, 256:]
        incoming = product(dy, down_ref[...])
        sigmoid_gate = jax.nn.sigmoid(gate_values)
        activated = gate_values * sigmoid_gate
        hidden_ref[:, pl.ds(core * 256, 256)] = lowered(activated * up_values)
        slope = sigmoid_gate * (1.0 + gate_values * (1.0 - sigmoid_gate))
        d_ref[:, pl.ds(0, 256)] = lowered(incoming * up_values * slope)
        d_ref[:, pl.ds(256, 256)] = lowered(incoming * activated)
        partial = contract(d_ref[...], weight, 1, 1)
        d_normed = partial if d_normed is None else d_normed + partial
    d_normed = lowered(d_normed)
    halves = ((0, stay_zero_ref, goes_zero_ref), (1, stay_one_ref, goes_one_ref))
    for b, stay_ref, goes_ref in halves:
        stays = ((step >> b) & 1) == ((own_ref[1] >> b) & 1)
        place = (step >> 1) if b == 0 else (step & 1)
        part = d_normed[:, b * (D // 2) : (b + 1) * (D // 2)]

        @pl.when(stays)
        def _():
            stay_ref[place] = part

        @pl.when(jnp.logical_not(stays))
        def _():
            goes_ref[place] = part


def feed_forward_blocks(own, normed_all, dy_all, gate_up_weights, down_weights):
    quarter = normed_all.shape[0] // 4

    def of_rows(width):
        return pl.BlockSpec((quarter, width), lambda i: (i, 0))

    def whole(*shape):
        return pl.BlockSpec(shape, lambda i: (0,) * len(shape))

    half = (2, quarter, D // 2)
    return pl.pallas_call(
        feed_forward_kernel,
        grid=(4,),
        in_specs=[
            pl.BlockSpec(memory_space=pltpu.SMEM),
            of_rows(D),
            of_rows(D),
            whole(D, 512),
            whole(D, 512),
            whole(D, 256),
            whole(D, 256),
        ],
        out_specs=[of_rows(512), of_rows(512), of_rows(512)] + [whole(*half)] * 4,
        out_shape=[jax.ShapeDtypeStruct((4 * quarter, 512), BF)] * 3
        + [jax.ShapeDtypeStruct(half, BF)] * 4,
        compiler_params=pltpu.CompilerParams(
            dimension_semantics=("arbitrary",), vmem_limit_bytes=60 * 1024 * 1024
        ),
        name="feed_forward",
    )(own, normed_all, dy_all, *gate_up_weights, *down_weights)


def pack_kernel(n_p, own_ref, gain_ref, gate_ref, up_ref, down_ref, *outs):
    gain = jnp.broadcast_to(gain_ref[...], (128, 256))
    for s in range(4):
        for p in range(n_p):
            at = pl.multiple_of(((own_ref[0] ^ s) * n_p + p) * 256, 256)
            outs[s][p, :, pl.ds(0, 256)] = lowered(gate_ref[:, pl.ds(at, 256)] * gain)
            outs[s][p, :, pl.ds(256, 256)] = lowered(up_ref[:, pl.ds(at, 256)] * gain)
            outs[s][p, :, pl.ds(512, 256)] = lowered(down_ref[pl.ds(at, 256), :].T)


def pack_feed(own, gain, w_gate, w_up, w_down, n_p):
    vmem = pl.BlockSpec(memory_space=pltpu.VMEM)
    return pl.pallas_call(
        lambda *refs: pack_kernel(n_p, *refs),
        in_specs=[pl.BlockSpec(memory_space=pltpu.SMEM), vmem, vmem, vmem, vmem],
        out_specs=[vmem] * 4,
        out_shape=[jax.ShapeDtypeStruct((n_p, 128, 768), BF)] * 4,
        compiler_params=pltpu.CompilerParams(vmem_limit_bytes=60 * 1024 * 1024),
        name="pack_feed",
    )(own, gain, w_gate, w_up, w_down)


def squares_body(gain_ref, blocks, plain, base_ref, row, out_ref, squares_ref, along_ref):
    step = pl.program_id(0)
    height = gain_ref.shape[0]
    here = pl.ds(pl.multiple_of(step * height, height), height)

    @pl.when(step == 0)
    def _():
        squares_ref[...] = jnp.zeros_like(squares_ref)

    nothing = jnp.zeros((height, 128), F32)
    scaled, unscaled, along = nothing, nothing, nothing
    for weight, gradient in blocks:
        gradient = gradient.astype(F32)
        scaled = scaled + gradient * gradient
        along = along + lowered(weight).astype(F32) * gradient
    for gradient in plain:
        gradient = gradient.astype(F32)
        unscaled = unscaled + gradient * gradient
    gain = gain_ref[...]
    along_ref[here, :] = along
    squares_ref[...] += scaled * (gain * gain) + unscaled

    @pl.when(step == pl.num_programs(0) - 1)
    def _():
        total = jnp.sum(squares_ref[...], keepdims=True)
        if base_ref is None:
            out_ref[...] = jnp.broadcast_to(total, (8, 128))
        else:
            out_ref[...] = base_ref[...] + total
            out_ref[1:2, :] = base_ref[1:2, :]
        out_ref[row : row + 1, :] = jnp.sum(along_ref[...].T, axis=0, keepdims=True)


def lanes_of(t):
    return pl.ds(t * 128, 128)


def feed_squares_kernel(gain_ref, gate_ref, up_ref, feed_ref, *outs):
    def column(c, t):
        return feed_ref[c, :, lanes_of(t)]

    blocks = [(gate_ref[:, lanes_of(t)], column(t // 2, t % 2)) for t in range(32)]
    blocks += [(up_ref[:, lanes_of(t)], column(t // 2, t % 2 + 2)) for t in range(32)]
    plain = [column(c, t) for c in range(16) for t in (4, 5)]
    squares_body(gain_ref, blocks, plain, None, 1, *outs)


def attention_squares_kernel(
    gain_ref, query_ref, key_ref, value_ref, zero_ref, one_ref, base_ref, *outs
):
    def column(ref, l, t):
        return ref[l, :, lanes_of(t)]

    blocks = [(query_ref[:, lanes_of(t)], column(zero_ref, t // 4, t % 4)) for t in range(8)]
    blocks += [(key_ref[:, lanes_of(t)], column(one_ref, t // 2, t % 2)) for t in range(4)]
    blocks += [(value_ref[:, lanes_of(t)], column(one_ref, t // 2, t % 2 + 2)) for t in range(4)]
    plain = [column(ref, l, t) for ref in (zero_ref, one_ref) for l in (0, 1) for t in (4, 5)]
    squares_body(gain_ref, blocks, plain, base_ref, 0, *outs)


def squares_call(kernel, arrays, height, name):
    def spec(array):
        if array.ndim == 3:
            return pl.BlockSpec((array.shape[0], height, array.shape[2]), lambda i: (0, i, 0))
        if array.shape[0] == 8:
            return pl.BlockSpec((8, 128), lambda i: (0, 0))
        return pl.BlockSpec((height, array.shape[1]), lambda i: (i, 0))

    return pl.pallas_call(
        kernel,
        grid=(128 // height,),
        in_specs=[spec(array) for array in arrays],
        out_specs=pl.BlockSpec((8, 128), lambda i: (0, 0)),
        out_shape=jax.ShapeDtypeStruct((8, 128), F32),
        scratch_shapes=[pltpu.VMEM((height, 128), F32), pltpu.VMEM((128, 128), F32)],
        compiler_params=pltpu.CompilerParams(
            dimension_semantics=("arbitrary",), vmem_limit_bytes=60 * 1024 * 1024
        ),
        name=name,
    )(*arrays)


def squares_of_feed(gain_two, w_gate, w_up, came):
    return squares_call(feed_squares_kernel, [gain_two, w_gate, w_up, came], 16, "feed_squares")


def squares_of_attention(gain_one, masters, part_zero, part_one, shares):
    arrays = [gain_one, *masters[:3], part_zero, part_one, shares]
    return squares_call(attention_squares_kernel, arrays, 64, "attention_squares")


STEP_ROWS = (128, 64, 64, 128, 512, 512, 512)
STEPS = 8


def adamw_kernel(rates, factor_ref, gain_one_ref, gain_two_ref, *refs):
    masters, firsts, seconds = refs[:7], refs[7:14], refs[14:21]
    query_ref, pair_ref, out_zero_ref, out_one_ref, feed_ref, down_ref = refs[21:27]
    new_refs, copy_refs = refs[27:34], refs[34:41]
    first_hbm, second_hbm, first_buf, second_buf, sems = refs[41:]
    step = pl.program_id(0)
    slot = lax.rem(step, 2)
    factor = factor_ref[0, 0]
    offsets = [sum(STEP_ROWS[:k]) for k in range(7)]

    def moves(of_step, of_slot):
        out = []
        for k in range(7):
            base = STEPS * offsets[k]
            for j, (buf, hbm) in enumerate(((first_buf, first_hbm), (second_buf, second_hbm))):
                out.append(
                    pltpu.make_async_copy(
                        buf.at[of_slot, pl.ds(offsets[k], STEP_ROWS[k])],
                        hbm.at[pl.ds(base + of_step * STEP_ROWS[k], STEP_ROWS[k])],
                        sems.at[of_slot, 2 * k + j],
                    )
                )
        return out

    @pl.when(step >= 2)
    def _():
        for move in moves(step - 2, slot):
            move.wait()

    def update(k, rows, lanes, flat, gradient):
        first = BETA_ONE * firsts[k][flat, :] + (1.0 - BETA_ONE) * gradient
        second = BETA_TWO * seconds[k][flat, :] + (1.0 - BETA_TWO) * gradient * gradient
        ratio = first / (jnp.sqrt(second * (1.0 / (1.0 - BETA_TWO**STEP))) + ADAM_EPS)
        weight = masters[k][rows, lanes]
        weight = weight * (1.0 - rates[k] * WEIGHT_DECAY) - ratio * (
            rates[k] / (1.0 - BETA_ONE**STEP)
        )
        new_refs[k][rows, lanes] = weight
        copy_refs[k][rows, lanes] = lowered(weight)
        return first, second

    def wide(k, gradient_of, scale):
        width = masters[k].shape[1] // 128
        for t in range(width):
            flat = pl.ds(t, 16, stride=width)
            first, second = update(
                k, slice(None), pl.ds(t * 128, 128), flat, gradient_of(t).astype(F32) * scale
            )
            store = pl.ds(offsets[k] + t, 16, stride=width)
            first_buf.at[slot][store, :] = first
            second_buf.at[slot][store, :] = second

    scale_one = jnp.broadcast_to(gain_one_ref[...] * factor, (16, 128))
    scale_two = jnp.broadcast_to(gain_two_ref[...] * factor, (16, 128))
    wide(0, lambda t: query_ref[t // 4, :, pl.ds(t % 4 * 128, 128)], scale_one)
    wide(1, lambda t: pair_ref[t // 2, :, pl.ds(t % 2 * 128, 128)], scale_one)
    wide(2, lambda t: pair_ref[t // 2, :, pl.ds(t % 2 * 128 + HD, 128)], scale_one)
    wide(4, lambda t: feed_ref[t // 2, :, pl.ds(t % 2 * 128, 128)], scale_two)
    wide(5, lambda t: feed_ref[t // 2, :, pl.ds(t % 2 * 128 + 256, 128)], scale_two)

    def tall(k, at, gradient):
        rows = pl.ds(at, 128)
        first, second = update(k, rows, slice(None), rows, gradient.astype(F32).T * factor)
        store = pl.ds(offsets[k] + at, 128)
        first_buf.at[slot][store, :] = first
        second_buf.at[slot][store, :] = second

    part = lax.rem(step // 2, 2) == 0
    tall(3, 0, jnp.where(part, out_zero_ref[0].astype(F32), out_one_ref[0].astype(F32)))
    for c in range(2):
        for t in range(2):
            tall(6, c * 256 + t * 128, down_ref[c, :, pl.ds(t * 128, 128)])

    for move in moves(step, slot):
        move.start()

    @pl.when(step == STEPS - 1)
    def _():
        for move in moves(step - 1, 1 - slot):
            move.wait()
        for move in moves(step, slot):
            move.wait()


def adamw_blocks(rates, factor, gain_one, gain_two, masters, moments, part_zero, part_one, came):
    shapes = [weight.shape for weight in masters]
    tables = [moment.reshape(-1, 128) for moment in moments]
    weight_specs = [
        pl.BlockSpec((shape[0] // STEPS, shape[1]), lambda i: (i, 0)) for shape in shapes
    ]
    starts = [sum(STEP_ROWS[:k]) * STEPS // STEP_ROWS[k] for k in range(7)]
    moment_specs = [
        pl.BlockSpec((STEP_ROWS[k], 128), lambda i, start=starts[k]: (start + i, 0))
        for k in range(7)
    ]
    gain_spec = pl.BlockSpec((16, 1), lambda i: (i, 0))
    rows_spec = pl.BlockSpec((2, 16, 2 * HD), lambda i: (0, i, 0))
    out_spec = pl.BlockSpec((1, 128, 128), lambda i: (i // 4, 0, 4 + i % 2))
    grad_specs = [
        rows_spec,
        rows_spec,
        out_spec,
        out_spec,
        pl.BlockSpec((16, 16, 512), lambda i: (0, i, 0)),
        pl.BlockSpec((2, 128, 256), lambda i: (i, 0, 2)),
    ]
    anywhere = pl.BlockSpec(memory_space=pl.ANY)
    outs = pl.pallas_call(
        lambda *refs: adamw_kernel(rates, *refs),
        grid=(STEPS,),
        in_specs=[
            pl.BlockSpec(memory_space=pltpu.SMEM),
            gain_spec,
            gain_spec,
            *weight_specs,
            *moment_specs,
            *moment_specs,
            *grad_specs,
        ],
        out_specs=[*weight_specs, *weight_specs, anywhere, anywhere],
        out_shape=[
            *[jax.ShapeDtypeStruct(shape, F32) for shape in shapes],
            *[jax.ShapeDtypeStruct(shape, BF) for shape in shapes],
            *[jax.ShapeDtypeStruct(table.shape, F32) for table in tables],
        ],
        scratch_shapes=[
            pltpu.VMEM((2, sum(STEP_ROWS), 128), F32),
            pltpu.VMEM((2, sum(STEP_ROWS), 128), F32),
            pltpu.SemaphoreType.DMA((2, 14)),
        ],
        compiler_params=pltpu.CompilerParams(
            dimension_semantics=("arbitrary",), vmem_limit_bytes=60 * 1024 * 1024
        ),
        name="adamw",
    )(
        factor.reshape(1, 1),
        gain_one,
        gain_two,
        *masters,
        *[tables[0]] * 7,
        *[tables[1]] * 7,
        part_zero,
        part_one,
        part_zero,
        part_one,
        came,
        came,
    )
    return outs[:7], outs[7:14], outs[14].reshape(-1), outs[15].reshape(-1)


def local(
    tokens,
    block_offsets,
    cotangent,
    w_query,
    w_key,
    w_value,
    w_out,
    w_gate,
    w_up,
    w_down,
    gains,
    moment_one,
    moment_two,
    gain_moment_one,
    gain_moment_two,
):
    lanes = Lanes()
    n_p, h = lanes.n_p, lanes.h
    n_ctx = 4 * n_p
    total_rows = n_ctx * 2 * SUB
    rows = D // n_ctx
    units = FF // (2 * n_ctx)
    chunk = 4 * SUB
    scaling = 1.0 / math.sqrt(HD)
    first_core = h == 0
    gain_low = lowered(gains).astype(F32)
    gain_one, gain_two = gain_low[0][:, None], gain_low[1][:, None]
    in_order = block_offsets[0] >= 0
    fits = rows == 128 and n_p == 4
    own = jnp.stack([lanes.z, lanes.p]).astype(jnp.int32)

    def stage(body):
        shapes = jax.eval_shape(body)
        return lax.cond(
            in_order, body, lambda: jax.tree.map(lambda a: jnp.zeros(a.shape, a.dtype), shapes)
        )

    def both_cores(own):
        other = lanes.swap(own)
        return jnp.where(
            first_core, jnp.concatenate([own, other]), jnp.concatenate([other, own])
        )

    def norm_back(inputs, inverse, incoming):
        inner = jnp.mean(incoming * inputs, axis=-1, keepdims=True)
        return inverse * incoming - inputs * (inverse * inverse * inverse * inner)

    x_own = lax.dynamic_slice_in_dim(tokens, h * SUB, SUB)
    dy_own = lax.dynamic_slice_in_dim(cotangent, h * SUB, SUB)

    query_part = lowered((w_query * gain_one).reshape(rows, 2, QW))
    key_part = lowered((w_key * gain_one).reshape(rows, 2, HD))
    value_part = lowered((w_value * gain_one).reshape(rows, 2, HD))
    out_part = lowered(w_out).T.reshape(rows, 2, QW)
    quarter = QW // 4
    out_parts = [out_part[:, :, k * quarter : (k + 1) * quarter] for k in range(4)]
    blocks = lanes.group_blocks(
        jnp.concatenate(
            [query_part[:, :, :HD], out_parts[0], query_part[:, :, HD:], out_parts[1]], axis=-1
        ),
        jnp.concatenate([key_part, out_parts[2], value_part, out_parts[3]], axis=-1),
    )
    split = rows * 3 * QW // 2 // SUB
    mine = []
    for step in range(4):
        block = pick(blocks, lanes.z ^ step, 0).reshape(2, rows // 2, 3 * QW // 2)
        if rows == 2 * SUB:
            block = jnp.concatenate([block[0], block[1]], axis=-1)
        else:
            block = block.reshape(SUB, split)
        mine.append(jnp.concatenate([block, x_own], axis=-1))
    mine = [mine[0]] + [lanes.over_z(mine[step], step) for step in (1, 2, 3)]
    if fits:
        feed = pack_feed(own, after(gain_two, blocks), w_gate, w_up, w_down, n_p)
    else:
        feed = w_gate * gain_two, w_up * gain_two, w_down.T
        feed = [lowered(matrix).reshape(rows, 4, n_p, units) for matrix in feed]
        feed = jnp.concatenate(feed, axis=-1).transpose(1, 2, 0, 3)
        feed = split_rows(own, feed, 0)
    mine = after(mine, feed[0])
    x_pieces = [piece[:, split:] for piece in mine]
    if rows == 2 * SUB:
        middle = split // 2
        mine = [jnp.concatenate([one[:, :middle], one[:, middle:split]]) for one in mine]
    else:
        mine = [one[:, :split].reshape(rows, 3 * QW // 2) for one in mine]
    mine = lanes.join_z(mine)
    dy_line = lax.all_gather(after(dy_own, mine), "z", axis=0, tiled=True)
    feed = after(list(feed), mine)
    feed = [feed[0]] + [lanes.over_z(feed[step], step) for step in (1, 2, 3)]

    x_chunk = jnp.concatenate(x_pieces).astype(F32)
    inverse_chunk = lax.rsqrt(jnp.mean(x_chunk * x_chunk, axis=-1, keepdims=True) + NORM_EPS)
    normed = lowered(x_chunk * inverse_chunk)

    def in_parts(four):
        here, there = four[:2], four[2:]
        zero = [jnp.where(first_core, a, b) for a, b in zip(here, there)]
        return zero + [jnp.where(first_core, b, a) for a, b in zip(here, there)]

    def quarters_of(pair, which):
        width = HD + quarter
        lanes_of = [(k * width, k * width + HD) if which == 0 else (k * width + HD, (k + 1) * width) for k in (0, 1)]
        return [one[:, low:high] for one in pair for low, high in lanes_of]

    def filled(four, which):
        pads = ((0, 0), (0, quarter)) if which == 0 else ((0, 0), (HD, 0))
        wide = [jnp.pad(one, pads) for one in four]
        return [jnp.concatenate(wide[:2], axis=-1), jnp.concatenate(wide[2:], axis=-1)]

    def project():
        cubes = [
            lanes.gather_cube(half, order) for half, order in zip(lanes.halves(mine), lanes.orders())
        ]
        here = placed(own, cubes, False).reshape(D, 2 * (HD + quarter))
        weights = [here, lanes.swap(here)]
        line = lanes.z ^ jnp.arange(4, dtype=jnp.int32)
        ring = lanes.p ^ jnp.arange(n_p, dtype=jnp.int32)
        cores = h ^ jnp.arange(2, dtype=jnp.int32)
        within = jnp.arange(SUB, dtype=jnp.int32)
        key_blocks = 2 * (line[None, None, :] * n_p + ring[None, :, None]) + cores[:, None, None]
        key_positions = (block_offsets[key_blocks.reshape(-1)][:, None] + within).reshape(-1)
        cosine, sine = rotary_tables(key_positions[:chunk])
        projected = in_parts(quarters_of([product(normed, weight) for weight in weights], 0))
        query_heads = lowered(
            jnp.concatenate([rotate(one, cosine, sine) for one in projected[:SHARE]])
        )
        key_here = lowered(rotate(projected[2], cosine, sine))
        cubes = [
            lanes.gather_cube(one.reshape(4, SUB, HD), order)
            for one, order in zip((key_here, lowered(projected[3])), lanes.orders())
        ]
        plane = placed(jnp.zeros_like(own), cubes, True).reshape(n_p * chunk, 2 * HD)
        pair_all = jnp.concatenate([plane, lanes.swap(plane)])
        return weights, cosine, sine, key_positions, query_heads, pair_all

    weights, cosine, sine, key_positions, query_heads, pair_all = stage(project)
    feed = turned(own, after(feed, pair_all), 0)
    dy_all = lax.all_gather(after(dy_line, feed[0]), "p", axis=0, tiled=True)
    query_heads = after(query_heads, *feed)
    feed = [feed[0]] + [lanes.over_p(feed[e], e) for e in range(1, n_p)]

    def attention_forward():
        keys_all, values_all = pair_all[:, :HD], pair_all[:, HD:]
        my_positions = key_positions[:chunk]
        allowed = key_positions[None, :] <= my_positions[:, None]
        allowed = jnp.concatenate([allowed] * SHARE)
        scores = contract(query_heads, keys_all, 1, 1) * scaling
        scores = jnp.where(allowed, scores, MASKED_SCORE)
        largest = jnp.max(scores, axis=-1, keepdims=True)
        expos = jnp.exp(scores - largest)
        probs = expos / jnp.sum(expos, axis=-1, keepdims=True)
        attended = lowered(product(lowered(probs), values_all))
        mixed = jnp.concatenate([attended[:chunk], attended[chunk:]], axis=-1)
        quarters = in_parts([mixed[:, k * quarter : (k + 1) * quarter] for k in range(4)])
        resid_part = sum(
            contract(part, weight, 1, 1) for part, weight in zip(filled(quarters, 1), weights)
        )
        return probs, mixed, lowered(resid_part).reshape(4, SUB, D)

    probs, mixed, resid_part = stage(attention_forward)
    def second_norm():
        resid = x_own.astype(F32) + lanes.scatter_z(resid_part, True)
        inverse_two = lax.rsqrt(jnp.mean(resid * resid, axis=-1, keepdims=True) + NORM_EPS)
        normed_two = lowered(resid * inverse_two)
        return resid, inverse_two, lanes.absolute(lanes.gather_z(normed_two), lanes.z)

    resid, inverse_two, stacked = stage(second_norm)
    feed = after(feed, stacked)
    if fits:
        here = feed_weights(own, feed)
    else:
        here = joined(own, feed, 1).reshape(D, 3 * units)
        here = [here[:, : 2 * units], here[:, 2 * units :]]

    def gather_normed():
        there = [lanes.swap(weight) for weight in here]
        cubes = [
            lanes.gather_cube(half, order)
            for half, order in zip(lanes.halves(stacked), lanes.orders())
        ]
        normed_all = placed(own, cubes, True).reshape(n_ctx * SUB, D)
        return normed_all, there

    normed_all, there = stage(gather_normed)
    gate_up_weights, down_weights = zip(here, there)

    def feed_forward():
        d_gate_up, hidden = [], []
        for gate_up_weight, down_weight in zip(gate_up_weights, down_weights):
            incoming = product(dy_all, down_weight)
            gate_up = product(normed_all, gate_up_weight)
            gate_values, up_values = gate_up[:, :units], gate_up[:, units:]
            sigmoid_gate = jax.nn.sigmoid(gate_values)
            activated = gate_values * sigmoid_gate
            hidden.append(lowered(activated * up_values))
            slope = sigmoid_gate * (1.0 + gate_values * (1.0 - sigmoid_gate))
            d_gate = lowered(incoming * up_values * slope)
            d_gate_up.append(jnp.concatenate([d_gate, lowered(incoming * activated)], axis=-1))
        cubes = []
        for part in (slice(0, D // 2), slice(D // 2, D)):
            partial = sum(
                contract(one, weight[part], 1, 1)
                for one, weight in zip(d_gate_up, gate_up_weights)
            )
            cubes.append(partial.reshape(lanes.cube + [4, SUB, D // 2]))
        d_normed_parts = [
            lanes.scatter_p(cube, order, False) for cube, order in zip(cubes, lanes.orders())
        ]
        return hidden, d_gate_up, jnp.concatenate(d_normed_parts, axis=-1)

    if fits:
        outs = feed_forward_blocks(own, normed_all, dy_all, gate_up_weights, down_weights)
        hidden, d_gate_up = [outs[0][:, :units], outs[0][:, units:]], list(outs[1:3])
        stays, goes = [outs[3], outs[5]], [outs[4], outs[6]]
        comes = [lanes.over_p(goes[b], 1 << b) for b in (0, 1)]
    else:
        hidden, d_gate_up, d_normed_part = stage(feed_forward)
        comes = []

    def feed_gradients(core):
        return [
            lowered(contract(normed_all, d_gate_up[core], 0, 0)),
            lowered(contract(dy_all, hidden[core], 0, 0)),
        ]

    def feed_gradients_both():
        came = [lanes.swap(one) for one in feed_gradients(1)]
        out_part = sum(contract(one, weight, 1, 1) for one, weight in zip(hidden, down_weights))
        return came, feed_gradients(0), lowered(out_part)

    came, home, out_part = stage(feed_gradients_both)
    if fits:
        comes = after(comes, out_part)
        totals = [stay.astype(F32) + one.astype(F32) for stay, one in zip(stays, comes)]
        goes = [lowered(pick(totals[b], 1 - lanes.bit(1 - b), 0)) for b in (0, 1)]
        stays = [pick(totals[b], lanes.bit(1 - b), 0) for b in (0, 1)]
        comes = [lanes.over_p(goes[b], 1 << (1 - b)) for b in (0, 1)]
        came = add_split(own, n_p, after(home, *goes), came)
        comes = after(comes, came[0])
        d_normed_part = jnp.concatenate(
            [stay + one.astype(F32) for stay, one in zip(stays, comes)], axis=-1
        ).reshape(4, SUB, D)
    else:
        home, came = [jnp.concatenate(two, axis=-1).astype(F32) for two in (home, came)]
        came = split_rows(own, lowered(home + came).reshape(4, n_p, rows, 3 * units), 1)
    came = [came[0]] + [lanes.over_p(came[e], e) for e in range(1, n_p)]
    out_line = lax.psum_scatter(
        after(out_part, d_normed_part), "p", scatter_dimension=0, tiled=True
    )

    def second_norm_backward():
        d_normed_two = lanes.scatter_z(d_normed_part, False)
        d_resid = dy_own.astype(F32) + norm_back(resid, inverse_two, d_normed_two)
        return d_resid, jnp.concatenate(lanes.gather_z(lowered(d_resid)))

    d_resid, d_resid_chunk = stage(second_norm_backward)
    came = turned(own, after(came, d_resid_chunk), 1)
    d_resid_chunk = after(d_resid_chunk, *came)
    came = [came[0]] + [lanes.over_z(came[step], step) for step in (1, 2, 3)]

    def attention_backward():
        d_mixed = [product(d_resid_chunk, weight) for weight in weights]
        d_mixed = in_parts(quarters_of(d_mixed, 1))
        d_mixed = lowered(jnp.concatenate(d_mixed, axis=-1))
        d_attended = jnp.concatenate([d_mixed[:, :HD], d_mixed[:, HD:]])
        keys_all, values_all = pair_all[:, :HD], pair_all[:, HD:]
        d_probs = contract(d_attended, values_all, 1, 1)
        delta = jnp.sum(probs * d_probs, axis=-1, keepdims=True)
        d_scores = lowered(probs * (d_probs - delta))
        d_query_heads = product(d_scores, keys_all) * scaling
        d_key_all = contract(d_scores, query_heads, 0, 0) * scaling
        d_value_all = contract(lowered(probs), d_attended, 0, 0)
        middle = n_p * chunk
        d_pair = [d_key_all, d_value_all]
        cames = [lanes.swap(lowered(one[middle:])) for one in d_pair]
        d_pair_keeps = [lowered(one[:middle]) for one in d_pair]

        def summed_over_group(place, lead, keeps, cames):
            halves = add_halved(place, lead, n_p, keeps, cames, lanes.orders())
            done = []
            for (stay, goes), order in zip(halves, lanes.orders()):
                have = list(range(lanes.bits))
                for b, following in zip(order, order[1:] + [None]):
                    other = lanes.over_p(goes, 1 << b)
                    have.remove(b)
                    if following is None:
                        stay = lowered(stay.astype(F32) + other.astype(F32))
                    else:
                        stay, goes = sum_halved(place, stay, other, have.index(following), following)
                done.append(stay.reshape(lead * stay.shape[2], stay.shape[-1]))
            return done

        keeps = [[keep] for keep in d_pair_keeps]
        d_key, d_value = [
            one.astype(F32)
            for one in summed_over_group(jnp.zeros_like(own), 1, keeps, cames)
        ]
        d_key = lowered(rotate(d_key, cosine, -sine))
        d_value = lowered(d_value)
        d_query = [
            lowered(rotate(one, cosine, -sine))
            for one in (d_query_heads[:chunk], d_query_heads[chunk:])
        ]
        lefts = (normed, d_resid_chunk)
        rights = [d_query[0], mixed[:, :quarter], d_query[1], mixed[:, quarter : 2 * quarter]]
        others = [d_key, mixed[:, 2 * quarter : 3 * quarter], d_value, mixed[:, 3 * quarter :]]
        keep, away = [], []
        for k in range(4):
            mine, theirs = jnp.where(first_core, rights[k], others[k]), jnp.where(
                first_core, others[k], rights[k]
            )
            keep.append(lowered(contract(lefts[k % 2], mine, 0, 0)))
            away.append(lowered(contract(lefts[k % 2], theirs, 0, 0)))
        cames = [
            lanes.swap(jnp.concatenate(away[at : at + 2], axis=-1)) for at in (0, 2)
        ]
        summed = summed_over_group(own, 4, [keep[:2], keep[2:]], cames)
        in_turn = [half[:, :HD] for half in summed] + [half[:, HD:] for half in summed]
        in_turn = jnp.concatenate(in_turn, axis=-1).reshape(4, rows, 3 * QW // 2)
        return in_turn, in_parts(d_query + [d_key, d_value])

    in_turn, d_projected = stage(attention_backward)
    homeward = lanes.send_z(in_turn)

    def beside_home():
        joined_came = joined(own, came, 0).reshape(n_ctx, rows, 3 * units)
        shares = squares_of_feed(gain_two, w_gate, w_up, joined_came) if fits else in_turn
        d_normed_part = sum(
            contract(part, weight, 1, 1) for part, weight in zip(filled(d_projected, 0), weights)
        ).reshape(4, SUB, D)
        parts = [
            jnp.concatenate(
                [d_normed_part[s], pick(out_line.reshape(4, SUB, D), lanes.z ^ s, 0).astype(F32)]
            )
            for s in range(4)
        ]
        near = lowered(jnp.stack([parts[3], parts[1]]))
        return joined_came, shares, parts[0], parts[2], near

    came, shares, line_own, line_far, line_near = stage(beside_home)
    near = lanes.over_z(line_near, 1)
    part_zero, part_one = lanes.group_home(lanes.join_z(after(homeward, line_near)))
    masters = (w_query, w_key, w_value, w_out, w_gate, w_up, w_down)
    if fits:
        shared = squares_of_attention(gain_one, masters, part_zero, part_one, shares)
    else:

        def of_owner(k):
            part = came[:, :, k * units : (k + 1) * units].transpose(1, 0, 2)
            return part.reshape(rows, n_ctx * units).astype(F32)

        inner_gate, inner_up, grad_down = of_owner(0), of_owner(1), of_owner(2).T
        grad_out = jnp.concatenate([part_zero[:, :, QW:], part_one[:, :, QW:]], axis=-1)
        grad_out = grad_out.astype(F32).transpose(0, 2, 1).reshape(2 * QW, rows)
        inner_query = part_zero[:, :, :QW].astype(F32).transpose(1, 0, 2).reshape(rows, 2 * QW)
        inner_pair = part_one[:, :, :QW].astype(F32).transpose(1, 0, 2)
        inner_key = inner_pair[:, :, :HD].reshape(rows, 2 * HD)
        inner_value = inner_pair[:, :, HD:].reshape(rows, 2 * HD)

        def weighed(matrix, inner):
            return jnp.sum(lowered(matrix).astype(F32) * inner, axis=1)

        first = weighed(w_query, inner_query) + weighed(w_key, inner_key)
        grad_gains = jnp.stack(
            [
                first + weighed(w_value, inner_value),
                weighed(w_gate, inner_gate) + weighed(w_up, inner_up),
            ]
        )
        gradients = (
            inner_query * gain_one,
            inner_key * gain_one,
            inner_value * gain_one,
            grad_out,
            inner_gate * gain_two,
            inner_up * gain_two,
            grad_down,
        )
        squares = sum(jnp.sum(gradient * gradient) for gradient in gradients)
        shared = jnp.concatenate([grad_gains, jnp.broadcast_to(squares, (6, rows))])
    shared = shared + lanes.swap(shared)
    grad_gains = shared[:2]
    row = lax.broadcasted_iota(jnp.int32, shared.shape, 0)
    squares = jnp.where(row < 2, shared * shared, shared)
    for b in range(lanes.bits):
        squares = squares + lanes.over_p(squares, 1 << b)
    for s in (1, 2):
        squares = squares + lanes.over_z(squares, s)
    near = after(near, squares)
    far = lanes.over_z(lowered(line_far + near[0].astype(F32)), 2)
    grad_norm = jnp.sqrt(jnp.sum(squares[:2]) + squares[2, 0])
    factor = CLIP_NORM / jnp.maximum(grad_norm, CLIP_NORM)
    wo_fan = min(HQ * HD, max(2, 131072 // total_rows))
    rate_in = 2.0 / math.sqrt(D)
    step_rates = (
        rate_in,
        rate_in,
        rate_in,
        2.0 / math.sqrt(wo_fan),
        rate_in,
        rate_in,
        2.0 / math.sqrt(FF),
    )
    if fits:
        new_weights, copies, moment_first, moment_second = adamw_blocks(
            step_rates,
            factor,
            gain_one,
            gain_two,
            masters,
            (moment_one, moment_two),
            part_zero,
            part_one,
            came,
        )
    else:
        new_weights = []
        firsts = []
        seconds = []
        offset = 0
        for index_now in range(7):
            weight = masters[index_now]
            length = weight.size
            first_moment = moment_one[offset : offset + length].reshape(weight.shape)
            second_moment = moment_two[offset : offset + length].reshape(weight.shape)
            updated, first_new, second_new = adamw_step(
                weight,
                factor * gradients[index_now],
                first_moment,
                second_moment,
                step_rates[index_now],
                WEIGHT_DECAY,
            )
            new_weights.append(updated)
            firsts.append(first_new.reshape(-1))
            seconds.append(second_new.reshape(-1))
            offset = offset + length
        copies = [lowered(weight) for weight in new_weights]
        moment_first, moment_second = jnp.concatenate(firsts), jnp.concatenate(seconds)
    line_sums = line_own + near[1].astype(F32) + after(far, new_weights[0]).astype(F32)
    d_normed, out_sum = line_sums[:SUB], line_sums[SUB:]
    x_float = x_own.astype(F32)
    inverse_own = lax.rsqrt(jnp.mean(x_float * x_float, axis=-1, keepdims=True) + NORM_EPS)
    input_grad = lowered(d_resid + norm_back(x_float, inverse_own, d_normed))
    input_grad, layer_out = both_cores(input_grad), both_cores(lowered(resid + out_sum))
    new_gains, gain_first, gain_second = adamw_step(
        gains, factor * grad_gains, gain_moment_one, gain_moment_two, GAIN_RATE, 0.0
    )
    return (
        layer_out,
        input_grad,
        grad_norm,
        *new_weights,
        new_gains,
        *copies,
        lowered(new_gains),
        moment_first,
        moment_second,
        gain_first,
        gain_second,
    )


def solution(mesh):
    n_ctx, n_head = mesh.devices.shape
    lanes_mesh = Mesh(mesh.devices.reshape(4, n_ctx // 4, n_head), ("z", "p", "head"))
    ctx = ("z", "p")
    rows = P(ctx, None)
    wide = P(ctx, "head")
    tall = P("head", ctx)
    flat = P(("z", "p", "head"))
    gain = P(None, ctx)
    weights = (wide, wide, wide, tall, wide, wide, tall, gain)
    return jax.shard_map(
        local,
        mesh=lanes_mesh,
        in_specs=(rows, P(), rows, *weights, flat, flat, gain, gain),
        out_specs=(rows, rows, P(), *weights, *weights, flat, flat, gain, gain),
        check_vma=False,
    )
```
